32 devices in a mesh: dp: 4 (over z), expert: 8 (over y, x, core).
Axes of the slice: x: 2, y: 2, z: 4, core: 2. Of those that a mesh axis runs over, the one named last changes fastest.
Arguments:
- tokens: bfloat16 [92160, 512], P(('dp', 'expert')), may hold values from -6 to 6
- cotangent: bfloat16 [92160, 512], P(('dp', 'expert')), may hold values from -6 to 6
- expert_ids: int32 [92160, 2], P(('dp', 'expert')), may hold values from 0 to 7, all different within a row
- priority: int32 [32, 5760], P(('dp', 'expert')), may hold values from 0 to 5759, each once within a row
- step: int32 [], replicated, may hold values from 2 to 20
- attn_qkv: float32 [512, 1536], P(None, 'dp'), may hold values from -0.25 to 0.25
- attn_out: float32 [512, 512], P('dp'), may hold values from -4 to 4
- router: float32 [512, 8], P(None, 'dp'), may hold values from -0.1875 to 0.1875
- norms: float32 [4, 512], P(None, 'dp'), as said below
- expert_in: float32 [8, 512, 2048], P('expert', None, 'dp'), may hold values from -0.25 to 0.25
- expert_out: float32 [8, 2048, 512], P('expert', 'dp'), as said below
- moments_qkv: float32 [2, 512, 1536], P(None, None, 'dp'), as said below
- moments_out: float32 [2, 512, 512], P(None, 'dp'), as said below
- moments_router: float32 [2, 512, 8], P(None, None, 'dp'), as said below
- moments_norms: float32 [2, 4, 512], P(None, None, 'dp'), as said below
- moments_in: float32 [2, 8, 512, 2048], P(None, 'expert', None, 'dp'), as said below
- moments_exp: float32 [2, 8, 2048, 512], P(None, 'expert', 'dp'), as said below
Outputs:
- activations: bfloat16 [92160, 512], P(('dp', 'expert'))
- grad_input: float32 [92160, 512], P(('dp', 'expert'))
- grad_norm: float32 [], replicated
- new_qkv: float32 [512, 1536], P(None, 'dp')
- first_qkv: float32 [512, 1536], P(None, 'dp')
- second_qkv: float32 [512, 1536], P(None, 'dp')
- copy_qkv: bfloat16 [512, 1536], P(None, 'dp')
- new_out: float32 [512, 512], P('dp')
- first_out: float32 [512, 512], P('dp')
- second_out: float32 [512, 512], P('dp')
- copy_out: bfloat16 [512, 512], P('dp')
- new_router: float32 [512, 8], P(None, 'dp')
- first_router: float32 [512, 8], P(None, 'dp')
- second_router: float32 [512, 8], P(None, 'dp')
- copy_router: bfloat16 [512, 8], P(None, 'dp')
- new_norms: float32 [4, 512], P(None, 'dp')
- first_norms: float32 [4, 512], P(None, 'dp')
- second_norms: float32 [4, 512], P(None, 'dp')
- copy_norms: bfloat16 [4, 512], P(None, 'dp')
- new_expert_in: float32 [8, 512, 2048], P('expert', None, 'dp')
- first_expert_in: float32 [8, 512, 2048], P('expert', None, 'dp')
- second_expert_in: float32 [8, 512, 2048], P('expert', None, 'dp')
- copy_expert_in: bfloat16 [8, 512, 2048], P('expert', None, 'dp')
- new_expert_out: float32 [8, 2048, 512], P('expert', 'dp')
- first_expert_out: float32 [8, 2048, 512], P('expert', 'dp')
- second_expert_out: float32 [8, 2048, 512], P('expert', 'dp')
- copy_expert_out: bfloat16 [8, 2048, 512], P('expert', 'dp')
The draws below stay inside these ranges and needn't reach their ends.
Inputs may be any that keep to these rules, and one draw needn't show every extreme that they name: `norms`: rows 0 and 2 are gains near one, rows 1 and 3 small biases. `expert_out`: entries of both signs. `moments_qkv`: index 1 (second moments) is positive. `moments_out`: index 1 (second moments) is positive. `moments_router`: index 1 (second moments) is positive. `moments_norms`: index 1 (second moments) is positive. `moments_in`: index 1 (second moments) is positive. `moments_exp`: index 1 (second moments) is positive.
All inputs are finite; a program needn't handle non-finite values.
Results may differ from the reference program's by a relative error of at most 0.015.
Values may be sent and summed in bfloat16 or wider, within the bound.
No kernel may reach another device: no remote copies, remote signals or barrier semaphores. Data moves between devices by JAX's collectives and lax.ppermute only.
A program may use at most 320 MiB of HBM per device.

```python
import math
import jax
import jax.numpy as jnp
from jax import lax

D = 512
HEADS = 8
HEAD = 64
FF = 2048
SEQ = 720
EXPERTS = 8
TOK_DEV = 2880
TOKENS = 92160
CAP = 360
N_DP = 4
N_EXPERT = 8


def ramp_base():
    return 6.0


def expert_ramp(count):
    return ramp_base() ** (jnp.arange(count, dtype=jnp.float32) / max(count - 1, 1))


def unit_noise(key, shape):
    return jnp.clip(jax.random.normal(key, shape, jnp.float32), -5.0, 5.0)


def norm_guess():
    return 3.2 * D * math.sqrt(TOKENS)


def state_pair(key, shape, scale):
    first_key, second_key = jax.random.split(key)
    first = 0.111 * scale * unit_noise(first_key, shape)
    factor = jnp.exp(jax.random.uniform(second_key, shape, jnp.float32, math.log(0.5), math.log(8.0)))
    second = 0.001001 * scale * scale * factor
    return jnp.stack([first, second])


def draw_norms(key, part):
    gain_key, shift_key = jax.random.split(key)
    gains = 1.0 + 0.1 * jnp.clip(jax.random.normal(gain_key, (2, D), jnp.float32), -2.5, 2.5)
    shifts = 0.1 * jnp.clip(jax.random.normal(shift_key, (2, D), jnp.float32), -2.5, 2.5)
    return jnp.stack([gains[0], shifts[0], gains[1], shifts[1]])


def draw_expert_out(key, part):
    scale = EXPERTS / (1.2 * math.sqrt(FF))
    return unit_noise(key, (EXPERTS, FF, D)) * scale * expert_ramp(EXPERTS)[:, None, None]


def draw_moments_qkv(key, part):
    return state_pair(key, (D, 3 * D), 1.2 * math.sqrt(TOKENS) / norm_guess())


def draw_moments_out(key, part):
    return state_pair(key, (D, D), 1.3 * math.sqrt(2.7 / SEQ) * math.sqrt(TOKENS) / norm_guess())


def draw_moments_router(key, part):
    scale = 0.6 * math.sqrt(D) * math.sqrt(TOKENS / EXPERTS) / norm_guess()
    return state_pair(key, (D, EXPERTS), scale * expert_ramp(EXPERTS)[None, :])


def draw_moments_norms(key, part):
    return state_pair(key, (4, D), 1.3 * math.sqrt(TOKENS) / norm_guess())


def draw_moments_in(key, part):
    scale = 0.5 * math.sqrt(D / FF) * math.sqrt(TOKENS / EXPERTS) / norm_guess()
    return state_pair(key, (EXPERTS, D, FF), scale * expert_ramp(EXPERTS)[:, None, None])


def draw_moments_exp(key, part):
    scale = 0.65 / EXPERTS * math.sqrt(TOKENS / EXPERTS) / norm_guess()
    return state_pair(key, (EXPERTS, FF, D), scale)


def steps_of(stream_key, dims, cuts, smallest, top_value):
    def one(dim, blocks):
        draws = jax.random.uniform(jax.random.fold_in(jax.random.fold_in(stream_key, 6), dim), (blocks,), jnp.float32, smallest / len(cuts), top_value / len(cuts))
        return jnp.repeat(jnp.exp(draws), dims[dim] // blocks).reshape((-1,) + (1,) * (len(dims) - dim - 1))

    gain = one(*cuts[0])
    for cut in cuts[1:]:
        gain = gain * one(*cut)
    return gain


def picks_of(stream_key, rows, amount, top, lift):
    ranking = jax.random.permutation(jax.random.fold_in(stream_key, 1), amount)
    boost = ranking
    for power in range(3):
        boost = boost * boost // amount
    boost = boost * lift // amount
    lots = jax.random.randint(jax.random.fold_in(stream_key, 2), (rows, amount), 0, 4096) + boost
    holders = jax.random.permutation(jax.random.fold_in(stream_key, 3), rows)[jnp.arange(amount) % rows]
    lots = jnp.where(jnp.arange(rows)[:, None] == holders[None, :], 1 << 14, lots)
    score = lots * amount + jnp.arange(amount)
    return lax.top_k(score.astype(jnp.int32), top)[1].astype(jnp.int32)


def bell_draw(stream_key, dims, deviation, bound, shards=(), held_as=jnp.bfloat16):
    array = deviation * jax.random.normal(stream_key, dims, jnp.float32)
    if shards:
        array = array * steps_of(stream_key, dims, shards, -0.22, 0.18)
    return jnp.clip(array, -bound, bound).astype(held_as)


def setup_inputs(seed: int = 0) -> dict:
    keys = jax.random.split(jax.random.key(seed), 18)
    tokens = bell_draw(keys[0], (TOKENS, D), 1.0, 6.0, ((0, 32),))
    cotangent = bell_draw(keys[1], (TOKENS, D), 1.0, 6.0, ((0, 32),))
    expert_ids = picks_of(keys[2], TOKENS, EXPERTS, 2, 2048)
    priority = jax.vmap(lambda own: jax.random.permutation(own, 2 * TOK_DEV))(jax.random.split(keys[3], (N_DP * N_EXPERT))).reshape((N_DP * N_EXPERT, 2 * TOK_DEV)).astype(jnp.int32)
    step = jax.random.randint(keys[4], (), 2, 21).astype(jnp.int32)
    attn_qkv = bell_draw(keys[5], (D, 3 * D), D ** -0.5, 0.25, ((1, 4),), jnp.float32)
    attn_out = bell_draw(keys[6], (D, D), (max(D * 4 // SEQ, 1)) ** -0.5, 4.0, ((0, 4),), jnp.float32)
    router = bell_draw(keys[7], (D, EXPERTS), (2 * D) ** -0.5, 0.1875, ((1, 4),), jnp.float32)
    norms = draw_norms(jax.random.fold_in(keys[17], 71), 0)
    expert_in = bell_draw(keys[9], (EXPERTS, D, FF), D ** -0.5, 0.25, ((0, 8), (2, 4)), jnp.float32)
    expert_out = draw_expert_out(jax.random.fold_in(keys[17], 71), 0)
    moments_qkv = draw_moments_qkv(jax.random.fold_in(keys[17], 71), 0)
    moments_out = draw_moments_out(jax.random.fold_in(keys[17], 71), 0)
    moments_router = draw_moments_router(jax.random.fold_in(keys[17], 71), 0)
    moments_norms = draw_moments_norms(jax.random.fold_in(keys[17], 71), 0)
    moments_in = draw_moments_in(jax.random.fold_in(keys[17], 71), 0)
    moments_exp = draw_moments_exp(jax.random.fold_in(keys[17], 71), 0)
    return dict(tokens=tokens, cotangent=cotangent, expert_ids=expert_ids, priority=priority, step=step, attn_qkv=attn_qkv, attn_out=attn_out, router=router, norms=norms, expert_in=expert_in, expert_out=expert_out, moments_qkv=moments_qkv, moments_out=moments_out, moments_router=moments_router, moments_norms=moments_norms, moments_in=moments_in, moments_exp=moments_exp)


@jax.custom_vjp
def low(v):
    return lax.optimization_barrier(v.astype(jnp.bfloat16)).astype(jnp.float32)

@jax.custom_vjp
def low_back(v):
    return v

def low_keep(v):
    return (low(v), None)

def low_pass(kept, grad):
    return (grad,)

def back_keep(v):
    return (v, None)

def back_low(kept, grad):
    return (low(grad),)
low.defvjp(low_keep, low_pass)
low_back.defvjp(back_keep, back_low)
EPS_NORM = 1e-06
BETA_ONE = 0.9
BETA_TWO = 0.999
ADAM_EPS = 1e-08
DECAY_RATE = 0.1
MAX_NORM = 1.0

def matmul_high(left, right):
    return jnp.dot(left, right, precision=lax.Precision.HIGHEST, preferred_element_type=jnp.float32)

def layer_norm(values, gain_row, shift_row):
    center = values - lax.optimization_barrier(jnp.mean(values, axis=-1, keepdims=True))
    spread = lax.optimization_barrier(jnp.mean(center * center, axis=-1, keepdims=True))
    return center * lax.rsqrt(spread + EPS_NORM) * gain_row + shift_row

def attend_image(picture, qkv_w, out_w, gain_row, shift_row):
    normed = low(layer_norm(picture, gain_row, shift_row))
    proj = low_back(low(matmul_high(normed, qkv_w)))
    queries = proj[:, :D].reshape(SEQ, HEADS, HEAD)
    keys_all = proj[:, D:2 * D].reshape(SEQ, HEADS, HEAD)
    values_all = proj[:, 2 * D:].reshape(SEQ, HEADS, HEAD)
    raw_scores = jnp.einsum('qhd,khd->hqk', queries, keys_all, precision=lax.Precision.HIGHEST)
    scores = low_back(raw_scores * HEAD ** (-0.5))
    probs = jax.nn.softmax(scores, axis=-1)
    context = jnp.einsum('hqk,khd->qhd', low(probs), values_all, precision=lax.Precision.HIGHEST)
    context = low_back(low(context.reshape(SEQ, D)))
    return low_back(matmul_high(context, out_w))

def slot_of(pair_expert, pair_rank):
    same_expert = pair_expert[:, None] == pair_expert[None, :]
    ranked_ahead = pair_rank[None, :] < pair_rank[:, None]
    return lax.optimization_barrier(jnp.sum(jnp.where(same_expert & ranked_ahead, 1, 0), axis=1)).astype(jnp.int32)

def pick_rows(table, index):
    return table[index]

def forward(inputs, qkv_m, out_m, router_m, norms_m, in_m, exp_m, expert_ids, priority):
    qkv_w = low(qkv_m)
    out_w = low(out_m)
    router_w = low(router_m)
    norm_w = low(norms_m)
    in_w = low(in_m)
    exp_w = low(exp_m)
    device_count = N_DP * N_EXPERT
    pair_count = 2 * TOK_DEV
    attend = jax.checkpoint(attend_image)
    pictures = inputs.reshape(-1, SEQ, D)
    attended = lax.map(lambda picture: attend(picture, qkv_w, out_w, norm_w[0], norm_w[1]), pictures)
    middle = inputs + attended.reshape(TOKENS, D)
    second = low(layer_norm(middle, norm_w[2], norm_w[3]))
    logits = low_back(matmul_high(second, router_w))
    gates_all = jax.nn.softmax(logits, axis=-1)
    pair_expert = expert_ids.reshape(device_count, pair_count)
    slot_rank = jax.vmap(slot_of)(pair_expert, priority)
    kept_mask = slot_rank < CAP
    chosen_prob = jnp.take_along_axis(gates_all.reshape(device_count, TOK_DEV, EXPERTS), expert_ids.reshape(device_count, TOK_DEV, 2), axis=2)
    gate_value = jnp.where(kept_mask, chosen_prob.reshape(device_count, pair_count), 0.0)
    position = jnp.where(kept_mask, pair_expert * CAP + slot_rank, EXPERTS * CAP).astype(jnp.int32)
    pair_index = jnp.arange(pair_count, dtype=jnp.int32)
    slot_pair = jax.vmap(lambda spot: jnp.full((EXPERTS * CAP,), pair_count, jnp.int32).at[spot].set(pair_index, mode='drop'))(position)
    slot_token = slot_pair // 2
    second_pad = jnp.concatenate([second.reshape(device_count, TOK_DEV, D), jnp.zeros((device_count, 1, D), jnp.float32)], axis=1)
    rows = low_back(jax.vmap(pick_rows)(second_pad, slot_token)).reshape(device_count, EXPERTS, CAP, D)
    hidden = low_back(jnp.einsum('secd,edf->secf', rows, in_w, precision=lax.Precision.HIGHEST))
    act = low(jax.nn.gelu(hidden, approximate=False))
    back = low_back(low(jnp.einsum('secf,efd->secd', act, exp_w, precision=lax.Precision.HIGHEST)))
    back_pad = jnp.concatenate([back.reshape(device_count, EXPERTS * CAP, D), jnp.zeros((device_count, 1, D), jnp.float32)], axis=1)
    picked = jax.vmap(pick_rows)(back_pad, position)
    mixed = lax.optimization_barrier(jnp.sum((gate_value[:, :, None] * picked).reshape(device_count, TOK_DEV, 2, D), axis=2))
    return middle + mixed.reshape(TOKENS, D)

def step_rates(experts):
    return (D ** (-0.5), 2.0 ** (-0.5), (2 * D) ** (-0.5), 0.1, D ** (-0.5), 2.0 * experts / (1.2 * FF ** 0.5))

def adam_update(weight, moments, grad, factor, rate, decay, step_float):
    clipped = grad * factor
    first = BETA_ONE * moments[0] + (1.0 - BETA_ONE) * clipped
    second = BETA_TWO * moments[1] + (1.0 - BETA_TWO) * clipped * clipped
    fix_one = 1.0 - jnp.power(BETA_ONE, step_float)
    fix_two = 1.0 - jnp.power(BETA_TWO, step_float)
    updated = weight - rate * (first / fix_one / (jnp.sqrt(second / fix_two) + ADAM_EPS) + decay * weight)
    return (updated, first, second, updated.astype(jnp.bfloat16))

def reference(tokens, cotangent, expert_ids, priority, step, attn_qkv, attn_out, router, norms, expert_in, expert_out, moments_qkv, moments_out, moments_router, moments_norms, moments_in, moments_exp):
    inputs = tokens.astype(jnp.float32)

    def run_block(inputs, qkv_m, out_m, router_m, norms_m, in_m, exp_m):
        return forward(inputs, qkv_m, out_m, router_m, norms_m, in_m, exp_m, expert_ids, priority)
    result, pull_back = jax.vjp(run_block, inputs, attn_qkv, attn_out, router, norms, expert_in, expert_out)
    grads = pull_back(cotangent.astype(jnp.float32))
    total = jnp.zeros((), jnp.float32)
    for grad in grads[1:]:
        total = total + jnp.sum(grad * grad)
    grad_norm = jnp.sqrt(total)
    factor = MAX_NORM / grad_norm
    rates = step_rates(EXPERTS)
    step_float = step.astype(jnp.float32)
    new_qkv, first_qkv, second_qkv, copy_qkv = adam_update(attn_qkv, moments_qkv, grads[1], factor, rates[0], DECAY_RATE, step_float)
    new_out, first_out, second_out, copy_out = adam_update(attn_out, moments_out, grads[2], factor, rates[1], DECAY_RATE, step_float)
    new_router, first_router, second_router, copy_router = adam_update(router, moments_router, grads[3], factor, rates[2], DECAY_RATE, step_float)
    new_norms, first_norms, second_norms, copy_norms = adam_update(norms, moments_norms, grads[4], factor, rates[3], 0.0, step_float)
    new_in, first_in, second_in, copy_in = adam_update(expert_in, moments_in, grads[5], factor, rates[4], DECAY_RATE, step_float)
    new_exp, first_exp, second_exp, copy_exp = adam_update(expert_out, moments_exp, grads[6], factor, rates[5], DECAY_RATE, step_float)
    return (result.astype(jnp.bfloat16), grads[0], grad_norm, new_qkv, first_qkv, second_qkv, copy_qkv, new_out, first_out, second_out, copy_out, new_router, first_router, second_router, copy_router, new_norms, first_norms, second_norms, copy_norms, new_in, first_in, second_in, copy_in, new_exp, first_exp, second_exp, copy_exp)
```

```python
import functools

import jax
import jax.numpy as jnp
from jax import lax
from jax.experimental import pallas as pl
from jax.experimental.pallas import tpu as pltpu
from jax.sharding import PartitionSpec as P

D = 512
HEADS = 8
HEAD = 64
FF = 2048
SEQ = 720

EPS_NORM = 1e-06
BETA_ONE = 0.9
BETA_TWO = 0.999
ADAM_EPS = 1e-08
DECAY_RATE = 0.1
MAX_NORM = 1.0

f32, bf16, i32 = jnp.float32, jnp.bfloat16, jnp.int32
NN = (((1,), (0,)), ((), ()))
NT = (((1,), (1,)), ((), ()))
TN = (((0,), (0,)), ((), ()))
LOG2E = 1.4426950408889634
SCALE = HEAD**-0.5
FAR = 1 << 20
VMEM_LIMIT = 60 * 2**20


def mm(a, b, dims=NN):
    return lax.dot_general(a, b, dims, preferred_element_type=f32)


def full(a):
    return pl.BlockSpec(a.shape, lambda *i: (0,) * a.ndim)


def whole(*shape):
    return pl.BlockSpec(shape, lambda *i: (0,) * len(shape))


def per_image(cols):
    return pl.BlockSpec((SEQ, cols), lambda i: (i, 0))


def per_image_t(rows):
    return pl.BlockSpec((1, rows, SEQ), lambda i: (i, 0, 0))


def sds(shape, dtype):
    return jax.ShapeDtypeStruct(shape, dtype)


def call(body, name, cost, **kw):
    flops, moved = cost
    return pl.pallas_call(
        body,
        name=name,
        compiler_params=pltpu.CompilerParams(vmem_limit_bytes=VMEM_LIMIT),
        cost_estimate=pl.CostEstimate(
            flops=int(flops), bytes_accessed=int(moved), transcendentals=0
        ),
        **kw,
    )


def normalize(v):
    c = v - jnp.mean(v, axis=-1, keepdims=True)
    r = lax.rsqrt(jnp.mean(c * c, axis=-1, keepdims=True) + EPS_NORM)
    return c * r, r


def assemble_kernel(experts, where, own, r1, r2, r3, s1, s2, s3, wT, ow, rT, nm):
    me, core = where[0], where[1]
    per = experts // 4

    def put(d, hh, piece):
        wT[d * 384 + hh * 192 : d * 384 + hh * 192 + 192, :] = piece[:192, :]
        ow[d * 128 + hh * 64 : d * 128 + hh * 64 + 64, :] = piece[192:256, :]
        if hh == 0:
            misc = piece[256:272, :].astype(f32)
            rT[d * per : (d + 1) * per, :] = misc[:per, :]
            for j in range(4):
                nm[j : j + 1, d * 128 : (d + 1) * 128] = misc[
                    per : per + 1, j * 128 : (j + 1) * 128
                ]

    for d in range(4):
        for k in range(4):

            @pl.when((me ^ k) == d)
            def _(d=d, k=k):
                if k == 0:
                    put(d, 0, own[0])
                    put(d, 1, own[1])
                else:
                    mine = (r1, r2, r3)[k - 1]
                    other = (s1, s2, s3)[k - 1]

                    @pl.when(core == 0)
                    def _():
                        put(d, 0, mine)
                        put(d, 1, other)

                    @pl.when(core == 1)
                    def _():
                        put(d, 0, other)
                        put(d, 1, mine)


def assemble(where, own, got, sib, experts):
    args = (own, *got, *sib)
    return call(
        functools.partial(assemble_kernel, experts),
        "assemble",
        (1e6, 5e6),
        in_specs=[pl.BlockSpec(memory_space=pltpu.SMEM)] + [whole(*a.shape) for a in args],
        out_specs=[whole(3 * D, D), whole(D, D), whole(experts, D), whole(4, D)],
        out_shape=[
            sds((3 * D, D), bf16),
            sds((D, D), bf16),
            sds((experts, D), f32),
            sds((4, D), f32),
        ],
    )(where, *args)


def dispatch(pos, x, u, pad, step):
    io = lax.broadcasted_iota(i32, (pad, SEQ), 0)
    acc = None
    for i in range(pos.shape[0]):
        hit = jnp.where(io == pos[i, pl.ds(step, 1), :], 1.0, 0.0).astype(bf16)
        part = mm(hit, x[i * SEQ : (i + 1) * SEQ, :])
        acc = part if acc is None else acc + part
    u[0] = acc.astype(bf16)


def slots_kernel(cap, pad, ids, prio, cot, pos, cols, u):
    step = pl.program_id(0)
    n = ids.shape[0]
    experts = pos.shape[1]
    nh = -(-(2 * n * SEQ) // 2048) * 16

    @pl.when(step == 0)
    def _():
        hi_io = lax.broadcasted_iota(i32, (nh, SEQ), 0)
        lo_io = lax.broadcasted_iota(i32, (128, SEQ), 0)

        def hot(i, k):
            q = prio[i, k : k + 1, :]
            return hi_io == (q >> 7), lo_io == (q & 127)

        table = jnp.zeros((nh, 128), f32)
        for i in range(n):
            for k in range(2):
                a, b = hot(i, k)
                ex = (ids[i, k : k + 1, :] + 1).astype(f32)
                table += mm(
                    jnp.where(a, 1.0, 0.0).astype(bf16), jnp.where(b, ex, 0.0).astype(bf16), NT
                )
        upper = (
            lax.broadcasted_iota(i32, (128, 128), 0) < lax.broadcasted_iota(i32, (128, 128), 1)
        ).astype(bf16)
        lower = (
            lax.broadcasted_iota(i32, (nh, nh), 1) < lax.broadcasted_iota(i32, (nh, nh), 0)
        ).astype(bf16)
        ones = jnp.ones((128, 128), bf16)
        rank = jnp.zeros((nh, 128), f32)
        for e in range(experts):
            m = (table == float(e + 1)).astype(f32)
            mb = m.astype(bf16)
            rank += m * (mm(mb, upper) + mm(mm(lower, mb).astype(bf16), ones))
        ri = jnp.minimum(rank.astype(i32), 16383)
        rlo = (ri & 127).astype(bf16)
        rhi = (ri >> 7).astype(bf16)
        eio = lax.broadcasted_iota(i32, (experts, SEQ), 0)
        for i in range(n):
            out = jnp.full((experts, SEQ), FAR, i32)
            flat = []
            for k in range(2):
                a, b = hot(i, k)
                bb = jnp.where(b, 1.0, 0.0).astype(bf16)
                x = mm(rlo, bb) + 128.0 * mm(rhi, bb)
                r = jnp.sum(jnp.where(a, x, 0.0), axis=0, keepdims=True).astype(i32)
                ex = ids[i, k : k + 1, :]
                keep = r < cap
                out = jnp.where((eio == ex) & keep, r, out)
                flat.append(jnp.where(keep, ex * pad + r, FAR))
            pos[i] = out
            fl = jnp.concatenate(flat + [jnp.zeros((6, SEQ), i32)], axis=0).astype(f32)
            cols[i * SEQ : (i + 1) * SEQ, :] = fl.T.astype(i32)

    dispatch(pos, cot, u, pad, step)


def slots(ids, prio, cot, experts, cap, pad):
    n = ids.shape[0]
    t = n * SEQ
    return call(
        functools.partial(slots_kernel, cap, pad),
        "slots",
        (12e9, 8e6),
        grid=(experts,),
        in_specs=[full(ids), full(prio), full(cot)],
        out_specs=[
            whole(n, experts, SEQ),
            whole(t, 8),
            pl.BlockSpec((1, pad, D), lambda e: (e, 0, 0)),
        ],
        out_shape=[
            sds((n, experts, SEQ), i32),
            sds((t, 8), i32),
            sds((experts, pad, D), bf16),
        ],
    )(ids, prio, cot)


def spread_kernel(pad, pos, x, u):
    dispatch(pos, x, u, pad, pl.program_id(0))


def spread(pos, x, pad):
    experts = pos.shape[1]
    return call(
        functools.partial(spread_kernel, pad),
        "spread",
        (9e9, 6e6),
        grid=(experts,),
        in_specs=[full(pos), full(x)],
        out_specs=pl.BlockSpec((1, pad, D), lambda e: (e, 0, 0)),
        out_shape=sds((experts, pad, D), bf16),
    )(pos, x)


def head_masks():
    lane = lax.broadcasted_iota(i32, (1, 128), 1)
    return (lane < 64).astype(bf16), (lane >= 64).astype(bf16)


def attend_kernel(tok, wT, ow, rT, nm, proj, ctxT, lse, mid, sec, gatesT, vT, ct):
    x = tok[...].astype(f32)
    xh, _ = normalize(x)
    fb = (xh * nm[0:1, :] + nm[1:2, :]).astype(bf16)
    proj[...] = mm(fb, wT[...], NT).astype(bf16)
    vT[...] = proj[:, 2 * D :].T
    masks = head_masks()
    for h in range(HEADS):
        p = h // 2
        qm = proj[:, p * 128 : (p + 1) * 128] * masks[h % 2]
        kk = proj[:, D + p * 128 : D + (p + 1) * 128]
        s = mm(kk, qm, NT)
        m = jnp.max(s, axis=0, keepdims=True)
        e = jnp.exp2((s - m) * (SCALE * LOG2E))
        total = jnp.sum(e, axis=0, keepdims=True)
        c = mm(vT[h * 64 : (h + 1) * 64, :], e.astype(bf16))
        ct[h * 64 : (h + 1) * 64, :] = (c * (1.0 / total)).astype(bf16)
        lse[0, h : h + 1, :] = m * (SCALE * LOG2E) + jnp.log2(total)
    ctxT[0] = ct[...]
    middle = x + mm(ct[...], ow[...], TN)
    mid[...] = middle
    xh2, _ = normalize(middle)
    s2 = (xh2 * nm[2:3, :] + nm[3:4, :]).astype(bf16)
    sec[...] = s2
    logits = mm(rT[...].astype(bf16), s2, NT)
    ex = jnp.exp(logits - jnp.max(logits, axis=0, keepdims=True))
    gatesT[0] = ex / jnp.sum(ex, axis=0, keepdims=True)


def attend(tok, wT, ow, rT, nm):
    t = tok.shape[0]
    n = t // SEQ
    experts = rT.shape[0]
    return call(
        attend_kernel,
        "attend",
        (45e9, 30e6),
        grid=(n,),
        in_specs=[per_image(D), full(wT), full(ow), full(rT), full(nm)],
        out_specs=[
            per_image(3 * D),
            per_image_t(D),
            per_image_t(HEADS),
            per_image(D),
            per_image(D),
            per_image_t(experts),
        ],
        out_shape=[
            sds((t, 3 * D), bf16),
            sds((n, D, SEQ), bf16),
            sds((n, HEADS, SEQ), f32),
            sds((t, D), f32),
            sds((t, D), bf16),
            sds((n, experts, SEQ), f32),
        ],
        scratch_shapes=[pltpu.VMEM((D, SEQ), bf16), pltpu.VMEM((D, SEQ), bf16)],
    )(tok, wT, ow, rT, nm)


def normal_cdf(h):
    t = 1.0 / (1.0 + (0.3275911 * 0.7071067811865476) * jnp.abs(h))
    g = jnp.exp2((-0.5 * LOG2E) * h * h)
    poly = t * (
        0.5 * 0.254829592
        + t
        * (
            0.5 * -0.284496736
            + t * (0.5 * 1.421413741 + t * (0.5 * -1.453152027 + t * (0.5 * 1.061405429)))
        )
    )
    q = poly * g
    return jnp.where(h >= 0, 1.0 - q, q), g


def experts_kernel(cap, where, rows, u, iw, xw, rT, gb, dr, din, dexpT):
    s = pl.program_id(0)
    x = rows[0]
    up = u[0]
    pad = x.shape[0]
    chunks = iw.shape[0]
    cols = iw.shape[2]
    logits = mm(x, rT[...].astype(bf16), NT)
    ex = jnp.exp(logits - jnp.max(logits, axis=1, keepdims=True))
    mine = lax.broadcasted_iota(i32, ex.shape, 1) == where[2]
    gate = jnp.sum(jnp.where(mine, ex, 0.0), axis=1, keepdims=True) / jnp.sum(
        ex, axis=1, keepdims=True
    )
    upf = up.astype(f32)
    db = (gate * upf).astype(bf16)
    back = None
    drow = None
    for j in range(chunks):
        h = mm(x, iw[j])
        cdf, g = normal_cdf(h)
        act = (h * cdf).astype(bf16)
        part = mm(act, xw[j])
        back = part if back is None else back + part
        dact = mm(db, xw[j], NT)
        dh = (dact * (cdf + h * g * 0.3989422804014327)).astype(bf16)
        part = mm(dh, iw[j], NT)
        drow = part if drow is None else drow + part
        di = mm(x, dh, TN)
        de = mm(db, act, TN)

        @pl.when(s == 0)
        def _(j=j, di=di, de=de):
            din[j] = di
            dexpT[j] = de

        @pl.when(s > 0)
        def _(j=j, di=di, de=de):
            din[j] += di
            dexpT[j] += de

    b = back.astype(bf16).astype(f32)
    gb[0] = (gate * b).astype(bf16)
    prod = upf * b
    first = prod.astype(bf16)
    rest = (prod - first.astype(f32)).astype(bf16)
    ones = jnp.ones((8, D), bf16)
    dg = (mm(ones, first, NT) + mm(ones, rest, NT))[0:1, :]
    dg = jnp.concatenate([dg, jnp.zeros((1, D - pad), f32)], axis=1)
    dg_first = dg.astype(bf16).astype(f32)
    line = lax.broadcasted_iota(i32, (pad, D), 0)
    drow = jnp.where(line == cap, dg_first, jnp.where(line == cap + 1, dg - dg_first, drow))
    dr[0] = drow.astype(bf16)


def run_experts(where, rows, u, iw, xw, rT, cap):
    groups, pad, _ = rows.shape
    chunks, _, cols = iw.shape
    blk = pl.BlockSpec((1, pad, D), lambda i: (i, 0, 0))
    return call(
        functools.partial(experts_kernel, cap),
        "experts",
        (70e9, 25e6),
        grid=(groups,),
        in_specs=[pl.BlockSpec(memory_space=pltpu.SMEM), blk, blk, full(iw), full(xw), full(rT)],
        out_specs=[blk, blk, whole(chunks, D, cols), whole(chunks, D, cols)],
        out_shape=[sds((groups, pad, D), bf16)] * 2 + [sds((chunks, D, cols), f32)] * 2,
    )(where, rows, u, iw, xw, rT)


def pick(cols, count):
    io = lax.broadcasted_iota(i32, (SEQ, count), 1)
    return jnp.where((io == cols[:, 0:1]) | (io == cols[:, 1:2]), 1.0, 0.0).astype(bf16)


def combine_kernel(cap, experts, dr, cols, gatesT, sec, mid, cot, rT, nm, dmid, dn, drT):
    i = pl.program_id(0)
    pad = dr.shape[0] // experts
    hits = pick(cols[...], dr.shape[0])
    ds = mm(hits, dr[...])
    base = cap // 16 * 16
    off = cap - base
    width = -(-pad // 128) * 128
    dg = []
    for e in range(experts):
        two = dr[e * pad + base : (e + 1) * pad, :pad]
        x = mm(two, hits[:, e * pad : (e + 1) * pad], NT)
        dg.append(x[off : off + 1, :] + x[off + 1 : off + 2, :])
    dg = jnp.concatenate(dg, axis=0)
    g = gatesT[0]
    dl = (g * (dg - jnp.sum(g * dg, axis=0, keepdims=True))).astype(bf16)
    ds = ds + mm(dl, rT[...].astype(bf16), TN)
    xh, r = normalize(mid[...])
    y = ds * nm[2:3, :]
    dmid[...] = cot[...].astype(f32) + r * (
        y - jnp.mean(y, axis=-1, keepdims=True) - xh * jnp.mean(y * xh, axis=-1, keepdims=True)
    )
    gg = jnp.sum(ds * xh, axis=0, keepdims=True)
    gs = jnp.sum(ds, axis=0, keepdims=True)
    dR = mm(dl, sec[...])

    @pl.when(i == 0)
    def _():
        dn[0:1, :] = gg
        dn[1:2, :] = gs
        drT[...] = dR

    @pl.when(i > 0)
    def _():
        dn[0:1, :] += gg
        dn[1:2, :] += gs
        drT[...] += dR


def combine(dr, cols, gatesT, sec, mid, cot, rT, nm, cap):
    experts, pad, _ = dr.shape
    t = cols.shape[0]
    n = t // SEQ
    dr = dr.reshape(experts * pad, D)
    return call(
        functools.partial(combine_kernel, cap, experts),
        "combine",
        (20e9, 25e6),
        grid=(n,),
        in_specs=[
            full(dr),
            per_image(8),
            per_image_t(experts),
            per_image(D),
            per_image(D),
            per_image(D),
            full(rT),
            full(nm),
        ],
        out_specs=[per_image(D), whole(2, D), whole(experts, D)],
        out_shape=[sds((t, D), f32), sds((2, D), f32), sds((experts, D), f32)],
    )(dr, cols, gatesT, sec, mid, cot, rT, nm)


def finish_kernel(gb, cols, mid, out):
    out[...] = (mid[...] + mm(pick(cols[...], gb.shape[0]), gb[...])).astype(bf16)


def finish(gb, cols, mid):
    experts, pad, _ = gb.shape
    t = cols.shape[0]
    gb = gb.reshape(experts * pad, D)
    return call(
        finish_kernel,
        "finish",
        (10e9, 12e6),
        grid=(t // SEQ,),
        in_specs=[full(gb), per_image(8), per_image(D)],
        out_specs=per_image(D),
        out_shape=sds((t, D), bf16),
    )(gb, cols, mid)


def attend_back_kernel(
    tok, dmid, proj, ctxT, lse, wT, ow, nm, gin, dqkv, dout, dn, kT, dqT, dp
):
    i = pl.program_id(0)
    da = dmid[...].astype(bf16)
    do = mm(da, ow[...], NT).astype(bf16)
    doT = mm(ow[...], da, NT).astype(bf16)
    prod = doT.astype(f32) * ctxT[0].astype(f32)
    kT[...] = proj[:, D : 2 * D].T
    masks = head_masks()
    low = lax.broadcasted_iota(i32, (SEQ, 128), 1) < 64
    for p in range(HEADS // 2):
        dv = []
        dk = []
        qq = proj[:, p * 128 : (p + 1) * 128]
        kk = proj[:, D + p * 128 : D + (p + 1) * 128]
        vv = proj[:, 2 * D + p * 128 : 2 * D + (p + 1) * 128]
        dd = do[:, p * 128 : (p + 1) * 128]
        for j in range(2):
            h = 2 * p + j
            s = mm(kk, qq * masks[j], NT)
            prob = jnp.exp2(s * (SCALE * LOG2E) - lse[0, h : h + 1, :])
            dprob = mm(vv, dd * masks[j], NT)
            dv.append(mm(prob.astype(bf16), dd))
            inner = jnp.sum(prod[h * 64 : (h + 1) * 64, :], axis=0, keepdims=True)
            ds = (prob * (dprob - inner)).astype(bf16)
            dk.append(mm(ds, qq))
            dqT[h * 64 : (h + 1) * 64, :] = (
                mm(kT[h * 64 : (h + 1) * 64, :], ds) * SCALE
            ).astype(bf16)
        lo = p * 128
        dp[:, 2 * D + lo : 2 * D + lo + 128] = jnp.where(low, dv[0], dv[1]).astype(bf16)
        dp[:, D + lo : D + lo + 128] = (jnp.where(low, dk[0], dk[1]) * SCALE).astype(bf16)
    dp[:, :D] = dqT[...].T
    dproj = dp[...]
    xh, r = normalize(tok[...].astype(f32))
    fb = (xh * nm[0:1, :] + nm[1:2, :]).astype(bf16)
    gq = mm(fb, dproj, TN)
    go = mm(ctxT[0], da)
    df = mm(dproj, wT[...])
    y = df * nm[0:1, :]
    gin[...] = dmid[...] + r * (
        y - jnp.mean(y, axis=-1, keepdims=True) - xh * jnp.mean(y * xh, axis=-1, keepdims=True)
    )
    gg = jnp.sum(df * xh, axis=0, keepdims=True)
    gs = jnp.sum(df, axis=0, keepdims=True)

    @pl.when(i == 0)
    def _():
        dqkv[...] = gq
        dout[...] = go
        dn[0:1, :] = gg
        dn[1:2, :] = gs

    @pl.when(i > 0)
    def _():
        dqkv[...] += gq
        dout[...] += go
        dn[0:1, :] += gg
        dn[1:2, :] += gs


def attend_back(tok, dmid, proj, ctxT, lse, wT, ow, nm):
    t = tok.shape[0]
    n = t // SEQ
    return call(
        attend_back_kernel,
        "attend_back",
        (80e9, 40e6),
        grid=(n,),
        in_specs=[
            per_image(D),
            per_image(D),
            per_image(3 * D),
            per_image_t(D),
            per_image_t(HEADS),
            full(wT),
            full(ow),
            full(nm),
        ],
        out_specs=[per_image(D), whole(D, 3 * D), whole(D, D), whole(2, D)],
        out_shape=[
            sds((t, D), f32),
            sds((D, 3 * D), f32),
            sds((D, D), f32),
            sds((2, D), f32),
        ],
        scratch_shapes=[
            pltpu.VMEM((D, SEQ), bf16),
            pltpu.VMEM((D, SEQ), bf16),
            pltpu.VMEM((SEQ, 3 * D), bf16),
        ],
    )(tok, dmid, proj, ctxT, lse, wT, ow, nm)


def step_rates(experts):
    return (
        D ** (-0.5),
        2.0 ** (-0.5),
        (2 * D) ** (-0.5),
        0.1,
        D ** (-0.5),
        2.0 * experts / (1.2 * FF**0.5),
    )


def adam_update(weight, moments, grad, factor, rate, decay, step_float):
    clipped = grad * factor
    first = BETA_ONE * moments[0] + (1.0 - BETA_ONE) * clipped
    second = BETA_TWO * moments[1] + (1.0 - BETA_TWO) * clipped * clipped
    fix_one = 1.0 - jnp.power(BETA_ONE, step_float)
    fix_two = 1.0 - jnp.power(BETA_TWO, step_float)
    updated = weight - rate * (
        first / fix_one / (jnp.sqrt(second / fix_two) + ADAM_EPS) + decay * weight
    )
    return (updated, first, second, updated.astype(bf16))


def square_sum(arrays):
    total = jnp.zeros((), f32)
    for member in arrays:
        total = total + jnp.sum(member * member)
    return total


def swap(x, axis, k):
    n = lax.axis_size(axis)
    return lax.ppermute(x, axis, [(i, i ^ k) for i in range(n)])


def exchange(x, axis):
    return lax.all_to_all(x, axis, split_axis=0, concat_axis=0, tiled=True)


def shards(
    tokens,
    cotangent,
    expert_ids,
    priority,
    step,
    attn_qkv,
    attn_out,
    router,
    norms,
    expert_in,
    expert_out,
    moments_qkv,
    moments_out,
    moments_router,
    moments_norms,
    moments_in,
    moments_exp,
):
    tok_dev = tokens.shape[0]
    groups = lax.axis_size("expert")
    n_dp = lax.axis_size("dp")
    assert expert_in.shape[0] == 1 and n_dp == 4 and tok_dev % SEQ == 0
    experts = groups
    per = experts // n_dp
    cap = (tok_dev + experts - 1) // experts
    pad = -(-(cap + 2) // 16) * 16
    n = tok_dev // SEQ
    devices = n_dp * groups
    me_dp = lax.axis_index("dp").astype(i32)
    me_e = lax.axis_index("expert").astype(i32)
    core = me_e % 2
    where = jnp.stack([me_dp, core, me_e])

    qkvT = attn_qkv.astype(bf16).T
    ob = attn_out.astype(bf16)
    misc = jnp.concatenate(
        [
            router.astype(bf16).T,
            norms.astype(bf16).reshape(1, D),
            jnp.zeros((16 - per - 1, D), bf16),
        ],
        axis=0,
    )
    own = jnp.stack(
        [jnp.concatenate([qkvT[:192], ob[:64], misc]), jnp.concatenate([qkvT[192:], ob[64:], misc])]
    )
    half = lax.dynamic_index_in_dim(own, core, 0, keepdims=False)
    got = [swap(half, "dp", k) for k in (1, 2, 3)]
    sib = [swap(g, "expert", 1) for g in got]
    wT, ow, rT, nm = assemble(where, own, got, sib, experts)

    own_in = expert_in[0].astype(bf16)
    own_exp = expert_out[0].astype(bf16)
    iw = jnp.stack([own_in] + [swap(own_in, "dp", k) for k in (1, 2, 3)])
    xw = jnp.stack([own_exp] + [swap(own_exp, "dp", k) for k in (1, 2, 3)])

    ids = expert_ids.reshape(n, SEQ, 2).transpose(0, 2, 1)
    prio = priority.reshape(n, SEQ, 2).transpose(0, 2, 1)
    pos, cols, up_slots = slots(ids, prio, cotangent, experts, cap, pad)
    up = exchange(up_slots, "expert")
    proj, ctxT, lse, mid, sec, gatesT = attend(tokens, wT, ow, rT, nm)
    rows = exchange(spread(pos, sec, pad), "expert")
    gb, dr, din, dexpT = run_experts(where, rows, up, iw, xw, rT, cap)
    dr = exchange(dr, "expert")
    gb = exchange(gb, "expert")
    dmid, dn_two, drT = combine(dr, cols, gatesT, sec, mid, cotangent, rT, nm, cap)
    grad_input, dqkv, dout, dn_one = attend_back(tokens, dmid, proj, ctxT, lse, wT, ow, nm)
    activations = finish(gb, cols, mid)

    share_in = din[0]
    share_expT = dexpT[0]
    for k in (1, 2, 3):
        share_in = share_in + swap(din[k].astype(bf16), "dp", k).astype(f32)
        share_expT = share_expT + swap(dexpT[k].astype(bf16), "dp", k).astype(f32)
    share_exp = share_expT.T

    dn = jnp.concatenate([dn_one, dn_two], axis=0)
    blocks = []
    for d in range(n_dp):
        rws = [dqkv[:, d * 384 + j * 128 : d * 384 + (j + 1) * 128] for j in range(3)]
        rws += [dout[d * 128 : (d + 1) * 128, j * 128 : (j + 1) * 128] for j in range(4)]
        rws += [drT[d * per : (d + 1) * per, j * 128 : (j + 1) * 128] for j in range(4)]
        rws += [dn[:, d * 128 : (d + 1) * 128]]
        blocks.append(jnp.concatenate(rws, axis=0))
    used = blocks[0].shape[0]
    piece = -(-used // (groups * 16)) * 16
    packed = jnp.stack(blocks).astype(bf16)
    packed = jnp.pad(packed, ((0, 0), (0, groups * piece - used), (0, 0)))
    packed = packed.reshape(n_dp, groups, piece, 128).transpose(1, 0, 2, 3)
    packed = exchange(packed, "expert").astype(f32).sum(0).astype(bf16)
    packed = exchange(packed, "dp").astype(f32).sum(0)
    term = square_sum((packed, share_in, share_expT))
    packed = exchange(
        jnp.broadcast_to(packed.astype(bf16)[None], (groups, piece, 128)), "expert"
    )
    packed = packed.reshape(groups * piece, 128).astype(f32)
    share_qkv = jnp.concatenate([packed[j * 512 : (j + 1) * 512] for j in range(3)], axis=1)
    at = 1536
    share_out = jnp.concatenate(
        [packed[at + j * 128 : at + (j + 1) * 128] for j in range(4)], axis=1
    )
    at += 512
    share_router = jnp.concatenate(
        [packed[at + j * per : at + (j + 1) * per] for j in range(4)], axis=1
    ).T
    at += 4 * per
    share_norms = packed[at : at + 4]

    terms = exchange(jnp.full((devices, 1, 128), term, f32), ("dp", "expert"))
    grad_norm = jnp.sqrt(jnp.sum(terms[:, 0, 0]))
    factor = MAX_NORM / grad_norm
    rates = step_rates(experts)
    step_float = step.astype(f32)
    outs = [activations, grad_input, grad_norm]
    outs += adam_update(
        attn_qkv, moments_qkv, share_qkv, factor, rates[0], DECAY_RATE, step_float
    )
    outs += adam_update(
        attn_out, moments_out, share_out, factor, rates[1], DECAY_RATE, step_float
    )
    outs += adam_update(
        router, moments_router, share_router, factor, rates[2], DECAY_RATE, step_float
    )
    outs += adam_update(norms, moments_norms, share_norms, factor, rates[3], 0.0, step_float)
    outs += adam_update(
        expert_in, moments_in, share_in[None], factor, rates[4], DECAY_RATE, step_float
    )
    outs += adam_update(
        expert_out, moments_exp, share_exp[None], factor, rates[5], DECAY_RATE, step_float
    )
    return tuple(outs)


def solution(mesh):
    tok = P(("dp", "expert"), None)
    cols = P(None, "dp")
    rows = P("dp", None)
    e_in = P("expert", None, "dp")
    e_out = P("expert", "dp", None)
    in_specs = (
        tok,
        tok,
        tok,
        tok,
        P(),
        cols,
        rows,
        cols,
        cols,
        e_in,
        e_out,
        P(None, None, "dp"),
        P(None, "dp", None),
        P(None, None, "dp"),
        P(None, None, "dp"),
        P(None, "expert", None, "dp"),
        P(None, "expert", "dp", None),
    )
    out_specs = (
        (tok, tok, P())
        + (cols,) * 4
        + (rows,) * 4
        + (cols,) * 4
        + (cols,) * 4
        + (e_in,) * 4
        + (e_out,) * 4
    )
    return jax.shard_map(shards, mesh=mesh, in_specs=in_specs, out_specs=out_specs, check_vma=False)
```

```python
import functools

import jax
import jax.numpy as jnp
from jax import lax
from jax.experimental import pallas as pl
from jax.experimental.pallas import tpu as pltpu
from jax.sharding import PartitionSpec as P

D = 512
HEADS = 8
HEAD = 64
FF = 2048
SEQ = 720

EPS_NORM = 1e-06
BETA_ONE = 0.9
BETA_TWO = 0.999
ADAM_EPS = 1e-08
DECAY_RATE = 0.1
MAX_NORM = 1.0

f32, bf16, i32 = jnp.float32, jnp.bfloat16, jnp.int32
NN = (((1,), (0,)), ((), ()))
NT = (((1,), (1,)), ((), ()))
TN = (((0,), (0,)), ((), ()))
LOG2E = 1.4426950408889634
SCALE = HEAD**-0.5
FAR = 1 << 20
VMEM_LIMIT = 60 * 2**20


def mm(a, b, dims=NN):
    return lax.dot_general(a, b, dims, preferred_element_type=f32)


def full(a):
    return pl.BlockSpec(a.shape, lambda *i: (0,) * a.ndim)


def whole(*shape):
    return pl.BlockSpec(shape, lambda *i: (0,) * len(shape))


def per_image(cols):
    return pl.BlockSpec((SEQ, cols), lambda i: (i, 0))


def per_image_t(rows):
    return pl.BlockSpec((1, rows, SEQ), lambda i: (i, 0, 0))


def sds(shape, dtype):
    return jax.ShapeDtypeStruct(shape, dtype)


SMEM = pl.BlockSpec(memory_space=pltpu.SMEM)


def call(body, name, us=0.1, **kw):
    return pl.pallas_call(
        body,
        name=name,
        compiler_params=pltpu.CompilerParams(vmem_limit_bytes=VMEM_LIMIT),
        cost_estimate=pl.CostEstimate(flops=int(us * 10**9), bytes_accessed=10**5, transcendentals=0),
        **kw,
    )


def normalize(v):
    c = v - jnp.mean(v, axis=-1, keepdims=True)
    r = lax.rsqrt(jnp.mean(c * c, axis=-1, keepdims=True) + EPS_NORM)
    return c * r, r


def assemble_kernel(experts, where, got, misc, near, far, wT, ow, rT, nm):
    me, slot = where[0], where[2] % 8
    per = experts // 4
    for c in range(4):
        for b in range(2):
            s = slot ^ (2 * c + b)
            for k in range(4):
                d = me ^ k
                if b == 0:
                    piece = got[k] if c == 0 else near[c - 1, k]
                else:
                    piece = far[c, k]
                lo = pl.multiple_of(d * 384 + s * 48, 16)
                wT[pl.ds(lo, 48), :] = piece[:48, :]
                lo = pl.multiple_of(d * 128 + s * 16, 16)
                ow[pl.ds(lo, 16), :] = piece[48:64, :]
    for d in range(4):
        for k in range(4):

            @pl.when((me ^ k) == d)
            def _(d=d, k=k):
                rest = misc[k].astype(f32)
                rT[d * per : (d + 1) * per, :] = rest[:per, :]
                for j in range(4):
                    nm[j : j + 1, d * 128 : (d + 1) * 128] = rest[
                        per : per + 1, j * 128 : (j + 1) * 128
                    ]


def assemble(where, got, misc, near, far, experts):
    args = (got, misc, near, far)
    return call(
        functools.partial(assemble_kernel, experts),
        "assemble",
        in_specs=[SMEM] + [whole(*a.shape) for a in args],
        out_specs=[whole(3 * D, D), whole(D, D), whole(experts, D), whole(4, D)],
        out_shape=[
            sds((3 * D, D), bf16),
            sds((D, D), bf16),
            sds((experts, D), f32),
            sds((4, D), f32),
        ],
    )(where, *args)


def dispatch(pos, x, pad, step):
    io = lax.broadcasted_iota(i32, (pad, SEQ), 0)
    acc = None
    for i in range(pos.shape[0]):
        hit = jnp.where(io == pos[i, pl.ds(step, 1), :], 1.0, 0.0).astype(bf16)
        part = mm(hit, x[i * SEQ : (i + 1) * SEQ, :])
        acc = part if acc is None else acc + part
    return acc.astype(bf16)


def slots_kernel(cap, pad, where, ids, prio, cot, pos, cols, u):
    step = pl.program_id(0)
    me = where[2]
    n = ids.shape[0]
    experts = pos.shape[1]
    nh = -(-(2 * n * SEQ) // 2048) * 16

    @pl.when(step == 0)
    def _():
        hi_io = lax.broadcasted_iota(i32, (nh, SEQ), 0)
        lo_io = lax.broadcasted_iota(i32, (128, SEQ), 0)

        def hot(i, k):
            q = prio[i, k : k + 1, :]
            return hi_io == (q >> 7), lo_io == (q & 127)

        table = jnp.zeros((nh, 128), f32)
        for i in range(n):
            for k in range(2):
                a, b = hot(i, k)
                ex = ((ids[i, k : k + 1, :] ^ me) + 1).astype(f32)
                table += mm(
                    jnp.where(a, 1.0, 0.0).astype(bf16), jnp.where(b, ex, 0.0).astype(bf16), NT
                )
        upper = (
            lax.broadcasted_iota(i32, (128, 128), 0) < lax.broadcasted_iota(i32, (128, 128), 1)
        ).astype(bf16)
        lower = (
            lax.broadcasted_iota(i32, (nh, nh), 1) < lax.broadcasted_iota(i32, (nh, nh), 0)
        ).astype(bf16)
        ones = jnp.ones((128, 128), bf16)
        rank = jnp.zeros((nh, 128), f32)
        for e in range(experts):
            m = (table == float(e + 1)).astype(f32)
            mb = m.astype(bf16)
            rank += m * (mm(mb, upper) + mm(mm(lower, mb).astype(bf16), ones))
        ri = jnp.minimum(rank.astype(i32), 16383)
        rlo = (ri & 127).astype(bf16)
        rhi = (ri >> 7).astype(bf16)
        eio = lax.broadcasted_iota(i32, (experts, SEQ), 0)
        for i in range(n):
            out = jnp.full((experts, SEQ), FAR, i32)
            flat = []
            for k in range(2):
                a, b = hot(i, k)
                bb = jnp.where(b, 1.0, 0.0).astype(bf16)
                x = mm(rlo, bb) + 128.0 * mm(rhi, bb)
                r = jnp.sum(jnp.where(a, x, 0.0), axis=0, keepdims=True).astype(i32)
                ex = ids[i, k : k + 1, :] ^ me
                keep = r < cap
                out = jnp.where((eio == ex) & keep, r, out)
                flat.append(jnp.where(keep, ex * pad + r, FAR))
            pos[i] = out
            fl = jnp.concatenate(flat + [jnp.zeros((6, SEQ), i32)], axis=0).astype(f32)
            cols[i * SEQ : (i + 1) * SEQ, :] = fl.T.astype(i32)

    u[pl.ds(step ^ me, 1)] = dispatch(pos, cot, pad, step)[None]


def slots(where, ids, prio, cot, experts, cap, pad):
    n = ids.shape[0]
    t = n * SEQ
    return call(
        functools.partial(slots_kernel, cap, pad),
        "slots",
        grid=(experts,),
        in_specs=[SMEM, full(ids), full(prio), full(cot)],
        out_specs=[whole(n, experts, SEQ), whole(t, 8), whole(experts, pad, D)],
        out_shape=[
            sds((n, experts, SEQ), i32),
            sds((t, 8), i32),
            sds((experts, pad, D), bf16),
        ],
    )(where, ids, prio, cot)


def spread_kernel(pad, pos, x, *outs):
    step = pl.program_id(0)
    block = dispatch(pos, x, pad, step)
    for j, out in enumerate(outs):

        @pl.when(step == j)
        def _(out=out):
            out[...] = block


def spread(pos, x, pad):
    experts = pos.shape[1]
    return call(
        functools.partial(spread_kernel, pad),
        "spread",
        grid=(experts,),
        in_specs=[full(pos), full(x)],
        out_specs=[whole(pad, D)] * experts,
        out_shape=[sds((pad, D), bf16)] * experts,
    )(pos, x)


def head_masks():
    lane = lax.broadcasted_iota(i32, (1, 128), 1)
    return (lane < 64).astype(bf16), (lane >= 64).astype(bf16)


def attend_kernel(tok, wT, ow, rT, nm, proj, ctxT, lse, mid, sec, gatesT, vT, ct):
    x = tok[...].astype(f32)
    xh, _ = normalize(x)
    fb = (xh * nm[0:1, :] + nm[1:2, :]).astype(bf16)
    proj[...] = mm(fb, wT[...], NT).astype(bf16)
    vT[...] = proj[:, 2 * D :].T
    masks = head_masks()
    for h in range(HEADS):
        p = h // 2
        qm = proj[:, p * 128 : (p + 1) * 128] * masks[h % 2]
        kk = proj[:, D + p * 128 : D + (p + 1) * 128]
        s = mm(kk, qm, NT)
        m = jnp.max(s, axis=0, keepdims=True)
        e = jnp.exp2((s - m) * (SCALE * LOG2E))
        total = jnp.sum(e, axis=0, keepdims=True)
        c = mm(vT[h * 64 : (h + 1) * 64, :], e.astype(bf16))
        ct[h * 64 : (h + 1) * 64, :] = (c * (1.0 / total)).astype(bf16)
        lse[0, h : h + 1, :] = m * (SCALE * LOG2E) + jnp.log2(total)
    ctxT[0] = ct[...]
    middle = x + mm(ct[...], ow[...], TN)
    mid[...] = middle
    xh2, _ = normalize(middle)
    s2 = (xh2 * nm[2:3, :] + nm[3:4, :]).astype(bf16)
    sec[...] = s2
    logits = mm(rT[...].astype(bf16), s2, NT)
    ex = jnp.exp(logits - jnp.max(logits, axis=0, keepdims=True))
    gatesT[0] = ex / jnp.sum(ex, axis=0, keepdims=True)


def attend(tok, wT, ow, rT, nm):
    t = tok.shape[0]
    n = t // SEQ
    experts = rT.shape[0]
    return call(
        attend_kernel,
        "attend",
        grid=(n,),
        in_specs=[per_image(D), full(wT), full(ow), full(rT), full(nm)],
        out_specs=[
            per_image(3 * D),
            per_image_t(D),
            per_image_t(HEADS),
            per_image(D),
            per_image(D),
            per_image_t(experts),
        ],
        out_shape=[
            sds((t, 3 * D), bf16),
            sds((n, D, SEQ), bf16),
            sds((n, HEADS, SEQ), f32),
            sds((t, D), f32),
            sds((t, D), bf16),
            sds((n, experts, SEQ), f32),
        ],
        scratch_shapes=[pltpu.VMEM((D, SEQ), bf16), pltpu.VMEM((D, SEQ), bf16)],
    )(tok, wT, ow, rT, nm)


def normal_cdf(h):
    t = 1.0 / (1.0 + (0.3275911 * 0.7071067811865476) * jnp.abs(h))
    g = jnp.exp2((-0.5 * LOG2E) * h * h)
    poly = t * (
        0.5 * 0.254829592
        + t
        * (
            0.5 * -0.284496736
            + t * (0.5 * 1.421413741 + t * (0.5 * -1.453152027 + t * (0.5 * 1.061405429)))
        )
    )
    q = poly * g
    return jnp.where(h >= 0, 1.0 - q, q), g


def experts_kernel(cap, ks, where, *refs):
    nb = len(ks)
    rows, (u, gw, rT) = refs[:nb], refs[nb : nb + 3]
    gb, dr = refs[nb + 3 : 2 * nb + 3], refs[2 * nb + 3 : 3 * nb + 3]
    xs, db, act, dh = refs[3 * nb + 3 : 3 * nb + 7]
    s = pl.program_id(0)
    pad = rows[0].shape[0]
    me = where[2]
    chunks, _, cols = gw.shape
    iw = [gw.at[j, :D] for j in range(chunks)]
    xw = [gw.at[j, D:] for j in range(chunks)]
    for i in range(nb // 2):

        @pl.when(s == i)
        def _(i=i):
            xs[:pad, :] = rows[2 * i][...]
            xs[pad:, :] = rows[2 * i + 1][...]
            db[:pad, :] = u[me ^ ks[2 * i]]
            db[pad:, :] = u[me ^ ks[2 * i + 1]]

    x = xs[...]
    upf = db[...].astype(f32)
    logits = mm(x, rT[...].astype(bf16), NT)
    ex = jnp.exp(logits - jnp.max(logits, axis=1, keepdims=True))
    mine = lax.broadcasted_iota(i32, ex.shape, 1) == me
    gate = jnp.sum(jnp.where(mine, ex, 0.0), axis=1, keepdims=True) / jnp.sum(
        ex, axis=1, keepdims=True
    )
    d = (gate * upf).astype(bf16)
    db[...] = d
    back = None
    drow = None
    for j in range(chunks):
        h = mm(x, iw[j][...])
        cdf, g = normal_cdf(h)
        a = (h * cdf).astype(bf16)
        act[:, j * cols : (j + 1) * cols] = a
        part = mm(a, xw[j][...])
        back = part if back is None else back + part
        dact = mm(d, xw[j][...], NT)
        dj = (dact * (cdf + h * g * 0.3989422804014327)).astype(bf16)
        dh[:, j * cols : (j + 1) * cols] = dj
        part = mm(dj, iw[j][...], NT)
        drow = part if drow is None else drow + part
    b = back.astype(bf16).astype(f32)
    gback = (gate * b).astype(bf16)
    prod = upf * b
    first = prod.astype(bf16)
    rest = (prod - first.astype(f32)).astype(bf16)
    ones = jnp.ones((8, D), bf16)
    dgs = (mm(ones, first, NT) + mm(ones, rest, NT))[0:1, :]
    line = lax.broadcasted_iota(i32, (pad, D), 0)
    for o in range(2):
        dg = dgs[:, o * pad : (o + 1) * pad]
        dg = jnp.concatenate([dg, jnp.zeros((1, D - pad), f32)], axis=1)
        top = dg.astype(bf16).astype(f32)
        part = drow[o * pad : (o + 1) * pad, :]
        part = jnp.where(line == cap, top, jnp.where(line == cap + 1, dg - top, part))
        part = part.astype(bf16)
        for i in range(nb // 2):

            @pl.when(s == i)
            def _(i=i, o=o, part=part):
                dr[2 * i + o][...] = part
                gb[2 * i + o][...] = gback[o * pad : (o + 1) * pad, :]


def run_experts(where, ks, rows, u, gw, rT, cap):
    nb = len(ks)
    pad = rows[0].shape[0]
    chunks, _, cols = gw.shape
    pair = lambda c: pl.BlockSpec((2 * pad, c), lambda i: (i, 0))
    blk = sds((pad, D), bf16)
    out = call(
        functools.partial(experts_kernel, cap, ks),
        "experts",
        us=8 * nb,
        grid=(nb // 2,),
        in_specs=[SMEM] + [whole(pad, D)] * nb + [full(u), full(gw), full(rT)],
        out_specs=[whole(pad, D)] * (2 * nb) + [pair(D), pair(D), pair(FF), pair(FF)],
        out_shape=[blk] * (2 * nb)
        + [sds((nb * pad, D), bf16)] * 2
        + [sds((nb * pad, chunks * cols), bf16)] * 2,
    )(where, *rows, u, gw, rT)
    return out[:nb], out[nb : 2 * nb], out[2 * nb :]


def weights_kernel(groups, *refs):
    xs, dbs, acts, dhs = (refs[i * groups : (i + 1) * groups] for i in range(4))
    out, xT, dT = refs[4 * groups :]
    pieces = []
    at = 0
    for g in range(groups):
        step = xT.shape[2]
        for r in range(xs[g].shape[0] // step):
            pieces.append((g, r * step, at))
            at += 1

    @pl.when(pl.program_id(0) == 0)
    def _():
        for g, r, p in pieces:
            xT[p] = xs[g][r : r + xT.shape[2], :].T
            dT[p] = dbs[g][r : r + xT.shape[2], :].T

    di = None
    de = None
    for g, r, p in pieces:
        part = mm(xT[p], dhs[g][r : r + xT.shape[2], :])
        di = part if di is None else di + part
        part = mm(dT[p], acts[g][r : r + xT.shape[2], :])
        de = part if de is None else de + part
    out[0, :D, :] = di.astype(bf16)
    out[0, D:, :] = de.astype(bf16)


def weight_grads(kept, pad):
    groups = len(kept)
    ins = [k[i] for i in range(4) for k in kept]
    total = sum(k[0].shape[0] for k in kept) // (2 * pad)
    col = lambda a: pl.BlockSpec((a.shape[0], D), lambda j: (0, j))
    return call(
        functools.partial(weights_kernel, groups),
        "weight_grads",
        grid=(FF // D,),
        in_specs=[full(a) for a in ins[: 2 * groups]] + [col(a) for a in ins[2 * groups :]],
        out_specs=pl.BlockSpec((1, 2 * D, D), lambda j: (j, 0, 0)),
        out_shape=sds((FF // D, 2 * D, D), bf16),
        scratch_shapes=[pltpu.VMEM((total, D, 2 * pad), bf16)] * 2,
    )(*ins)


def pick(cols, count):
    io = lax.broadcasted_iota(i32, (SEQ, count), 1)
    return jnp.where((io == cols[:, 0:1]) | (io == cols[:, 1:2]), 1.0, 0.0).astype(bf16)


def stack_once(blocks, scratch):
    pad = blocks[0].shape[0]

    @pl.when(pl.program_id(0) == 0)
    def _():
        for j, block in enumerate(blocks):
            scratch[j * pad : (j + 1) * pad, :] = block[...]


def combine_kernel(cap, experts, where, *refs):
    cols, gatesT, sec, mid, cot, rT, nm, dmid, dn, drT, dr, dgs = refs[experts:]
    stack_once(refs[:experts], dr)
    i = pl.program_id(0)
    me = where[2]
    pad = dr.shape[0] // experts
    hits = pick(cols[...], dr.shape[0])
    ds = mm(hits, dr[...])
    base = cap // 16 * 16
    off = cap - base
    for e in range(experts):
        two = dr[e * pad + base : (e + 1) * pad, :pad]
        x = mm(two, hits[:, e * pad : (e + 1) * pad], NT)
        dgs[pl.ds(e ^ me, 1), :] = x[off : off + 1, :] + x[off + 1 : off + 2, :]
    dg = dgs[...]
    g = gatesT[0]
    dl = (g * (dg - jnp.sum(g * dg, axis=0, keepdims=True))).astype(bf16)
    ds = ds + mm(dl, rT[...].astype(bf16), TN)
    xh, r = normalize(mid[...])
    y = ds * nm[2:3, :]
    dmid[...] = cot[...].astype(f32) + r * (
        y - jnp.mean(y, axis=-1, keepdims=True) - xh * jnp.mean(y * xh, axis=-1, keepdims=True)
    )
    gg = jnp.sum(ds * xh, axis=0, keepdims=True)
    gs = jnp.sum(ds, axis=0, keepdims=True)
    dR = mm(dl, sec[...])

    @pl.when(i == 0)
    def _():
        dn[0:1, :] = gg
        dn[1:2, :] = gs
        drT[...] = dR

    @pl.when(i > 0)
    def _():
        dn[0:1, :] += gg
        dn[1:2, :] += gs
        drT[...] += dR


def combine(where, blocks, cols, gatesT, sec, mid, cot, rT, nm, cap):
    experts = len(blocks)
    pad = blocks[0].shape[0]
    t = cols.shape[0]
    return call(
        functools.partial(combine_kernel, cap, experts),
        "combine",
        grid=(t // SEQ,),
        in_specs=[SMEM]
        + [whole(pad, D)] * experts
        + [
            per_image(8),
            per_image_t(experts),
            per_image(D),
            per_image(D),
            per_image(D),
            full(rT),
            full(nm),
        ],
        out_specs=[per_image(D), whole(2, D), whole(experts, D)],
        out_shape=[sds((t, D), f32), sds((2, D), f32), sds((experts, D), f32)],
        scratch_shapes=[pltpu.VMEM((experts * pad, D), bf16), pltpu.VMEM((experts, SEQ), f32)],
    )(where, *blocks, cols, gatesT, sec, mid, cot, rT, nm)


def finish_kernel(experts, *refs):
    cols, mid, out, gb = refs[experts:]
    stack_once(refs[:experts], gb)
    out[...] = (mid[...] + mm(pick(cols[...], gb.shape[0]), gb[...])).astype(bf16)


def finish(blocks, cols, mid):
    experts = len(blocks)
    pad = blocks[0].shape[0]
    t = cols.shape[0]
    return call(
        functools.partial(finish_kernel, experts),
        "finish",
        grid=(t // SEQ,),
        in_specs=[whole(pad, D)] * experts + [per_image(8), per_image(D)],
        out_specs=per_image(D),
        out_shape=sds((t, D), bf16),
        scratch_shapes=[pltpu.VMEM((experts * pad, D), bf16)],
    )(*blocks, cols, mid)


TILES = (
    (((0, 0), (0, 1)), ((0, 4), (0, 5)), ((0, 8), (1, 2)), ((0, 9), (1, 3))),
    (((0, 2), (1, 0)), ((0, 3), (1, 1)), ((0, 6), (0, 7)), ((0, 10), (0, 11))),
)


def attend_back_kernel(part, tok, dmid, proj, ctxT, lse, ow, nm, dproj, packed, kT, dqT, gq, go):
    i = pl.program_id(0)
    half = D // 2
    base = part * half
    da = dmid[...].astype(bf16)
    owp = ow[base : base + half, :]
    do = mm(da, owp, NT).astype(bf16)
    doT = mm(owp, da, NT).astype(bf16)
    prod = doT.astype(f32) * ctxT[0, base : base + half, :].astype(f32)
    kT[...] = proj[:, D + base : D + base + half].T
    masks = head_masks()
    low = lax.broadcasted_iota(i32, (SEQ, 128), 1) < 64
    for p in range(HEADS // 4):
        dv = []
        dk = []
        lo = base + p * 128
        qq = proj[:, lo : lo + 128]
        kk = proj[:, D + lo : D + lo + 128]
        vv = proj[:, 2 * D + lo : 2 * D + lo + 128]
        dd = do[:, p * 128 : (p + 1) * 128]
        for j in range(2):
            hl = 2 * p + j
            h = part * (HEADS // 2) + hl
            s = mm(kk, qq * masks[j], NT)
            prob = jnp.exp2(s * (SCALE * LOG2E) - lse[0, h : h + 1, :])
            dprob = mm(vv, dd * masks[j], NT)
            dv.append(mm(prob.astype(bf16), dd))
            inner = jnp.sum(prod[hl * 64 : (hl + 1) * 64, :], axis=0, keepdims=True)
            ds = (prob * (dprob - inner)).astype(bf16)
            dk.append(mm(ds, qq))
            dqT[hl * 64 : (hl + 1) * 64, :] = (
                mm(kT[hl * 64 : (hl + 1) * 64, :], ds) * SCALE
            ).astype(bf16)
        at = p * 128
        dproj[:, 2 * half + at : 2 * half + at + 128] = jnp.where(low, dv[0], dv[1]).astype(bf16)
        dproj[:, half + at : half + at + 128] = (jnp.where(low, dk[0], dk[1]) * SCALE).astype(bf16)
    dproj[:, :half] = dqT[...].T
    xh, _ = normalize(tok[...].astype(f32))
    fb = (xh * nm[0:1, :] + nm[1:2, :]).astype(bf16)
    dq = mm(fb, dproj[...], TN)
    other = (1 - part) * half
    do_ = mm(ctxT[0, other : other + half, :], da)

    @pl.when(i == 0)
    def _():
        gq[...] = dq
        go[...] = do_

    @pl.when(i > 0)
    def _():
        gq[...] += dq
        go[...] += do_

    @pl.when(i == pl.num_programs(0) - 1)
    def _():
        groups, _, r, _ = packed.shape
        for d in range(4):
            for t in range(2):
                kind, c = TILES[part][d][t]
                if kind == 0:
                    third, at = c // 4, c % 4 - 2 * part
                    tile = gq[:, third * half + at * 128 : third * half + (at + 1) * 128]
                else:
                    row = (c - (2 - 2 * part)) * 128
                    tile = jnp.concatenate(
                        [go[row : row + 128, j * 128 : (j + 1) * 128] for j in range(4)], axis=0
                    )
                tile = tile.astype(bf16)
                for m in range(512 // r):
                    packed[t * (512 // r) + m, d] = tile[m * r : (m + 1) * r, :]


def attend_back(part, groups, tok, dmid, proj, ctxT, lse, ow, nm):
    t = tok.shape[0]
    r = 1024 // groups
    return call(
        functools.partial(attend_back_kernel, part),
        "attend_back",
        grid=(t // SEQ,),
        in_specs=[
            per_image(D),
            per_image(D),
            per_image(3 * D),
            per_image_t(D),
            per_image_t(HEADS),
            full(ow),
            full(nm),
        ],
        out_specs=[per_image(3 * D // 2), whole(groups, 4, r, 128)],
        out_shape=[sds((t, 3 * D // 2), bf16), sds((groups, 4, r, 128), bf16)],
        scratch_shapes=[
            pltpu.VMEM((D // 2, SEQ), bf16),
            pltpu.VMEM((D // 2, SEQ), bf16),
            pltpu.VMEM((D, 3 * D // 2), f32),
            pltpu.VMEM((D // 2, D), f32),
        ],
    )(tok, dmid, proj, ctxT, lse, ow, nm)


def enter_kernel(tok, dmid, dp0, dp1, wT, nm, gin, dn):
    i = pl.program_id(0)
    half = D // 2
    df = None
    for part, dp in enumerate((dp0, dp1)):
        for third in range(3):
            lo = third * D + part * half
            term = mm(dp[:, third * half : (third + 1) * half], wT[lo : lo + half, :])
            df = term if df is None else df + term
    xh, r = normalize(tok[...].astype(f32))
    y = df * nm[0:1, :]
    gin[...] = dmid[...] + r * (
        y - jnp.mean(y, axis=-1, keepdims=True) - xh * jnp.mean(y * xh, axis=-1, keepdims=True)
    )
    gg = jnp.sum(df * xh, axis=0, keepdims=True)
    gs = jnp.sum(df, axis=0, keepdims=True)

    @pl.when(i == 0)
    def _():
        dn[0:1, :] = gg
        dn[1:2, :] = gs

    @pl.when(i > 0)
    def _():
        dn[0:1, :] += gg
        dn[1:2, :] += gs


def enter(tok, dmid, dp0, dp1, wT, nm):
    t = tok.shape[0]
    return call(
        enter_kernel,
        "enter",
        grid=(t // SEQ,),
        in_specs=[
            per_image(D),
            per_image(D),
            per_image(3 * D // 2),
            per_image(3 * D // 2),
            full(wT),
            full(nm),
        ],
        out_specs=[per_image(D), whole(2, D)],
        out_shape=[sds((t, D), f32), sds((2, D), f32)],
    )(tok, dmid, dp0, dp1, wT, nm)


def step_rates(experts):
    return (
        D ** (-0.5),
        2.0 ** (-0.5),
        (2 * D) ** (-0.5),
        0.1,
        D ** (-0.5),
        2.0 * experts / (1.2 * FF**0.5),
    )


def adam_update(weight, moments, grad, factor, rate, decay, fixes):
    clipped = grad * factor
    first = BETA_ONE * moments[0] + (1.0 - BETA_ONE) * clipped
    second = BETA_TWO * moments[1] + (1.0 - BETA_TWO) * clipped * clipped
    updated = weight - rate * (
        first / fixes[0] / (jnp.sqrt(second / fixes[1]) + ADAM_EPS) + decay * weight
    )
    return (updated, first, second, updated.astype(bf16))


def adam_kernel(rates, where, nums, *refs):
    parts, owned = refs[:2], refs[2]
    weights, moments, outs = refs[3:7], refs[7:11], refs[11:27]
    gq, go = refs[27:]
    i = pl.program_id(0)

    @pl.when(i == 0)
    def _():
        for d in range(4):

            @pl.when(where[0] == d)
            def _(d=d):
                for part in range(2):
                    for t in range(2):
                        kind, c = TILES[part][d][t]
                        if kind == 0:
                            at = (c - 3 * d) * 128
                            gq[:, at : at + 128] = parts[part][t * 512 : (t + 1) * 512, :]
                        else:
                            for j in range(4):
                                lo = t * 512 + j * 128
                                go[:, j * 128 : (j + 1) * 128] = parts[part][lo : lo + 128, :]

    rows_q, rows_o = weights[0].shape[0], weights[1].shape[0]
    rows_e = weights[2].shape[1]
    grads = (
        gq[pl.ds(i * rows_q, rows_q), :].astype(f32),
        go[pl.ds(i * rows_o, rows_o), :].astype(f32),
        owned[pl.ds(i * rows_e, rows_e), :],
        owned[D:, pl.ds(pl.multiple_of(i * rows_e, 128), rows_e)].T,
    )
    factor = nums[0]
    fixes = (nums[1], nums[2])
    for j in range(4):
        lead = j >= 2
        w = weights[j][0] if lead else weights[j][...]
        m = (moments[j][0, 0], moments[j][1, 0]) if lead else (moments[j][0], moments[j][1])
        new = adam_update(w, m, grads[j], factor, rates[j], DECAY_RATE, fixes)
        for o in range(4):
            if lead:
                outs[4 * j + o][0] = new[o]
            else:
                outs[4 * j + o][...] = new[o]


def adam(rates, where, nums, part0, part1, owned, weights, moments):
    steps = 4
    specs = []
    mspecs = []
    for w in weights:
        if w.ndim == 2:
            specs.append(pl.BlockSpec((w.shape[0] // steps, w.shape[1]), lambda i: (i, 0)))
            mspecs.append(pl.BlockSpec((2, w.shape[0] // steps, w.shape[1]), lambda i: (0, i, 0)))
        else:
            specs.append(
                pl.BlockSpec((1, w.shape[1] // steps, w.shape[2]), lambda i: (0, i, 0))
            )
            mspecs.append(
                pl.BlockSpec((2, 1, w.shape[1] // steps, w.shape[2]), lambda i: (0, 0, i, 0))
            )
    return call(
        functools.partial(adam_kernel, rates),
        "adam",
        grid=(steps,),
        in_specs=[SMEM, SMEM, full(part0), full(part1), full(owned)] + specs + mspecs,
        out_specs=[sp for sp in specs for _ in range(4)],
        out_shape=[sds(w.shape, dt) for w in weights for dt in (f32, f32, f32, bf16)],
        scratch_shapes=[pltpu.VMEM((D, 384), bf16), pltpu.VMEM((128, D), bf16)],
    )(where, nums, part0, part1, owned, *weights, *moments)


def swap(x, axis, k):
    n = lax.axis_size(axis)
    return lax.ppermute(x, axis, [(i, i ^ k) for i in range(n)])


def exchange(x, axis):
    return lax.all_to_all(x, axis, split_axis=0, concat_axis=0, tiled=True)


def total(blocks):
    return functools.reduce(lambda a, b: a + b, [b.astype(f32) for b in blocks])


def at(x, i):
    return lax.dynamic_index_in_dim(x, i, 0, keepdims=False)


def fence(*groups):
    flat, tree = jax.tree.flatten(groups)
    return jax.tree.unflatten(tree, lax.optimization_barrier(tuple(flat)))


class Sums:
    def __init__(self, me_dp, me_e, groups):
        self.d, self.core, self.chip = me_dp, me_e % 2, me_e // 2
        self.chips = groups // 2

    def send_core(self, packed):
        groups, n_dp, r, c = packed.shape
        x = packed.reshape(2, self.chips, n_dp, r, c)
        self.own = at(x, self.core)
        return [swap(at(x, 1 - self.core), "expert", 1)]

    def take_core(self, got):
        self.own = total([self.own] + got).astype(bf16)

    def send_chip(self):
        return [swap(at(self.own, self.chip ^ k), "expert", 2 * k) for k in range(1, self.chips)]

    def take_chip(self, got):
        self.own = total([at(self.own, self.chip)] + got).astype(bf16)

    def send_dp(self):
        return [swap(at(self.own, self.d ^ k), "dp", k) for k in range(1, 4)]

    def take_dp(self, got):
        self.piece = total([at(self.own, self.d)] + got)
        self.own = self.piece.astype(bf16)

    def spread_chip(self):
        return [swap(self.own, "expert", 2 * k) for k in range(1, self.chips)]

    def join_chip(self, got):
        got = jnp.stack([self.own] + got)
        self.own = jnp.concatenate(
            [lax.dynamic_slice_in_dim(got, self.chip ^ k, 1, 0) for k in range(self.chips)]
        )

    def spread_core(self):
        return [swap(self.own, "expert", 1)]

    def join_core(self, got):
        own, other = self.own, got[0]
        x = jnp.stack(
            [jnp.where(self.core == 0, own, other), jnp.where(self.core == 0, other, own)]
        )
        return x.reshape(-1, 128)


def shards(
    tokens,
    cotangent,
    expert_ids,
    priority,
    step,
    attn_qkv,
    attn_out,
    router,
    norms,
    expert_in,
    expert_out,
    moments_qkv,
    moments_out,
    moments_router,
    moments_norms,
    moments_in,
    moments_exp,
):
    tok_dev = tokens.shape[0]
    groups = lax.axis_size("expert")
    n_dp = lax.axis_size("dp")
    assert expert_in.shape[0] == 1 and n_dp == 4 and tok_dev % SEQ == 0
    experts = groups
    per = experts // n_dp
    cap = (tok_dev + experts - 1) // experts
    pad = -(-(cap + 2) // 16) * 16
    n = tok_dev // SEQ
    devices = n_dp * groups
    me_dp = lax.axis_index("dp").astype(i32)
    me_e = lax.axis_index("expert").astype(i32)
    core = me_e % 2
    where = jnp.stack([me_dp, core, me_e])

    qkvT = attn_qkv.astype(bf16).T
    misc = jnp.concatenate(
        [
            router.astype(bf16).T,
            norms.astype(bf16).reshape(1, D),
            jnp.zeros((16 - per - 1, D), bf16),
        ],
        axis=0,
    )
    eighth = me_e % 8
    own = jnp.concatenate(
        [
            lax.dynamic_slice_in_dim(qkvT, eighth * 48, 48, 0),
            lax.dynamic_slice_in_dim(attn_out.astype(bf16), eighth * 16, 16, 0),
            misc,
        ],
        axis=0,
    )
    own_e = jnp.concatenate([expert_in[0].astype(bf16), expert_out[0].astype(bf16)], axis=0)
    ids = expert_ids.reshape(n, SEQ, 2).transpose(0, 2, 1)
    prio = priority.reshape(n, SEQ, 2).transpose(0, 2, 1)
    got = [own] + [swap(own, "dp", k) for k in (1, 2, 3)]
    got, own_e, ids, prio = fence(got, own_e, ids, prio)
    gathered = lax.all_gather(own_e, "dp", axis=0)
    got = jnp.stack(got)
    got, misc = got[:, :64], got[:, 64:]
    near = [swap(got, "expert", 2 * k) for k in (1, 2, 3)]
    pos, cols, up_slots = slots(where, ids, prio, cotangent, experts, cap, pad)
    near, pos, cols, up_slots = fence(near, pos, cols, up_slots)
    far = swap(jnp.stack([got] + near), "expert", 1)
    up = exchange(up_slots, "expert")
    wT, ow, rT, nm = assemble(where, got, misc, jnp.stack(near), far, experts)
    proj, ctxT, lse, mid, sec, gatesT = attend(tokens, wT, ow, rT, nm)

    blocks = spread(pos, sec, pad)
    near = [k for k in range(2, groups) if (k >> 1) & ((k >> 1) - 1) == 0]
    distant = [k for k in range(2, groups) if (k >> 1) & ((k >> 1) - 1)]
    gb, dr, kept = {}, {}, []

    def experts_on(ks, rows):
        g, d, keep = run_experts(where, tuple(ks), rows, up, gathered, rT, cap)
        kept.append(keep)
        for k, gk, dk in zip(ks, g, d):
            gb[k], dr[k] = gk, dk

    send = lambda ks: [swap(blocks[k], "expert", k) for k in ks]
    here, there = [blocks[0]] + send([1]), send(near)
    experts_on([0, 1], here)
    there, kept[0] = fence(there, kept[0])
    ends = [blocks[k] for k in distant]
    ends, there = fence(ends, there)
    last = [swap(b, "expert", k) for k, b in zip(distant, ends)]
    dr[1] = swap(dr[1], "expert", 1)
    experts_on(near, there)
    last, kept[1], dr[1] = fence(last, kept[1], dr[1])
    for k in near:
        dr[k] = swap(dr[k], "expert", k)
    experts_on(distant, last)
    for k in distant:
        dr[k] = swap(dr[k], "expert", k)
    partial = weight_grads(kept, pad)
    dr, gb, partial = fence([dr[k] for k in range(groups)], [gb[k] for k in range(groups)], partial)
    owned = exchange(partial, "dp")
    dmid, dn_two, drT = combine(where, dr, cols, gatesT, sec, mid, cotangent, rT, nm, cap)

    back = functools.partial(attend_back, groups=groups, proj=proj, ctxT=ctxT, lse=lse, ow=ow, nm=nm)
    dmid, gb = fence(dmid, gb)
    split = 1 + 5 * groups // 8
    early = [gb[0]] + [swap(gb[k], "expert", k) for k in range(1, split)]
    late = gb[split:]
    dp0, packed0 = back(0, tok=tokens, dmid=dmid)
    early, late, dmid, dp0, packed0 = fence(early, late, dmid, dp0, packed0)
    sum0, sum1 = Sums(me_dp, me_e, groups), Sums(me_dp, me_e, groups)
    sum0.take_core(sum0.send_core(packed0))
    sum0.own, dmid = fence(sum0.own, dmid)
    late = [swap(b, "expert", k) for k, b in enumerate(late, split)]
    got = sum0.send_chip()
    dp1, packed1 = back(1, tok=tokens, dmid=dmid)
    got, late, dp1, packed1, owned, dmid = fence(got, late, dp1, packed1, owned, dmid)
    sum0.take_chip(got)
    got0, got1 = sum0.send_dp(), sum1.send_core(packed1)
    grad_input, dn_one = enter(tokens, dmid, dp0, dp1, wT, nm)
    got0, got1, grad_input, dn_one, mid = fence(got0, got1, grad_input, dn_one, mid)
    sum0.take_dp(got0)
    sum1.take_core(got1)
    got0, got1 = sum0.spread_chip(), sum1.send_chip()

    dn = jnp.concatenate([dn_one, dn_two], axis=0)
    small = jnp.stack(
        [
            jnp.concatenate(
                [drT[d * per : (d + 1) * per, j * 128 : (j + 1) * 128] for j in range(4)]
                + [dn[:, d * 128 : (d + 1) * 128]],
                axis=0,
            )
            for d in range(n_dp)
        ]
    )
    lines = small.shape[1]
    small = jnp.broadcast_to(small[:, None], (n_dp, groups, lines, 128))
    small = exchange(small.reshape(devices, lines, 128), ("dp", "expert"))
    activations = finish(early + late, cols, mid)
    got0, got1, small, activations = fence(got0, got1, small, activations)
    sum0.join_chip(got0)
    sum1.take_chip(got1)
    got0, got1 = sum0.spread_core(), sum1.send_dp()
    owned = total([owned[d] for d in range(n_dp)])
    small = small.sum(0)
    term = jnp.sum(sum0.piece * sum0.piece) + jnp.sum(owned * owned)
    term = term + jnp.sum(small * small) / groups
    got0, got1, term, owned, small = fence(got0, got1, term, owned, small)
    part0 = sum0.join_core(got0)
    sum1.take_dp(got1)
    term = term + jnp.sum(sum1.piece * sum1.piece)
    terms = exchange(jnp.full((devices, 1, 128), term, f32), ("dp", "expert"))
    sum1.join_chip(sum1.spread_chip())
    part1 = sum1.join_core(sum1.spread_core())
    share_router = jnp.concatenate(
        [small[j * per : (j + 1) * per] for j in range(4)], axis=1
    ).T
    share_norms = small[4 * per :]
    grad_norm = jnp.sqrt(jnp.sum(terms[:, 0, 0]))
    factor = MAX_NORM / grad_norm
    rates = step_rates(experts)
    step_float = step.astype(f32)
    fixes = (1.0 - jnp.power(BETA_ONE, step_float), 1.0 - jnp.power(BETA_TWO, step_float))
    new = adam(
        (rates[0], rates[1], rates[4], rates[5]),
        where,
        jnp.stack([factor, *fixes]),
        part0,
        part1,
        owned,
        (attn_qkv, attn_out, expert_in, expert_out),
        (moments_qkv, moments_out, moments_in, moments_exp),
    )
    new_router = adam_update(
        router, moments_router, share_router, factor, rates[2], DECAY_RATE, fixes
    )
    new_norms = adam_update(norms, moments_norms, share_norms, factor, rates[3], 0.0, fixes)
    return (
        activations,
        grad_input,
        grad_norm,
        *new[:8],
        *new_router,
        *new_norms,
        *new[8:],
    )


def solution(mesh):
    tok = P(("dp", "expert"), None)
    cols = P(None, "dp")
    rows = P("dp", None)
    e_in = P("expert", None, "dp")
    e_out = P("expert", "dp", None)
    in_specs = (
        tok,
        tok,
        tok,
        tok,
        P(),
        cols,
        rows,
        cols,
        cols,
        e_in,
        e_out,
        P(None, None, "dp"),
        P(None, "dp", None),
        P(None, None, "dp"),
        P(None, None, "dp"),
        P(None, "expert", None, "dp"),
        P(None, "expert", "dp", None),
    )
    out_specs = (
        (tok, tok, P())
        + (cols,) * 4
        + (rows,) * 4
        + (cols,) * 4
        + (cols,) * 4
        + (e_in,) * 4
        + (e_out,) * 4
    )
    return jax.shard_map(shards, mesh=mesh, in_specs=in_specs, out_specs=out_specs, check_vma=False)
```

```python
import functools

import jax
import jax.numpy as jnp
from jax import lax
from jax.experimental import pallas as pl
from jax.experimental.pallas import tpu as pltpu
from jax.sharding import PartitionSpec as P

D = 512
HEADS = 8
HEAD = 64
FF = 2048
SEQ = 720

EPS_NORM = 1e-06
BETA_ONE = 0.9
BETA_TWO = 0.999
ADAM_EPS = 1e-08
DECAY_RATE = 0.1
MAX_NORM = 1.0

f32, bf16, i32 = jnp.float32, jnp.bfloat16, jnp.int32
NN = (((1,), (0,)), ((), ()))
NT = (((1,), (1,)), ((), ()))
TN = (((0,), (0,)), ((), ()))
LOG2E = 1.4426950408889634
SCALE = HEAD**-0.5
FAR = 1 << 20
VMEM_LIMIT = 60 * 2**20


def mm(a, b, dims=NN):
    return lax.dot_general(a, b, dims, preferred_element_type=f32)


def full(a):
    return pl.BlockSpec(a.shape, lambda *i: (0,) * a.ndim)


def whole(*shape):
    return pl.BlockSpec(shape, lambda *i: (0,) * len(shape))


def per_image(cols):
    return pl.BlockSpec((SEQ, cols), lambda i: (i, 0))


def per_image_t(rows):
    return pl.BlockSpec((1, rows, SEQ), lambda i: (i, 0, 0))


def sds(shape, dtype):
    return jax.ShapeDtypeStruct(shape, dtype)


SMEM = pl.BlockSpec(memory_space=pltpu.SMEM)
ANY = pl.BlockSpec(memory_space=pl.ANY)


def call(body, name, us=0.1, **kw):
    return pl.pallas_call(
        body,
        name=name,
        compiler_params=pltpu.CompilerParams(vmem_limit_bytes=VMEM_LIMIT),
        cost_estimate=pl.CostEstimate(flops=int(us * 10**9), bytes_accessed=10**5, transcendentals=0),
        **kw,
    )


def normalize(v):
    c = v - jnp.mean(v, axis=-1, keepdims=True)
    r = lax.rsqrt(jnp.mean(c * c, axis=-1, keepdims=True) + EPS_NORM)
    return c * r, r


def assemble_kernel(experts, where, got, misc, near, far, wT, ow, rT, nm):
    me, slot = where[0], where[2] % 8
    per = experts // 4
    for c in range(4):
        for b in range(2):
            s = slot ^ (2 * c + b)
            for k in range(4):
                d = me ^ k
                if b == 0:
                    piece = got[k] if c == 0 else near[c - 1, k]
                else:
                    piece = far[c, k]
                lo = pl.multiple_of(d * 384 + s * 48, 16)
                wT[pl.ds(lo, 48), :] = piece[:48, :]
                lo = pl.multiple_of(d * 128 + s * 16, 16)
                ow[pl.ds(lo, 16), :] = piece[48:64, :]
    for d in range(4):
        for k in range(4):

            @pl.when((me ^ k) == d)
            def _(d=d, k=k):
                rest = misc[k].astype(f32)
                rT[d * per : (d + 1) * per, :] = rest[:per, :]
                for j in range(4):
                    nm[j : j + 1, d * 128 : (d + 1) * 128] = rest[
                        per : per + 1, j * 128 : (j + 1) * 128
                    ]


def assemble(where, got, misc, near, far, experts):
    args = (got, misc, near, far)
    return call(
        functools.partial(assemble_kernel, experts),
        "assemble",
        in_specs=[SMEM] + [whole(*a.shape) for a in args],
        out_specs=[whole(3 * D, D), whole(D, D), whole(experts, D), whole(4, D)],
        out_shape=[
            sds((3 * D, D), bf16),
            sds((D, D), bf16),
            sds((experts, D), f32),
            sds((4, D), f32),
        ],
    )(where, *args)


def route_kernel(cap, pad, where, ids, prio, pos, cols):
    me = where[2]
    n = ids.shape[0]
    experts = pos.shape[1]
    nh = -(-(2 * n * SEQ) // 2048) * 16

    hi_io = lax.broadcasted_iota(i32, (nh, SEQ), 0)
    lo_io = lax.broadcasted_iota(i32, (128, SEQ), 0)

    def hot(i, k):
        q = prio[i, k : k + 1, :]
        return hi_io == (q >> 7), lo_io == (q & 127)

    table = jnp.zeros((nh, 128), f32)
    for i in range(n):
        for k in range(2):
            a, b = hot(i, k)
            ex = ((ids[i, k : k + 1, :] ^ me) + 1).astype(f32)
            table += mm(
                jnp.where(a, 1.0, 0.0).astype(bf16), jnp.where(b, ex, 0.0).astype(bf16), NT
            )
    upper = (
        lax.broadcasted_iota(i32, (128, 128), 0) < lax.broadcasted_iota(i32, (128, 128), 1)
    ).astype(bf16)
    lower = (
        lax.broadcasted_iota(i32, (nh, nh), 1) < lax.broadcasted_iota(i32, (nh, nh), 0)
    ).astype(bf16)
    ones = jnp.ones((128, 128), bf16)
    rank = jnp.zeros((nh, 128), f32)
    for e in range(experts):
        m = (table == float(e + 1)).astype(f32)
        mb = m.astype(bf16)
        rank += m * (mm(mb, upper) + mm(mm(lower, mb).astype(bf16), ones))
    ri = jnp.minimum(rank.astype(i32), 16383)
    rlo = (ri & 127).astype(bf16)
    rhi = (ri >> 7).astype(bf16)
    eio = lax.broadcasted_iota(i32, (experts, SEQ), 0)
    for i in range(n):
        out = jnp.full((experts, SEQ), FAR, i32)
        flat = []
        for k in range(2):
            a, b = hot(i, k)
            bb = jnp.where(b, 1.0, 0.0).astype(bf16)
            x = mm(rlo, bb) + 128.0 * mm(rhi, bb)
            r = jnp.sum(jnp.where(a, x, 0.0), axis=0, keepdims=True).astype(i32)
            ex = ids[i, k : k + 1, :] ^ me
            keep = r < cap
            out = jnp.where((eio == ex) & keep, r, out)
            flat.append(jnp.where(keep, ex * pad + r, FAR))
        pos[i] = out
        fl = jnp.concatenate(flat + [jnp.zeros((6, SEQ), i32)], axis=0).astype(f32)
        cols[i * SEQ : (i + 1) * SEQ, :] = fl.T.astype(i32)


def route(where, ids, prio, experts, cap, pad):
    n = ids.shape[0]
    t = n * SEQ
    return call(
        functools.partial(route_kernel, cap, pad),
        "route",
        in_specs=[SMEM, whole(*ids.shape), whole(*prio.shape)],
        out_specs=[whole(n, experts, SEQ), whole(t, 8)],
        out_shape=[sds((n, experts, SEQ), i32), sds((t, 8), i32)],
    )(where, ids, prio)


def spread_kernel(pad, together, where, pos, x, *outs):
    step = pl.program_id(0)
    io = lax.broadcasted_iota(i32, (pad, SEQ), 0)
    acc = None
    for i in range(pos.shape[0]):
        hit = [
            jnp.where(io == pos[i, pl.ds(2 * step + o, 1), :], 1.0, 0.0).astype(bf16)
            for o in range(2)
        ]
        part = mm(jnp.concatenate(hit, axis=0), x[i * SEQ : (i + 1) * SEQ, :])
        acc = part if acc is None else acc + part
    block = acc.astype(bf16)
    for o in range(2):
        half = block[o * pad : (o + 1) * pad, :]
        if together:
            outs[0][pl.ds((2 * step + o) ^ where[2], 1)] = half[None]
            continue
        for j in range(o, len(outs), 2):

            @pl.when(2 * step + o == j)
            def _(j=j, half=half):
                outs[j][...] = half


def spread(where, pos, x, pad, together):
    experts = pos.shape[1]
    if together:
        out_specs, out_shape = whole(experts, pad, D), sds((experts, pad, D), bf16)
    else:
        out_specs, out_shape = [whole(pad, D)] * experts, [sds((pad, D), bf16)] * experts
    return call(
        functools.partial(spread_kernel, pad, together),
        "spread",
        grid=(experts // 2,),
        in_specs=[SMEM, full(pos), full(x)],
        out_specs=out_specs,
        out_shape=out_shape,
    )(where, pos, x)


def head_masks():
    lane = lax.broadcasted_iota(i32, (1, 128), 1)
    return (lane < 64).astype(bf16), (lane >= 64).astype(bf16)


def attend_kernel(tok, wT, ow, rT, nm, proj, ctxT, lse, mid, sec, gatesT, vT, ct):
    x = tok[...].astype(f32)
    xh, _ = normalize(x)
    fb = (xh * nm[0:1, :] + nm[1:2, :]).astype(bf16)
    proj[...] = mm(fb, wT[...], NT).astype(bf16)
    vT[...] = proj[:, 2 * D :].T
    masks = head_masks()
    for h in range(HEADS):
        p = h // 2
        qm = proj[:, p * 128 : (p + 1) * 128] * masks[h % 2]
        kk = proj[:, D + p * 128 : D + (p + 1) * 128]
        s = mm(kk, qm, NT)
        m = jnp.max(s, axis=0, keepdims=True)
        e = jnp.exp2((s - m) * (SCALE * LOG2E))
        total = jnp.sum(e, axis=0, keepdims=True)
        c = mm(vT[h * 64 : (h + 1) * 64, :], e.astype(bf16))
        ct[h * 64 : (h + 1) * 64, :] = (c * (1.0 / total)).astype(bf16)
        lse[0, h : h + 1, :] = m * (SCALE * LOG2E) + jnp.log2(total)
    ctxT[0] = ct[...]
    middle = x + mm(ct[...], ow[...], TN)
    mid[...] = middle
    xh2, _ = normalize(middle)
    s2 = (xh2 * nm[2:3, :] + nm[3:4, :]).astype(bf16)
    sec[...] = s2
    logits = mm(rT[...].astype(bf16), s2, NT)
    ex = jnp.exp(logits - jnp.max(logits, axis=0, keepdims=True))
    gatesT[0] = ex / jnp.sum(ex, axis=0, keepdims=True)


def attend(tok, wT, ow, rT, nm):
    t = tok.shape[0]
    n = t // SEQ
    experts = rT.shape[0]
    return call(
        attend_kernel,
        "attend",
        grid=(n,),
        in_specs=[per_image(D), full(wT), full(ow), full(rT), full(nm)],
        out_specs=[
            per_image(3 * D),
            per_image_t(D),
            per_image_t(HEADS),
            per_image(D),
            per_image(D),
            per_image_t(experts),
        ],
        out_shape=[
            sds((t, 3 * D), bf16),
            sds((n, D, SEQ), bf16),
            sds((n, HEADS, SEQ), f32),
            sds((t, D), f32),
            sds((t, D), bf16),
            sds((n, experts, SEQ), f32),
        ],
        scratch_shapes=[pltpu.VMEM((D, SEQ), bf16), pltpu.VMEM((D, SEQ), bf16)],
    )(tok, wT, ow, rT, nm)


def normal_cdf(h):
    return 0.5 + 0.5 * lax.erf(h * 0.7071067811865476), jnp.exp2((-0.5 * LOG2E) * h * h)


def experts_kernel(cap, nb, first, sources, where, *refs):
    rows, (u0, u1), gw, rT = refs[:nb], refs[nb : nb + 2], refs[nb + 2 : nb + 10], refs[nb + 10]
    refs = refs[nb + 11 :] if first else refs[nb + 12 :]
    dr = refs[:nb]
    gated, xs, db, act, dh, gb, sems = refs[nb:]
    s = pl.program_id(0)
    pad = rows[0].shape[0]
    me = where[2]
    iw, xw = gw[:4], gw[4:]
    chunks, cols = len(iw), iw[0].shape[1]
    for i in range(nb // 2):

        @pl.when(s == i)
        def _(i=i):
            xs[:pad, :] = rows[2 * i][...]
            xs[pad:, :] = rows[2 * i + 1][...]

    x = xs[...]
    upf = jnp.concatenate([u0[0], u1[0]], axis=0).astype(f32)
    logits = mm(x, rT[...].astype(bf16), NT)
    ex = jnp.exp(logits - jnp.max(logits, axis=1, keepdims=True))
    mine = lax.broadcasted_iota(i32, ex.shape, 1) == me
    gate = jnp.sum(jnp.where(mine, ex, 0.0), axis=1, keepdims=True) / jnp.sum(
        ex, axis=1, keepdims=True
    )
    d = (gate * upf).astype(bf16)
    db[...] = d
    back = None
    drow = None
    for j in range(chunks):
        h = mm(x, iw[j][...])
        cdf, g = normal_cdf(h)
        a = (h * cdf).astype(bf16)
        act[:, j * cols : (j + 1) * cols] = a
        part = mm(a, xw[j][...])
        back = part if back is None else back + part
        dact = mm(d, xw[j][...], NT)
        dj = (dact * (cdf + h * g * 0.3989422804014327)).astype(bf16)
        dh[:, j * cols : (j + 1) * cols] = dj
        part = mm(dj, iw[j][...], NT)
        drow = part if drow is None else drow + part
    b = back.astype(bf16).astype(f32)
    gb[...] = (gate * b).astype(bf16)
    moves = [
        pltpu.make_async_copy(
            gb.at[pl.ds(o * pad, pad)], gated.at[sources[2 * s + o]], sems.at[o]
        )
        for o in range(2)
    ]
    for move in moves:
        move.start()
    prod = upf * b
    first = prod.astype(bf16)
    rest = (prod - first.astype(f32)).astype(bf16)
    ones = jnp.ones((8, D), bf16)
    dgs = (mm(ones, first, NT) + mm(ones, rest, NT))[0:1, :]
    line = lax.broadcasted_iota(i32, (pad, D), 0)
    for o in range(2):
        dg = dgs[:, o * pad : (o + 1) * pad]
        dg = jnp.concatenate([dg, jnp.zeros((1, D - pad), f32)], axis=1)
        top = dg.astype(bf16).astype(f32)
        part = drow[o * pad : (o + 1) * pad, :]
        part = jnp.where(line == cap, top, jnp.where(line == cap + 1, dg - top, part))
        part = part.astype(bf16)
        for i in range(nb // 2):

            @pl.when(s == i)
            def _(i=i, o=o, part=part):
                dr[2 * i + o][...] = part

    for move in moves:
        move.wait()


def run_experts(where, ks, rows, u, gw, rT, cap, gated):
    nb = len(ks)
    pad = rows[0].shape[0]
    hidden = len(gw) // 2 * gw[0].shape[1]
    pair = lambda c: pl.BlockSpec((2 * pad, c), lambda i, src: (i, 0))
    source = lambda o: pl.BlockSpec((1, pad, D), lambda i, src: (src[2 * i + o], 0, 0))
    blk = sds((pad, D), bf16)
    prior = [] if gated is None else [gated]
    out = call(
        functools.partial(experts_kernel, cap, nb, gated is None),
        "experts",
        us=8 * nb,
        grid_spec=pltpu.PrefetchScalarGridSpec(
            num_scalar_prefetch=1,
            grid=(nb // 2,),
            in_specs=[SMEM]
            + [whole(pad, D)] * nb
            + [source(0), source(1)]
            + [full(w) for w in gw]
            + [full(rT)]
            + [ANY] * len(prior),
            out_specs=[whole(pad, D)] * nb + [ANY, pair(D), pair(D), pair(FF), pair(FF)],
            scratch_shapes=[pltpu.VMEM((2 * pad, D), bf16), pltpu.SemaphoreType.DMA((2,))],
        ),
        out_shape=[blk] * nb
        + [sds(u.shape, bf16)]
        + [sds((nb * pad, D), bf16)] * 2
        + [sds((nb * pad, hidden), bf16)] * 2,
        input_output_aliases={nb + 13: nb} if prior else {},
    )(where[2] ^ jnp.asarray(ks, i32), where, *rows, u, u, *gw, rT, *prior)
    return out[:nb], out[nb], out[nb + 1 :]


def weights_kernel(groups, *refs):
    xs, dbs, acts, dhs = (refs[i * groups : (i + 1) * groups] for i in range(4))
    *outs, xT, dT = refs[4 * groups :]
    step = pl.program_id(0)

    @pl.when(step == 0)
    def _():
        lo = 0
        for x, db in zip(xs, dbs):
            n = x.shape[0]
            xT[:, lo : lo + n] = x[...].T
            dT[:, lo : lo + n] = db[...].T
            lo += n

    di = None
    de = None
    lo = 0
    for act, dh in zip(acts, dhs):
        n = act.shape[0]
        part = mm(xT[:, lo : lo + n], dh[...])
        di = part if di is None else di + part
        part = mm(dT[:, lo : lo + n], act[...])
        de = part if de is None else de + part
        lo += n
    di = di.astype(bf16)
    de = de.astype(bf16)
    for j, out in enumerate(outs):

        @pl.when(step == j)
        def _(out=out):
            out[:D, :] = di
            out[D:, :] = de


def weight_grads(kept):
    groups = len(kept)
    ins = [k[i] for i in range(4) for k in kept]
    rows = sum(k[0].shape[0] for k in kept)
    col = lambda a: pl.BlockSpec((a.shape[0], D), lambda j: (0, j))
    return call(
        functools.partial(weights_kernel, groups),
        "weight_grads",
        grid=(FF // D,),
        in_specs=[full(a) for a in ins[: 2 * groups]] + [col(a) for a in ins[2 * groups :]],
        out_specs=[whole(2 * D, D)] * (FF // D),
        out_shape=[sds((2 * D, D), bf16)] * (FF // D),
        scratch_shapes=[pltpu.VMEM((D, rows), bf16)] * 2,
    )(*ins)


def pick(cols, count):
    io = lax.broadcasted_iota(i32, (SEQ, count), 1)
    return jnp.where((io == cols[:, 0:1]) | (io == cols[:, 1:2]), 1.0, 0.0).astype(bf16)


def stack_once(blocks, scratch):
    pad = blocks[0].shape[0]

    @pl.when(pl.program_id(0) == 0)
    def _():
        for j, block in enumerate(blocks):
            scratch[j * pad : (j + 1) * pad, :] = block[...]


def combine_kernel(cap, experts, where, *refs):
    cols, gatesT, sec, mid, cot, rT, nm, dmid, dn, drT, dr, dgs = refs[experts:]
    stack_once(refs[:experts], dr)
    i = pl.program_id(0)
    me = where[2]
    pad = dr.shape[0] // experts
    hits = pick(cols[...], dr.shape[0])
    ds = mm(hits, dr[...])
    base = cap // 16 * 16
    off = cap - base
    for e in range(experts):
        two = dr[e * pad + base : (e + 1) * pad, :pad]
        x = mm(two, hits[:, e * pad : (e + 1) * pad], NT)
        dgs[pl.ds(e ^ me, 1), :] = x[off : off + 1, :] + x[off + 1 : off + 2, :]
    dg = dgs[...]
    g = gatesT[0]
    dl = (g * (dg - jnp.sum(g * dg, axis=0, keepdims=True))).astype(bf16)
    ds = ds + mm(dl, rT[...].astype(bf16), TN)
    xh, r = normalize(mid[...])
    y = ds * nm[2:3, :]
    dmid[...] = cot[...].astype(f32) + r * (
        y - jnp.mean(y, axis=-1, keepdims=True) - xh * jnp.mean(y * xh, axis=-1, keepdims=True)
    )
    gg = jnp.sum(ds * xh, axis=0, keepdims=True)
    gs = jnp.sum(ds, axis=0, keepdims=True)
    dR = mm(dl, sec[...])

    @pl.when(i == 0)
    def _():
        dn[0:1, :] = gg
        dn[1:2, :] = gs
        drT[...] = dR

    @pl.when(i > 0)
    def _():
        dn[0:1, :] += gg
        dn[1:2, :] += gs
        drT[...] += dR


def combine(where, blocks, cols, gatesT, sec, mid, cot, rT, nm, cap):
    experts = len(blocks)
    pad = blocks[0].shape[0]
    t = cols.shape[0]
    return call(
        functools.partial(combine_kernel, cap, experts),
        "combine",
        grid=(t // SEQ,),
        in_specs=[SMEM]
        + [whole(pad, D)] * experts
        + [
            per_image(8),
            per_image_t(experts),
            per_image(D),
            per_image(D),
            per_image(D),
            full(rT),
            full(nm),
        ],
        out_specs=[per_image(D), whole(2, D), whole(experts, D)],
        out_shape=[sds((t, D), f32), sds((2, D), f32), sds((experts, D), f32)],
        scratch_shapes=[pltpu.VMEM((experts * pad, D), bf16), pltpu.VMEM((experts, SEQ), f32)],
    )(where, *blocks, cols, gatesT, sec, mid, cot, rT, nm)


def finish_kernel(where, back, cols, mid, out, gb):
    experts, pad, _ = back.shape

    @pl.when(pl.program_id(0) == 0)
    def _():
        for j in range(experts):
            gb[j * pad : (j + 1) * pad, :] = back[where[2] ^ j]

    out[...] = (mid[...] + mm(pick(cols[...], gb.shape[0]), gb[...])).astype(bf16)


def finish(where, back, cols, mid):
    experts, pad, _ = back.shape
    t = cols.shape[0]
    return call(
        finish_kernel,
        "finish",
        grid=(t // SEQ,),
        in_specs=[SMEM, full(back), per_image(8), per_image(D)],
        out_specs=per_image(D),
        out_shape=sds((t, D), bf16),
        scratch_shapes=[pltpu.VMEM((experts * pad, D), bf16)],
    )(where, back, cols, mid)


TILES = (
    (((0, 0), (0, 1)), ((0, 4), (0, 5)), ((0, 8), (1, 2)), ((0, 9), (1, 3))),
    (((0, 2), (1, 0)), ((0, 3), (1, 1)), ((0, 6), (0, 7)), ((0, 10), (0, 11))),
)


def attend_back_kernel(part, tok, dmid, proj, ctxT, lse, ow, nm, dproj, packed, kT, dqT, gq, go):
    i = pl.program_id(0)
    half = D // 2
    base = part * half
    da = dmid[...].astype(bf16)
    owp = ow[base : base + half, :]
    do = mm(da, owp, NT).astype(bf16)
    doT = mm(owp, da, NT).astype(bf16)
    prod = doT.astype(f32) * ctxT[0, base : base + half, :].astype(f32)
    kT[...] = proj[:, D + base : D + base + half].T
    masks = head_masks()
    low = lax.broadcasted_iota(i32, (SEQ, 128), 1) < 64
    for p in range(HEADS // 4):
        dv = []
        dk = []
        lo = base + p * 128
        qq = proj[:, lo : lo + 128]
        kk = proj[:, D + lo : D + lo + 128]
        vv = proj[:, 2 * D + lo : 2 * D + lo + 128]
        dd = do[:, p * 128 : (p + 1) * 128]
        for j in range(2):
            hl = 2 * p + j
            h = part * (HEADS // 2) + hl
            s = mm(kk, qq * masks[j], NT)
            prob = jnp.exp2(s * (SCALE * LOG2E) - lse[0, h : h + 1, :])
            dprob = mm(vv, dd * masks[j], NT)
            dv.append(mm(prob.astype(bf16), dd))
            inner = jnp.sum(prod[hl * 64 : (hl + 1) * 64, :], axis=0, keepdims=True)
            ds = (prob * (dprob - inner)).astype(bf16)
            dk.append(mm(ds, qq))
            dqT[hl * 64 : (hl + 1) * 64, :] = (
                mm(kT[hl * 64 : (hl + 1) * 64, :], ds) * SCALE
            ).astype(bf16)
        at = p * 128
        dproj[:, 2 * half + at : 2 * half + at + 128] = jnp.where(low, dv[0], dv[1]).astype(bf16)
        dproj[:, half + at : half + at + 128] = (jnp.where(low, dk[0], dk[1]) * SCALE).astype(bf16)
    dproj[:, :half] = dqT[...].T
    xh, _ = normalize(tok[...].astype(f32))
    fb = (xh * nm[0:1, :] + nm[1:2, :]).astype(bf16)
    dq = mm(fb, dproj[...], TN)
    other = (1 - part) * half
    do_ = mm(ctxT[0, other : other + half, :], da)

    @pl.when(i == 0)
    def _():
        gq[...] = dq
        go[...] = do_

    @pl.when(i > 0)
    def _():
        gq[...] += dq
        go[...] += do_

    @pl.when(i == pl.num_programs(0) - 1)
    def _():
        groups, _, r, _ = packed.shape
        for d in range(4):
            for t in range(2):
                kind, c = TILES[part][d][t]
                if kind == 0:
                    third, at = c // 4, c % 4 - 2 * part
                    tile = gq[:, third * half + at * 128 : third * half + (at + 1) * 128]
                else:
                    row = (c - (2 - 2 * part)) * 128
                    tile = jnp.concatenate(
                        [go[row : row + 128, j * 128 : (j + 1) * 128] for j in range(4)], axis=0
                    )
                tile = tile.astype(bf16)
                for m in range(512 // r):
                    packed[t * (512 // r) + m, d] = tile[m * r : (m + 1) * r, :]


def attend_back(part, groups, tok, dmid, proj, ctxT, lse, ow, nm):
    t = tok.shape[0]
    r = 1024 // groups
    return call(
        functools.partial(attend_back_kernel, part),
        "attend_back",
        grid=(t // SEQ,),
        in_specs=[
            per_image(D),
            per_image(D),
            per_image(3 * D),
            per_image_t(D),
            per_image_t(HEADS),
            full(ow),
            full(nm),
        ],
        out_specs=[per_image(3 * D // 2), whole(groups, 4, r, 128)],
        out_shape=[sds((t, 3 * D // 2), bf16), sds((groups, 4, r, 128), bf16)],
        scratch_shapes=[
            pltpu.VMEM((D // 2, SEQ), bf16),
            pltpu.VMEM((D // 2, SEQ), bf16),
            pltpu.VMEM((D, 3 * D // 2), f32),
            pltpu.VMEM((D // 2, D), f32),
        ],
    )(tok, dmid, proj, ctxT, lse, ow, nm)


def enter_kernel(tok, dmid, dp0, dp1, wT, nm, gin, dn):
    i = pl.program_id(0)
    half = D // 2
    df = None
    for part, dp in enumerate((dp0, dp1)):
        for third in range(3):
            lo = third * D + part * half
            term = mm(dp[:, third * half : (third + 1) * half], wT[lo : lo + half, :])
            df = term if df is None else df + term
    xh, r = normalize(tok[...].astype(f32))
    y = df * nm[0:1, :]
    gin[...] = dmid[...] + r * (
        y - jnp.mean(y, axis=-1, keepdims=True) - xh * jnp.mean(y * xh, axis=-1, keepdims=True)
    )
    gg = jnp.sum(df * xh, axis=0, keepdims=True)
    gs = jnp.sum(df, axis=0, keepdims=True)

    @pl.when(i == 0)
    def _():
        dn[0:1, :] = gg
        dn[1:2, :] = gs

    @pl.when(i > 0)
    def _():
        dn[0:1, :] += gg
        dn[1:2, :] += gs


def enter(tok, dmid, dp0, dp1, wT, nm):
    t = tok.shape[0]
    return call(
        enter_kernel,
        "enter",
        grid=(t // SEQ,),
        in_specs=[
            per_image(D),
            per_image(D),
            per_image(3 * D // 2),
            per_image(3 * D // 2),
            full(wT),
            full(nm),
        ],
        out_specs=[per_image(D), whole(2, D)],
        out_shape=[sds((t, D), f32), sds((2, D), f32)],
    )(tok, dmid, dp0, dp1, wT, nm)


def step_rates(experts):
    return (
        D ** (-0.5),
        2.0 ** (-0.5),
        (2 * D) ** (-0.5),
        0.1,
        D ** (-0.5),
        2.0 * experts / (1.2 * FF**0.5),
    )


def adam_update(weight, moments, grad, factor, rate, decay, fixes):
    clipped = grad * factor
    first = BETA_ONE * moments[0] + (1.0 - BETA_ONE) * clipped
    second = BETA_TWO * moments[1] + (1.0 - BETA_TWO) * clipped * clipped
    updated = weight - rate * (
        first / fixes[0] / (jnp.sqrt(second / fixes[1]) + ADAM_EPS) + decay * weight
    )
    return (updated, first, second, updated.astype(bf16))


def adam_kernel(rates, where, nums, *refs):
    own, other, owned = refs[:3]
    weights, moments, outs = refs[3:7], refs[7:11], refs[11:27]
    gq, go, pieces = refs[27:]
    groups, _, r, _ = pieces.shape
    i = pl.program_id(0)

    @pl.when(i == 0)
    def _():
        chip = where[2] // 2
        for g in range(groups):

            @pl.when(where[1] == g % 2)
            def _(g=g):
                pieces[g] = own[chip ^ (g // 2)]

            @pl.when(where[1] != g % 2)
            def _(g=g):
                pieces[g] = other[chip ^ (g // 2)]

        for d in range(4):

            @pl.when(where[0] == d)
            def _(d=d):
                for part in range(2):
                    for t in range(2):
                        kind, c = TILES[part][d][t]
                        for m in range(512 // r):
                            tile = pieces[t * (512 // r) + m, part]
                            if kind == 0:
                                at = (c - 3 * d) * 128
                                gq[m * r : (m + 1) * r, at : at + 128] = tile
                            else:
                                j, row = m * r // 128, m * r % 128
                                go[row : row + r, j * 128 : (j + 1) * 128] = tile

    rows_q, rows_o = weights[0].shape[0], weights[1].shape[0]
    rows_e = weights[2].shape[1]
    grads = (
        gq[pl.ds(i * rows_q, rows_q), :].astype(f32),
        go[pl.ds(i * rows_o, rows_o), :].astype(f32),
        owned[pl.ds(i * rows_e, rows_e), :],
        owned[D:, pl.ds(pl.multiple_of(i * rows_e, 128), rows_e)].T,
    )
    factor = nums[0]
    fixes = (nums[1], nums[2])
    for j in range(4):
        lead = j >= 2
        w = weights[j][0] if lead else weights[j][...]
        m = (moments[j][0, 0], moments[j][1, 0]) if lead else (moments[j][0], moments[j][1])
        new = adam_update(w, m, grads[j], factor, rates[j], DECAY_RATE, fixes)
        for o in range(4):
            if lead:
                outs[4 * j + o][0] = new[o]
            else:
                outs[4 * j + o][...] = new[o]


def adam(rates, where, nums, own, other, owned, weights, moments):
    steps = 4
    specs = []
    mspecs = []
    for w in weights:
        if w.ndim == 2:
            specs.append(pl.BlockSpec((w.shape[0] // steps, w.shape[1]), lambda i: (i, 0)))
            mspecs.append(pl.BlockSpec((2, w.shape[0] // steps, w.shape[1]), lambda i: (0, i, 0)))
        else:
            specs.append(
                pl.BlockSpec((1, w.shape[1] // steps, w.shape[2]), lambda i: (0, i, 0))
            )
            mspecs.append(
                pl.BlockSpec((2, 1, w.shape[1] // steps, w.shape[2]), lambda i: (0, 0, i, 0))
            )
    return call(
        functools.partial(adam_kernel, rates),
        "adam",
        grid=(steps,),
        in_specs=[SMEM, SMEM, full(own), full(other), full(owned)] + specs + mspecs,
        out_specs=[sp for sp in specs for _ in range(4)],
        out_shape=[sds(w.shape, dt) for w in weights for dt in (f32, f32, f32, bf16)],
        scratch_shapes=[
            pltpu.VMEM((D, 384), bf16),
            pltpu.VMEM((128, D), bf16),
            pltpu.VMEM((2 * own.shape[0], *own.shape[1:]), bf16),
        ],
    )(where, nums, own, other, owned, *weights, *moments)


def swap(x, axis, k):
    n = lax.axis_size(axis)
    return lax.ppermute(x, axis, [(i, i ^ k) for i in range(n)])


def exchange(x, axis):
    return lax.all_to_all(x, axis, split_axis=0, concat_axis=0, tiled=True)


def add_up(blocks):
    return functools.reduce(lambda a, b: a + b, [b.astype(f32) for b in blocks])


def to_owners(x, axis, me):
    part = lambda k: lax.dynamic_index_in_dim(x, me ^ k, 0, keepdims=False)
    return [part(0)] + [swap(part(k), axis, k) for k in range(1, x.shape[0])]


def fence(*groups):
    flat, tree = jax.tree.flatten(groups)
    return jax.tree.unflatten(tree, lax.optimization_barrier(tuple(flat)))


def shards(
    tokens,
    cotangent,
    expert_ids,
    priority,
    step,
    attn_qkv,
    attn_out,
    router,
    norms,
    expert_in,
    expert_out,
    moments_qkv,
    moments_out,
    moments_router,
    moments_norms,
    moments_in,
    moments_exp,
):
    tok_dev = tokens.shape[0]
    groups = lax.axis_size("expert")
    n_dp = lax.axis_size("dp")
    assert expert_in.shape[0] == 1 and n_dp == 4 and tok_dev % SEQ == 0
    experts = groups
    per = experts // n_dp
    cap = (tok_dev + experts - 1) // experts
    pad = -(-(cap + 2) // 128) * 128
    n = tok_dev // SEQ
    devices = n_dp * groups
    me_dp = lax.axis_index("dp").astype(i32)
    me_e = lax.axis_index("expert").astype(i32)
    core = me_e % 2
    where = jnp.stack([me_dp, core, me_e])

    qkvT = attn_qkv.astype(bf16).T
    misc = jnp.concatenate(
        [
            router.astype(bf16).T,
            norms.astype(bf16).reshape(1, D),
            jnp.zeros((16 - per - 1, D), bf16),
        ],
        axis=0,
    )
    eighth = me_e % 8
    own = jnp.concatenate(
        [
            lax.dynamic_slice_in_dim(qkvT, eighth * 48, 48, 0),
            lax.dynamic_slice_in_dim(attn_out.astype(bf16), eighth * 16, 16, 0),
            misc,
        ],
        axis=0,
    )
    got = [own] + [swap(own, "dp", k) for k in (1, 2, 3)]
    ids = expert_ids.reshape(n, SEQ, 2).transpose(0, 2, 1)
    prio = priority.reshape(n, SEQ, 2).transpose(0, 2, 1)
    pos, cols = route(where, ids, prio, experts, cap, pad)
    own_in, own_out = expert_in[0].astype(bf16), expert_out[0].astype(bf16)
    in_w = [own_in, None, swap(own_in, "dp", 2), None]
    got, pos, cols = fence(got, pos, cols)
    got = jnp.stack(got)
    got, misc = got[:, :64], got[:, 64:]
    near = [swap(got, "expert", 2 * k) for k in (1, 2, 3)]
    up_slots = spread(where, pos, cotangent, pad, True)
    near, up_slots, in_w[2], own_in = fence(near, up_slots, in_w[2], own_in)
    in_w[1], in_w[3] = swap(own_in, "dp", 1), swap(own_in, "dp", 3)
    out_w = [own_out] + [swap(own_out, "dp", k) for k in (1, 2, 3)]
    far = swap(jnp.stack([got] + near), "expert", 1)
    up = exchange(up_slots, "expert")
    wT, ow, rT, nm = assemble(where, got, misc, jnp.stack(near), far, experts)
    proj, ctxT, lse, mid, sec, gatesT = attend(tokens, wT, ow, rT, nm)

    blocks = spread(where, pos, sec, pad, False)
    near = [k for k in range(2, groups) if (k >> 1) & ((k >> 1) - 1) == 0]
    distant = [k for k in range(2, groups) if (k >> 1) & ((k >> 1) - 1)]
    in_w, out_w, blocks = fence(in_w, out_w, blocks)
    gated, dr, kept = None, {}, []

    def experts_on(ks, rows):
        d, gated_now, keep = run_experts(
            where, tuple(ks), rows, up, in_w + out_w, rT, cap, gated
        )
        kept.append(keep)
        dr.update(zip(ks, d))
        return gated_now

    send = lambda ks: [swap(blocks[k], "expert", k) for k in ks]
    here, there = [blocks[0]] + send([1]), send(near)
    gated = experts_on([0, 1], here)
    there, kept[0] = fence(there, kept[0])
    ends = [blocks[k] for k in distant]
    ends, there = fence(ends, there)
    last = [swap(b, "expert", k) for k, b in zip(distant, ends)]
    dr[1] = swap(dr[1], "expert", 1)
    gated = experts_on(near, there)
    last, kept[1], dr[1] = fence(last, kept[1], dr[1])
    for k in near:
        dr[k] = swap(dr[k], "expert", k)
    gated = experts_on(distant, last)
    for k in distant:
        dr[k] = swap(dr[k], "expert", k)
    chunks = weight_grads(kept)
    dr, chunks, gated = fence([dr[k] for k in range(groups)], chunks, gated)
    owned = [chunks[0]] + [swap(chunks[k], "dp", k) for k in (1, 2, 3)]
    gated = exchange(gated, "expert")
    dmid, dn_two, drT = combine(where, dr, cols, gatesT, sec, mid, cotangent, rT, nm, cap)

    back = functools.partial(attend_back, groups=groups, proj=proj, ctxT=ctxT, lse=lse, ow=ow, nm=nm)
    dp0, packed0 = back(0, tok=tokens, dmid=dmid)
    gated, dmid, dp0, packed0 = fence(gated, dmid, dp0, packed0)
    got0 = exchange(packed0, "expert")
    dp1, packed1 = back(1, tok=tokens, dmid=dmid)
    got0, dp1, packed1, owned, dmid = fence(got0, dp1, packed1, owned, dmid)

    got0 = to_owners(add_up(got0).astype(bf16), "dp", me_dp)
    got1 = exchange(packed1, "expert")
    grad_input, dn_one = enter(tokens, dmid, dp0, dp1, wT, nm)
    got0, got1, grad_input, dn_one, mid = fence(got0, got1, grad_input, dn_one, mid)
    got1 = to_owners(add_up(got1).astype(bf16), "dp", me_dp)

    dn = jnp.concatenate([dn_one, dn_two], axis=0)
    small = jnp.stack(
        [
            jnp.concatenate(
                [drT[d * per : (d + 1) * per, j * 128 : (j + 1) * 128] for j in range(4)]
                + [dn[:, d * 128 : (d + 1) * 128]],
                axis=0,
            )
            for d in range(n_dp)
        ]
    )
    lines = small.shape[1]
    small = jnp.broadcast_to(small[:, None], (n_dp, groups, lines, 128))
    small = exchange(small.reshape(devices, lines, 128), ("dp", "expert"))
    activations = finish(where, gated, cols, mid)
    piece0 = add_up(got0)
    owned = add_up(owned)
    term = jnp.sum(piece0 * piece0) + jnp.sum(owned * owned)
    got1, small, activations, piece0, owned, term = fence(
        got1, small, activations, piece0, owned, term
    )
    piece1 = add_up(got1)
    small = small.sum(0)
    term = term + jnp.sum(piece1 * piece1) + jnp.sum(small * small) / groups
    terms = exchange(jnp.full((devices, 1, 128), term, f32), ("dp", "expert"))
    pieces = jnp.stack([piece0, piece1]).astype(bf16)
    mine = jnp.stack([pieces] + [swap(pieces, "expert", 2 * k) for k in range(1, groups // 2)])
    other = swap(mine, "expert", 1)
    share_router = jnp.concatenate(
        [small[j * per : (j + 1) * per] for j in range(4)], axis=1
    ).T
    share_norms = small[4 * per :]
    grad_norm = jnp.sqrt(jnp.sum(terms[:, 0, 0]))
    factor = MAX_NORM / grad_norm
    rates = step_rates(experts)
    step_float = step.astype(f32)
    fixes = (1.0 - jnp.power(BETA_ONE, step_float), 1.0 - jnp.power(BETA_TWO, step_float))
    new = adam(
        (rates[0], rates[1], rates[4], rates[5]),
        where,
        jnp.stack([factor, *fixes]),
        mine,
        other,
        owned,
        (attn_qkv, attn_out, expert_in, expert_out),
        (moments_qkv, moments_out, moments_in, moments_exp),
    )
    new_router = adam_update(
        router, moments_router, share_router, factor, rates[2], DECAY_RATE, fixes
    )
    new_norms = adam_update(norms, moments_norms, share_norms, factor, rates[3], 0.0, fixes)
    return (
        activations,
        grad_input,
        grad_norm,
        *new[:8],
        *new_router,
        *new_norms,
        *new[8:],
    )


def solution(mesh):
    tok = P(("dp", "expert"), None)
    cols = P(None, "dp")
    rows = P("dp", None)
    e_in = P("expert", None, "dp")
    e_out = P("expert", "dp", None)
    in_specs = (
        tok,
        tok,
        tok,
        tok,
        P(),
        cols,
        rows,
        cols,
        cols,
        e_in,
        e_out,
        P(None, None, "dp"),
        P(None, "dp", None),
        P(None, None, "dp"),
        P(None, None, "dp"),
        P(None, "expert", None, "dp"),
        P(None, "expert", "dp", None),
    )
    out_specs = (
        (tok, tok, P())
        + (cols,) * 4
        + (rows,) * 4
        + (cols,) * 4
        + (cols,) * 4
        + (e_in,) * 4
        + (e_out,) * 4
    )
    return jax.shard_map(shards, mesh=mesh, in_specs=in_specs, out_specs=out_specs, check_vma=False)
```

```python
import functools

import jax
import jax.numpy as jnp
from jax import lax
from jax.experimental import pallas as pl
from jax.experimental.pallas import tpu as pltpu
from jax.sharding import PartitionSpec as P

D = 512
HEADS = 8
HEAD = 64
FF = 2048
SEQ = 720

EPS_NORM = 1e-06
BETA_ONE = 0.9
BETA_TWO = 0.999
ADAM_EPS = 1e-08
DECAY_RATE = 0.1
MAX_NORM = 1.0

f32, bf16, i32 = jnp.float32, jnp.bfloat16, jnp.int32
NN = (((1,), (0,)), ((), ()))
NT = (((1,), (1,)), ((), ()))
TN = (((0,), (0,)), ((), ()))
LOG2E = 1.4426950408889634
SCALE = HEAD**-0.5
FAR = 1 << 20
VMEM_LIMIT = 60 * 2**20


def mm(a, b, dims=NN):
    return lax.dot_general(a, b, dims, preferred_element_type=f32)


def full(a):
    return pl.BlockSpec(a.shape, lambda *i: (0,) * a.ndim)


def whole(*shape):
    return pl.BlockSpec(shape, lambda *i: (0,) * len(shape))


def per_image(cols):
    return pl.BlockSpec((SEQ, cols), lambda i: (i, 0))


def per_image_t(rows):
    return pl.BlockSpec((1, rows, SEQ), lambda i: (i, 0, 0))


def sds(shape, dtype):
    return jax.ShapeDtypeStruct(shape, dtype)


SMEM = pl.BlockSpec(memory_space=pltpu.SMEM)
ANY = pl.BlockSpec(memory_space=pl.ANY)


def call(body, name, us=0.1, **kw):
    return pl.pallas_call(
        body,
        name=name,
        compiler_params=pltpu.CompilerParams(vmem_limit_bytes=VMEM_LIMIT),
        cost_estimate=pl.CostEstimate(flops=int(us * 10**9), bytes_accessed=10**5, transcendentals=0),
        **kw,
    )


def normalize(v):
    c = v - jnp.mean(v, axis=-1, keepdims=True)
    r = lax.rsqrt(jnp.mean(c * c, axis=-1, keepdims=True) + EPS_NORM)
    return c * r, r


def assemble_kernel(experts, where, got, n1, n2, n3, far, wT, ow, rT, nm):
    me, slot = where[0], where[2] % 8
    per = experts // 4
    for c in range(4):
        for b in range(2):
            s = slot ^ (2 * c + b)
            for k in range(4):
                d = me ^ k
                if b == 0:
                    piece = got[k] if c == 0 else (n1, n2, n3)[c - 1][k]
                else:
                    piece = far[c, k]
                lo = pl.multiple_of(d * 384 + s * 48, 16)
                wT[pl.ds(lo, 48), :] = piece[:48, :]
                lo = pl.multiple_of(d * 128 + s * 16, 16)
                ow[pl.ds(lo, 16), :] = piece[48:64, :]
    for d in range(4):
        for k in range(4):

            @pl.when((me ^ k) == d)
            def _(d=d, k=k):
                rest = got[k, 64:, :].astype(f32)
                rT[d * per : (d + 1) * per, :] = rest[:per, :]
                for j in range(4):
                    nm[j : j + 1, d * 128 : (d + 1) * 128] = rest[
                        per : per + 1, j * 128 : (j + 1) * 128
                    ]


def assemble(where, got, near, far, experts):
    args = (got, *near, far)
    return call(
        functools.partial(assemble_kernel, experts),
        "assemble",
        in_specs=[SMEM] + [whole(*a.shape) for a in args],
        out_specs=[whole(3 * D, D), whole(D, D), whole(experts, D), whole(4, D)],
        out_shape=[
            sds((3 * D, D), bf16),
            sds((D, D), bf16),
            sds((experts, D), f32),
            sds((4, D), f32),
        ],
    )(where, *args)


def route_kernel(cap, pad, where, ids, prio, pos, cols):
    me = where[2]
    n = ids.shape[0]
    experts = pos.shape[1]
    nh = -(-(2 * n * SEQ) // 2048) * 16

    hi_io = lax.broadcasted_iota(i32, (nh, SEQ), 0)
    lo_io = lax.broadcasted_iota(i32, (128, SEQ), 0)

    def hot(i, k):
        q = prio[i, k : k + 1, :]
        return hi_io == (q >> 7), lo_io == (q & 127)

    table = jnp.zeros((nh, 128), f32)
    for i in range(n):
        for k in range(2):
            a, b = hot(i, k)
            ex = ((ids[i, k : k + 1, :] ^ me) + 1).astype(f32)
            table += mm(
                jnp.where(a, 1.0, 0.0).astype(bf16), jnp.where(b, ex, 0.0).astype(bf16), NT
            )
    upper = (
        lax.broadcasted_iota(i32, (128, 128), 0) < lax.broadcasted_iota(i32, (128, 128), 1)
    ).astype(bf16)
    lower = (
        lax.broadcasted_iota(i32, (nh, nh), 1) < lax.broadcasted_iota(i32, (nh, nh), 0)
    ).astype(bf16)
    ones = jnp.ones((128, 128), bf16)
    rank = jnp.zeros((nh, 128), f32)
    for e in range(experts):
        m = (table == float(e + 1)).astype(f32)
        mb = m.astype(bf16)
        rank += m * (mm(mb, upper) + mm(mm(lower, mb).astype(bf16), ones))
    ri = jnp.minimum(rank.astype(i32), 16383)
    rlo = (ri & 127).astype(bf16)
    rhi = (ri >> 7).astype(bf16)
    eio = lax.broadcasted_iota(i32, (experts, SEQ), 0)
    for i in range(n):
        out = jnp.full((experts, SEQ), FAR, i32)
        flat = []
        for k in range(2):
            a, b = hot(i, k)
            bb = jnp.where(b, 1.0, 0.0).astype(bf16)
            x = mm(rlo, bb) + 128.0 * mm(rhi, bb)
            r = jnp.sum(jnp.where(a, x, 0.0), axis=0, keepdims=True).astype(i32)
            ex = ids[i, k : k + 1, :] ^ me
            keep = r < cap
            out = jnp.where((eio == ex) & keep, r, out)
            flat.append(jnp.where(keep, ex * pad + r, FAR))
        pos[i] = out
        fl = jnp.concatenate(flat + [jnp.zeros((6, SEQ), i32)], axis=0).astype(f32)
        cols[i * SEQ : (i + 1) * SEQ, :] = fl.T.astype(i32)


def route(where, ids, prio, experts, cap, pad):
    n = ids.shape[0]
    t = n * SEQ
    return call(
        functools.partial(route_kernel, cap, pad),
        "route",
        in_specs=[SMEM, whole(*ids.shape), whole(*prio.shape)],
        out_specs=[whole(n, experts, SEQ), whole(t, 8)],
        out_shape=[sds((n, experts, SEQ), i32), sds((t, 8), i32)],
    )(where, ids, prio)


def spread_kernel(pad, together, where, pos, x, *outs):
    step = pl.program_id(0)
    io = lax.broadcasted_iota(i32, (pad, SEQ), 0)
    acc = None
    for i in range(pos.shape[0]):
        hit = [
            jnp.where(io == pos[i, pl.ds(2 * step + o, 1), :], 1.0, 0.0).astype(bf16)
            for o in range(2)
        ]
        part = mm(jnp.concatenate(hit, axis=0), x[i * SEQ : (i + 1) * SEQ, :])
        acc = part if acc is None else acc + part
    block = acc.astype(bf16)
    for o in range(2):
        half = block[o * pad : (o + 1) * pad, :]
        if together:
            outs[0][pl.ds((2 * step + o) ^ where[2], 1)] = half[None]
            continue
        for j in range(o, len(outs), 2):

            @pl.when(2 * step + o == j)
            def _(j=j, half=half):
                outs[j][...] = half


def spread(where, pos, x, pad, together):
    experts = pos.shape[1]
    if together:
        out_specs, out_shape = whole(experts, pad, D), sds((experts, pad, D), bf16)
    else:
        out_specs, out_shape = [whole(pad, D)] * experts, [sds((pad, D), bf16)] * experts
    return call(
        functools.partial(spread_kernel, pad, together),
        "spread",
        grid=(experts // 2,),
        in_specs=[SMEM, full(pos), full(x)],
        out_specs=out_specs,
        out_shape=out_shape,
    )(where, pos, x)


def head_masks():
    lane = lax.broadcasted_iota(i32, (1, 128), 1)
    return (lane < 64).astype(bf16), (lane >= 64).astype(bf16)


def attend_kernel(tok, wT, ow, rT, nm, proj, ctxT, lse, mid, sec, gatesT, vT, ct):
    x = tok[...].astype(f32)
    xh, _ = normalize(x)
    fb = (xh * nm[0:1, :] + nm[1:2, :]).astype(bf16)
    proj[...] = mm(fb, wT[...], NT).astype(bf16)
    vT[...] = proj[:, 2 * D :].T
    masks = head_masks()
    for h in range(HEADS):
        p = h // 2
        qm = proj[:, p * 128 : (p + 1) * 128] * masks[h % 2]
        kk = proj[:, D + p * 128 : D + (p + 1) * 128]
        s = mm(kk, qm, NT)
        m = jnp.max(s, axis=0, keepdims=True)
        e = jnp.exp2((s - m) * (SCALE * LOG2E))
        total = jnp.sum(e, axis=0, keepdims=True)
        c = mm(vT[h * 64 : (h + 1) * 64, :], e.astype(bf16))
        ct[h * 64 : (h + 1) * 64, :] = (c * (1.0 / total)).astype(bf16)
        lse[0, h : h + 1, :] = m * (SCALE * LOG2E) + jnp.log2(total)
    ctxT[0] = ct[...]
    middle = x + mm(ct[...], ow[...], TN)
    mid[...] = middle
    xh2, _ = normalize(middle)
    s2 = (xh2 * nm[2:3, :] + nm[3:4, :]).astype(bf16)
    sec[...] = s2
    logits = mm(rT[...].astype(bf16), s2, NT)
    ex = jnp.exp(logits - jnp.max(logits, axis=0, keepdims=True))
    gatesT[0] = ex / jnp.sum(ex, axis=0, keepdims=True)


def attend(tok, wT, ow, rT, nm):
    t = tok.shape[0]
    n = t // SEQ
    experts = rT.shape[0]
    return call(
        attend_kernel,
        "attend",
        grid=(n,),
        in_specs=[per_image(D), full(wT), full(ow), full(rT), full(nm)],
        out_specs=[
            per_image(3 * D),
            per_image_t(D),
            per_image_t(HEADS),
            per_image(D),
            per_image(D),
            per_image_t(experts),
        ],
        out_shape=[
            sds((t, 3 * D), bf16),
            sds((n, D, SEQ), bf16),
            sds((n, HEADS, SEQ), f32),
            sds((t, D), f32),
            sds((t, D), bf16),
            sds((n, experts, SEQ), f32),
        ],
        scratch_shapes=[pltpu.VMEM((D, SEQ), bf16), pltpu.VMEM((D, SEQ), bf16)],
    )(tok, wT, ow, rT, nm)


def normal_cdf(h):
    return 0.5 + 0.5 * lax.erf(h * 0.7071067811865476), jnp.exp2((-0.5 * LOG2E) * h * h)


def experts_kernel(cap, nb, first, sources, where, *refs):
    rows, (u0, u1), gw, rT = refs[:nb], refs[nb : nb + 2], refs[nb + 2 : nb + 8], refs[nb + 8]
    refs = refs[nb + 9 :] if first else refs[nb + 10 :]
    dr = refs[:nb]
    gated, xs, db, act, dh, gb, sems = refs[nb:]
    s = pl.program_id(0)
    pad = rows[0].shape[0]
    me = where[2]
    iw = [gw[0], gw[4].at[:D], gw[1], gw[5].at[:D]]
    xw = [gw[2], gw[4].at[D:], gw[3], gw[5].at[D:]]
    chunks, cols = len(iw), iw[0].shape[1]
    for i in range(nb // 2):

        @pl.when(s == i)
        def _(i=i):
            xs[:pad, :] = rows[2 * i][...]
            xs[pad:, :] = rows[2 * i + 1][...]

    x = xs[...]
    upf = jnp.concatenate([u0[0], u1[0]], axis=0).astype(f32)
    logits = mm(x, rT[...].astype(bf16), NT)
    ex = jnp.exp(logits - jnp.max(logits, axis=1, keepdims=True))
    mine = lax.broadcasted_iota(i32, ex.shape, 1) == me
    gate = jnp.sum(jnp.where(mine, ex, 0.0), axis=1, keepdims=True) / jnp.sum(
        ex, axis=1, keepdims=True
    )
    d = (gate * upf).astype(bf16)
    db[...] = d
    back = None
    drow = None
    for j in range(chunks):
        h = mm(x, iw[j][...])
        cdf, g = normal_cdf(h)
        a = (h * cdf).astype(bf16)
        act[:, j * cols : (j + 1) * cols] = a
        part = mm(a, xw[j][...])
        back = part if back is None else back + part
        dact = mm(d, xw[j][...], NT)
        dj = (dact * (cdf + h * g * 0.3989422804014327)).astype(bf16)
        dh[:, j * cols : (j + 1) * cols] = dj
        part = mm(dj, iw[j][...], NT)
        drow = part if drow is None else drow + part
    b = back.astype(bf16).astype(f32)
    gb[...] = (gate * b).astype(bf16)
    moves = [
        pltpu.make_async_copy(
            gb.at[pl.ds(o * pad, pad)], gated.at[sources[2 * s + o]], sems.at[o]
        )
        for o in range(2)
    ]
    for move in moves:
        move.start()
    prod = upf * b
    first = prod.astype(bf16)
    rest = (prod - first.astype(f32)).astype(bf16)
    ones = jnp.ones((8, D), bf16)
    dgs = (mm(ones, first, NT) + mm(ones, rest, NT))[0:1, :]
    line = lax.broadcasted_iota(i32, (pad, D), 0)
    for o in range(2):
        dg = dgs[:, o * pad : (o + 1) * pad]
        dg = jnp.concatenate([dg, jnp.zeros((1, D - pad), f32)], axis=1)
        top = dg.astype(bf16).astype(f32)
        part = drow[o * pad : (o + 1) * pad, :]
        part = jnp.where(line == cap, top, jnp.where(line == cap + 1, dg - top, part))
        part = part.astype(bf16)
        for i in range(nb // 2):

            @pl.when(s == i)
            def _(i=i, o=o, part=part):
                dr[2 * i + o][...] = part

    for move in moves:
        move.wait()


def run_experts(where, ks, rows, u, gw, rT, cap, gated):
    nb = len(ks)
    pad = rows[0].shape[0]
    hidden = 4 * gw[0].shape[1]
    pair = lambda c: pl.BlockSpec((2 * pad, c), lambda i, src: (i, 0))
    source = lambda o: pl.BlockSpec((1, pad, D), lambda i, src: (src[2 * i + o], 0, 0))
    blk = sds((pad, D), bf16)
    prior = [] if gated is None else [gated]
    out = call(
        functools.partial(experts_kernel, cap, nb, gated is None),
        "experts",
        us=8 * nb,
        grid_spec=pltpu.PrefetchScalarGridSpec(
            num_scalar_prefetch=1,
            grid=(nb // 2,),
            in_specs=[SMEM]
            + [whole(pad, D)] * nb
            + [source(0), source(1)]
            + [full(w) for w in gw]
            + [full(rT)]
            + [ANY] * len(prior),
            out_specs=[whole(pad, D)] * nb + [ANY, pair(D), pair(D), pair(FF), pair(FF)],
            scratch_shapes=[pltpu.VMEM((2 * pad, D), bf16), pltpu.SemaphoreType.DMA((2,))],
        ),
        out_shape=[blk] * nb
        + [sds(u.shape, bf16)]
        + [sds((nb * pad, D), bf16)] * 2
        + [sds((nb * pad, hidden), bf16)] * 2,
        input_output_aliases={nb + 11: nb} if prior else {},
    )(where[2] ^ jnp.asarray(ks, i32), where, *rows, u, u, *gw, rT, *prior)
    return out[:nb], out[nb], out[nb + 1 :]


def weights_kernel(groups, *refs):
    xs, dbs, acts, dhs = (refs[i * groups : (i + 1) * groups] for i in range(4))
    *outs, xT, dT = refs[4 * groups :]
    step = pl.program_id(0)

    @pl.when(step == 0)
    def _():
        lo = 0
        for x, db in zip(xs, dbs):
            n = x.shape[0]
            xT[:, lo : lo + n] = x[...].T
            dT[:, lo : lo + n] = db[...].T
            lo += n

    di = None
    de = None
    lo = 0
    for act, dh in zip(acts, dhs):
        n = act.shape[0]
        part = mm(xT[:, lo : lo + n], dh[...])
        di = part if di is None else di + part
        part = mm(dT[:, lo : lo + n], act[...])
        de = part if de is None else de + part
        lo += n
    di = di.astype(bf16)
    de = de.astype(bf16)
    for j, out in enumerate(outs):

        @pl.when(step == j)
        def _(out=out):
            out[:D, :] = di
            out[D:, :] = de


def weight_grads(kept):
    groups = len(kept)
    ins = [k[i] for i in range(4) for k in kept]
    rows = sum(k[0].shape[0] for k in kept)
    col = lambda a: pl.BlockSpec((a.shape[0], D), lambda j: (0, j))
    return call(
        functools.partial(weights_kernel, groups),
        "weight_grads",
        grid=(FF // D,),
        in_specs=[full(a) for a in ins[: 2 * groups]] + [col(a) for a in ins[2 * groups :]],
        out_specs=[whole(2 * D, D)] * (FF // D),
        out_shape=[sds((2 * D, D), bf16)] * (FF // D),
        scratch_shapes=[pltpu.VMEM((D, rows), bf16)] * 2,
    )(*ins)


def pick(cols, count):
    io = lax.broadcasted_iota(i32, (SEQ, count), 1)
    return jnp.where((io == cols[:, 0:1]) | (io == cols[:, 1:2]), 1.0, 0.0).astype(bf16)


def stack_once(blocks, scratch):
    pad = blocks[0].shape[0]

    @pl.when(pl.program_id(0) == 0)
    def _():
        for j, block in enumerate(blocks):
            scratch[j * pad : (j + 1) * pad, :] = block[...]


def combine_kernel(cap, experts, where, *refs):
    cols, gatesT, sec, mid, cot, rT, nm, dmid, dn, drT, dr, dgs = refs[experts:]
    stack_once(refs[:experts], dr)
    i = pl.program_id(0)
    me = where[2]
    pad = dr.shape[0] // experts
    hits = pick(cols[...], dr.shape[0])
    ds = mm(hits, dr[...])
    base = cap // 16 * 16
    off = cap - base
    for e in range(experts):
        two = dr[e * pad + base : (e + 1) * pad, :pad]
        x = mm(two, hits[:, e * pad : (e + 1) * pad], NT)
        dgs[pl.ds(e ^ me, 1), :] = x[off : off + 1, :] + x[off + 1 : off + 2, :]
    dg = dgs[...]
    g = gatesT[0]
    dl = (g * (dg - jnp.sum(g * dg, axis=0, keepdims=True))).astype(bf16)
    ds = ds + mm(dl, rT[...].astype(bf16), TN)
    xh, r = normalize(mid[...])
    y = ds * nm[2:3, :]
    dmid[...] = cot[...].astype(f32) + r * (
        y - jnp.mean(y, axis=-1, keepdims=True) - xh * jnp.mean(y * xh, axis=-1, keepdims=True)
    )
    gg = jnp.sum(ds * xh, axis=0, keepdims=True)
    gs = jnp.sum(ds, axis=0, keepdims=True)
    dR = mm(dl, sec[...])

    @pl.when(i == 0)
    def _():
        dn[0:1, :] = gg
        dn[1:2, :] = gs
        drT[...] = dR

    @pl.when(i > 0)
    def _():
        dn[0:1, :] += gg
        dn[1:2, :] += gs
        drT[...] += dR


def combine(where, blocks, cols, gatesT, sec, mid, cot, rT, nm, cap):
    experts = len(blocks)
    pad = blocks[0].shape[0]
    t = cols.shape[0]
    return call(
        functools.partial(combine_kernel, cap, experts),
        "combine",
        grid=(t // SEQ,),
        in_specs=[SMEM]
        + [whole(pad, D)] * experts
        + [
            per_image(8),
            per_image_t(experts),
            per_image(D),
            per_image(D),
            per_image(D),
            full(rT),
            full(nm),
        ],
        out_specs=[per_image(D), whole(2, D), whole(experts, D)],
        out_shape=[sds((t, D), f32), sds((2, D), f32), sds((experts, D), f32)],
        scratch_shapes=[pltpu.VMEM((experts * pad, D), bf16), pltpu.VMEM((experts, SEQ), f32)],
    )(where, *blocks, cols, gatesT, sec, mid, cot, rT, nm)


def finish_kernel(where, back, cols, mid, out, gb):
    experts, pad, _ = back.shape

    @pl.when(pl.program_id(0) == 0)
    def _():
        for j in range(experts):
            gb[j * pad : (j + 1) * pad, :] = back[where[2] ^ j]

    out[...] = (mid[...] + mm(pick(cols[...], gb.shape[0]), gb[...])).astype(bf16)


def finish(where, back, cols, mid):
    experts, pad, _ = back.shape
    t = cols.shape[0]
    return call(
        finish_kernel,
        "finish",
        grid=(t // SEQ,),
        in_specs=[SMEM, full(back), per_image(8), per_image(D)],
        out_specs=per_image(D),
        out_shape=sds((t, D), bf16),
        scratch_shapes=[pltpu.VMEM((experts * pad, D), bf16)],
    )(where, back, cols, mid)


TILES = (
    (((0, 0), (0, 1)), ((0, 4), (0, 5)), ((0, 8), (1, 2)), ((0, 9), (1, 3))),
    (((0, 2), (1, 0)), ((0, 3), (1, 1)), ((0, 6), (0, 7)), ((0, 10), (0, 11))),
)


def attend_back_kernel(part, tok, dmid, proj, ctxT, lse, ow, nm, dproj, packed, kT, dqT, gq, go):
    i = pl.program_id(0)
    half = D // 2
    base = part * half
    da = dmid[...].astype(bf16)
    owp = ow[base : base + half, :]
    do = mm(da, owp, NT).astype(bf16)
    doT = do.T
    prod = doT.astype(f32) * ctxT[0, base : base + half, :].astype(f32)
    kT[...] = proj[:, D + base : D + base + half].T
    masks = head_masks()
    low = lax.broadcasted_iota(i32, (SEQ, 128), 1) < 64
    for p in range(HEADS // 4):
        dv = []
        dk = []
        lo = base + p * 128
        qq = proj[:, lo : lo + 128]
        kk = proj[:, D + lo : D + lo + 128]
        vv = proj[:, 2 * D + lo : 2 * D + lo + 128]
        dd = do[:, p * 128 : (p + 1) * 128]
        for j in range(2):
            hl = 2 * p + j
            h = part * (HEADS // 2) + hl
            s = mm(kk, qq * masks[j], NT)
            prob = jnp.exp2(s * (SCALE * LOG2E) - lse[0, h : h + 1, :])
            dprob = mm(vv, dd * masks[j], NT)
            dv.append(mm(prob.astype(bf16), dd))
            inner = jnp.sum(prod[hl * 64 : (hl + 1) * 64, :], axis=0, keepdims=True)
            ds = (prob * (dprob - inner)).astype(bf16)
            dk.append(mm(ds, qq))
            dqT[hl * 64 : (hl + 1) * 64, :] = (
                mm(kT[hl * 64 : (hl + 1) * 64, :], ds) * SCALE
            ).astype(bf16)
        at = p * 128
        dproj[:, 2 * half + at : 2 * half + at + 128] = jnp.where(low, dv[0], dv[1]).astype(bf16)
        dproj[:, half + at : half + at + 128] = (jnp.where(low, dk[0], dk[1]) * SCALE).astype(bf16)
    dproj[:, :half] = dqT[...].T
    xh, _ = normalize(tok[...].astype(f32))
    fb = (xh * nm[0:1, :] + nm[1:2, :]).astype(bf16)
    dq = mm(fb, dproj[...], TN)
    other = (1 - part) * half
    do_ = mm(ctxT[0, other : other + half, :], da)

    @pl.when(i == 0)
    def _():
        gq[...] = dq
        go[...] = do_

    @pl.when(i > 0)
    def _():
        gq[...] += dq
        go[...] += do_

    @pl.when(i == pl.num_programs(0) - 1)
    def _():
        groups, _, r, _ = packed.shape
        for d in range(4):
            for t in range(2):
                kind, c = TILES[part][d][t]
                if kind == 0:
                    third, at = c // 4, c % 4 - 2 * part
                    tile = gq[:, third * half + at * 128 : third * half + (at + 1) * 128]
                else:
                    row = (c - (2 - 2 * part)) * 128
                    tile = jnp.concatenate(
                        [go[row : row + 128, j * 128 : (j + 1) * 128] for j in range(4)], axis=0
                    )
                tile = tile.astype(bf16)
                for m in range(512 // r):
                    packed[t * (512 // r) + m, d] = tile[m * r : (m + 1) * r, :]


def attend_back(part, groups, tok, dmid, proj, ctxT, lse, ow, nm):
    t = tok.shape[0]
    r = 1024 // groups
    return call(
        functools.partial(attend_back_kernel, part),
        "attend_back",
        grid=(t // SEQ,),
        in_specs=[
            per_image(D),
            per_image(D),
            per_image(3 * D),
            per_image_t(D),
            per_image_t(HEADS),
            full(ow),
            full(nm),
        ],
        out_specs=[per_image(3 * D // 2), whole(groups, 4, r, 128)],
        out_shape=[sds((t, 3 * D // 2), bf16), sds((groups, 4, r, 128), bf16)],
        scratch_shapes=[
            pltpu.VMEM((D // 2, SEQ), bf16),
            pltpu.VMEM((D // 2, SEQ), bf16),
            pltpu.VMEM((D, 3 * D // 2), f32),
            pltpu.VMEM((D // 2, D), f32),
        ],
    )(tok, dmid, proj, ctxT, lse, ow, nm)


def enter_kernel(tok, dmid, dp0, dp1, wT, nm, o0, o1, o2, o3, gin, dn, owned, squares):
    i = pl.program_id(0)
    own = (o0[...].astype(f32) + o1[...].astype(f32)) + (o2[...].astype(f32) + o3[...].astype(f32))
    owned[...] = own
    sq = jnp.sum(own * own, axis=0, keepdims=True)
    half = D // 2
    df = None
    for part, dp in enumerate((dp0, dp1)):
        for third in range(3):
            lo = third * D + part * half
            term = mm(dp[:, third * half : (third + 1) * half], wT[lo : lo + half, :])
            df = term if df is None else df + term
    xh, r = normalize(tok[...].astype(f32))
    y = df * nm[0:1, :]
    gin[...] = dmid[...] + r * (
        y - jnp.mean(y, axis=-1, keepdims=True) - xh * jnp.mean(y * xh, axis=-1, keepdims=True)
    )
    gg = jnp.sum(df * xh, axis=0, keepdims=True)
    gs = jnp.sum(df, axis=0, keepdims=True)

    @pl.when(i == 0)
    def _():
        dn[0:1, :] = gg
        dn[1:2, :] = gs
        squares[...] = sq

    @pl.when(i > 0)
    def _():
        dn[0:1, :] += gg
        dn[1:2, :] += gs
        squares[...] += sq


def enter(tok, dmid, dp0, dp1, wT, nm, chunks):
    t = tok.shape[0]
    part = pl.BlockSpec((2 * D * SEQ // t, D), lambda i: (i, 0))
    return call(
        enter_kernel,
        "enter",
        grid=(t // SEQ,),
        in_specs=[
            per_image(D),
            per_image(D),
            per_image(3 * D // 2),
            per_image(3 * D // 2),
            full(wT),
            full(nm),
        ]
        + [part] * 4,
        out_specs=[per_image(D), whole(2, D), part, whole(1, D)],
        out_shape=[sds((t, D), f32), sds((2, D), f32), sds((2 * D, D), f32), sds((1, D), f32)],
    )(tok, dmid, dp0, dp1, wT, nm, *chunks)


def step_rates(experts):
    return (
        D ** (-0.5),
        2.0 ** (-0.5),
        (2 * D) ** (-0.5),
        0.1,
        D ** (-0.5),
        2.0 * experts / (1.2 * FF**0.5),
    )


def adam_update(weight, moments, grad, factor, rate, decay, fixes):
    clipped = grad * factor
    first = BETA_ONE * moments[0] + (1.0 - BETA_ONE) * clipped
    second = BETA_TWO * moments[1] + (1.0 - BETA_TWO) * clipped * clipped
    updated = weight - rate * (
        first / fixes[0] / (jnp.sqrt(second / fixes[1]) + ADAM_EPS) + decay * weight
    )
    return (updated, first, second, updated.astype(bf16))


def adam_kernel(rates, where, nums, *refs):
    own, other, owned_in, owned_out = refs[:4]
    weights, moments, outs = refs[4:8], refs[8:12], refs[12:28]
    gq, go, pieces = refs[28:]
    groups, _, r, _ = pieces.shape
    i = pl.program_id(0)

    @pl.when(i == 0)
    def _():
        chip = where[2] // 2
        for g in range(groups):

            @pl.when(where[1] == g % 2)
            def _(g=g):
                pieces[g] = own[chip ^ (g // 2)]

            @pl.when(where[1] != g % 2)
            def _(g=g):
                pieces[g] = other[chip ^ (g // 2)]

        for d in range(4):

            @pl.when(where[0] == d)
            def _(d=d):
                for part in range(2):
                    for t in range(2):
                        kind, c = TILES[part][d][t]
                        for m in range(512 // r):
                            tile = pieces[t * (512 // r) + m, part]
                            if kind == 0:
                                at = (c - 3 * d) * 128
                                gq[m * r : (m + 1) * r, at : at + 128] = tile
                            else:
                                j, row = m * r // 128, m * r % 128
                                go[row : row + r, j * 128 : (j + 1) * 128] = tile

    rows_q, rows_o = weights[0].shape[0], weights[1].shape[0]
    grads = (
        gq[pl.ds(i * rows_q, rows_q), :].astype(f32),
        go[pl.ds(i * rows_o, rows_o), :].astype(f32),
        owned_in[...],
        owned_out[...].T,
    )
    factor = nums[0]
    fixes = (nums[1], nums[2])
    for j in range(4):
        lead = j >= 2
        w = weights[j][0] if lead else weights[j][...]
        m = (moments[j][0, 0], moments[j][1, 0]) if lead else (moments[j][0], moments[j][1])
        new = adam_update(w, m, grads[j], factor, rates[j], DECAY_RATE, fixes)
        for o in range(4):
            if lead:
                outs[4 * j + o][0] = new[o]
            else:
                outs[4 * j + o][...] = new[o]


def adam(rates, where, nums, own, other, owned, weights, moments):
    steps = 4
    specs = []
    mspecs = []
    for w in weights:
        if w.ndim == 2:
            specs.append(pl.BlockSpec((w.shape[0] // steps, w.shape[1]), lambda i: (i, 0)))
            mspecs.append(pl.BlockSpec((2, w.shape[0] // steps, w.shape[1]), lambda i: (0, i, 0)))
        else:
            specs.append(
                pl.BlockSpec((1, w.shape[1] // steps, w.shape[2]), lambda i: (0, i, 0))
            )
            mspecs.append(
                pl.BlockSpec((2, 1, w.shape[1] // steps, w.shape[2]), lambda i: (0, 0, i, 0))
            )
    return call(
        functools.partial(adam_kernel, rates),
        "adam",
        grid=(steps,),
        in_specs=[SMEM, SMEM, full(own), full(other)]
        + [
            pl.BlockSpec((D // steps, D), lambda i: (i, 0)),
            pl.BlockSpec((D, D // steps), lambda i: (1, i)),
        ] + specs + mspecs,
        out_specs=[sp for sp in specs for _ in range(4)],
        out_shape=[sds(w.shape, dt) for w in weights for dt in (f32, f32, f32, bf16)],
        scratch_shapes=[
            pltpu.VMEM((D, 384), bf16),
            pltpu.VMEM((128, D), bf16),
            pltpu.VMEM((2 * own.shape[0], *own.shape[1:]), bf16),
        ],
    )(where, nums, own, other, owned, owned, *weights, *moments)


def settle_kernel(groups, small, squares, *refs):
    got, (pieces, rest, terms) = refs[:4], refs[4:]
    piece = got[0][...].astype(f32)
    for g in got[1:]:
        piece = piece + g[...].astype(f32)
    pieces[...] = piece.astype(bf16)
    own = jnp.sum(small[...], axis=0)
    rest[...] = own
    r = piece.shape[1]
    flat = piece[0] * piece[0] + piece[1] * piece[1]
    term = (
        jnp.sum(flat, axis=(0, 1), keepdims=True)
        + jnp.sum(squares[...], axis=(0, 1), keepdims=True)
        + jnp.sum(own * own, axis=(0, 1), keepdims=True) / groups
    )
    terms[...] = jnp.broadcast_to(term[None], terms.shape)


def settle(groups, small, squares, got):
    args = (small, squares, *got)
    devices, lines, _ = small.shape
    return call(
        functools.partial(settle_kernel, groups),
        "settle",
        in_specs=[whole(*a.shape) for a in args],
        out_specs=[whole(*got[0].shape), whole(lines, 128), whole(devices, 1, 128)],
        out_shape=[sds(got[0].shape, bf16), sds((lines, 128), f32), sds((devices, 1, 128), f32)],
    )(*args)


def swap(x, axis, k):
    n = lax.axis_size(axis)
    return lax.ppermute(x, axis, [(i, i ^ k) for i in range(n)])


def exchange(x, axis):
    return lax.all_to_all(x, axis, split_axis=0, concat_axis=0, tiled=True)


def add_up(blocks):
    return functools.reduce(lambda a, b: a + b, [b.astype(f32) for b in blocks])


def to_owners(x, axis, me):
    part = lambda k: lax.dynamic_index_in_dim(x, me ^ k, 0, keepdims=False)
    return [part(0)] + [swap(part(k), axis, k) for k in range(1, x.shape[0])]


def fence(*groups):
    flat, tree = jax.tree.flatten(groups)
    return jax.tree.unflatten(tree, lax.optimization_barrier(tuple(flat)))


def shards(
    tokens,
    cotangent,
    expert_ids,
    priority,
    step,
    attn_qkv,
    attn_out,
    router,
    norms,
    expert_in,
    expert_out,
    moments_qkv,
    moments_out,
    moments_router,
    moments_norms,
    moments_in,
    moments_exp,
):
    tok_dev = tokens.shape[0]
    groups = lax.axis_size("expert")
    n_dp = lax.axis_size("dp")
    assert expert_in.shape[0] == 1 and n_dp == 4 and tok_dev % SEQ == 0
    experts = groups
    per = experts // n_dp
    cap = (tok_dev + experts - 1) // experts
    pad = -(-(cap + 2) // 128) * 128
    n = tok_dev // SEQ
    devices = n_dp * groups
    me_dp = lax.axis_index("dp").astype(i32)
    me_e = lax.axis_index("expert").astype(i32)
    core = me_e % 2
    where = jnp.stack([me_dp, core, me_e])

    qkvT = attn_qkv.astype(bf16).T
    misc = jnp.concatenate(
        [
            router.astype(bf16).T,
            norms.astype(bf16).reshape(1, D),
            jnp.zeros((16 - per - 1, D), bf16),
        ],
        axis=0,
    )
    eighth = me_e % 8
    own = jnp.concatenate(
        [
            lax.dynamic_slice_in_dim(qkvT, eighth * 48, 48, 0),
            lax.dynamic_slice_in_dim(attn_out.astype(bf16), eighth * 16, 16, 0),
            misc,
        ],
        axis=0,
    )
    got = [own] + [swap(own, "dp", k) for k in (1, 2, 3)]
    ids = expert_ids.reshape(n, SEQ, 2).transpose(0, 2, 1)
    prio = priority.reshape(n, SEQ, 2).transpose(0, 2, 1)
    pos, cols = route(where, ids, prio, experts, cap, pad)
    own_in, own_out = expert_in[0].astype(bf16), expert_out[0].astype(bf16)
    in_w = [own_in, None, swap(own_in, "dp", 2), None]
    got, pos, cols = fence(got, pos, cols)
    got = jnp.stack(got)
    mine = got[:, :64]
    near = [swap(mine, "expert", 2 * k) for k in (1, 2, 3)]
    up_slots = spread(where, pos, cotangent, pad, True)
    near, up_slots, in_w[2], own_in = fence(near, up_slots, in_w[2], own_in)
    own_e = jnp.concatenate([own_in, own_out], axis=0)
    others = [swap(own_e, "dp", k) for k in (1, 3)]
    out_w = [own_out, None, swap(own_out, "dp", 2), None]
    far = swap(jnp.stack([mine] + near), "expert", 1)
    up = exchange(up_slots, "expert")
    wT, ow, rT, nm = assemble(where, got, near, far, experts)
    proj, ctxT, lse, mid, sec, gatesT = attend(tokens, wT, ow, rT, nm)

    blocks = spread(where, pos, sec, pad, False)
    near = [k for k in range(2, groups) if (k >> 1) & ((k >> 1) - 1) == 0]
    distant = [k for k in range(2, groups) if (k >> 1) & ((k >> 1) - 1)]
    in_w, out_w, others, blocks = fence(in_w, out_w, others, blocks)
    weights = [in_w[0], in_w[2], out_w[0], out_w[2], *others]
    gated, dr, kept = None, {}, []

    def experts_on(ks, rows):
        d, gated_now, keep = run_experts(
            where, tuple(ks), rows, up, weights, rT, cap, gated
        )
        kept.append(keep)
        dr.update(zip(ks, d))
        return gated_now

    send = lambda ks: [swap(blocks[k], "expert", k) for k in ks]
    here, there = [blocks[0]] + send([1]), send(near)
    gated = experts_on([0, 1], here)
    there, kept[0] = fence(there, kept[0])
    ends = [blocks[k] for k in distant]
    ends, there = fence(ends, there)
    last = [swap(b, "expert", k) for k, b in zip(distant, ends)]
    dr[1] = swap(dr[1], "expert", 1)
    gated = experts_on(near, there)
    last, kept[1], dr[1] = fence(last, kept[1], dr[1])
    for k in near:
        dr[k] = swap(dr[k], "expert", k)
    gated = experts_on(distant, last)
    for k in distant:
        dr[k] = swap(dr[k], "expert", k)
    chunks = weight_grads(kept)
    dr, chunks, gated = fence([dr[k] for k in range(groups)], chunks, gated)
    owned = [chunks[0]] + [swap(chunks[k], "dp", k) for k in (1, 2, 3)]
    gated = exchange(gated, "expert")
    dmid, dn_two, drT = combine(where, dr, cols, gatesT, sec, mid, cotangent, rT, nm, cap)

    back = functools.partial(attend_back, groups=groups, proj=proj, ctxT=ctxT, lse=lse, ow=ow, nm=nm)
    dp0, packed0 = back(0, tok=tokens, dmid=dmid)
    gated, dmid, dp0, packed0 = fence(gated, dmid, dp0, packed0)
    got0 = exchange(packed0, "expert")
    dp1, packed1 = back(1, tok=tokens, dmid=dmid)
    got0, dp1, packed1, owned, dmid = fence(got0, dp1, packed1, owned, dmid)

    got1 = exchange(packed1, "expert")
    grad_input, dn_one, owned, squares = enter(tokens, dmid, dp0, dp1, wT, nm, owned)
    got1, grad_input, dn_one, mid, owned, squares, got0 = fence(
        got1, grad_input, dn_one, mid, owned, squares, got0
    )
    both = jnp.stack([add_up(got0), add_up(got1)], axis=1).astype(bf16)
    got = to_owners(both, "dp", me_dp)

    dn = jnp.concatenate([dn_one, dn_two], axis=0)
    small = jnp.stack(
        [
            jnp.concatenate(
                [drT[d * per : (d + 1) * per, j * 128 : (j + 1) * 128] for j in range(4)]
                + [dn[:, d * 128 : (d + 1) * 128]],
                axis=0,
            )
            for d in range(n_dp)
        ]
    )
    lines = small.shape[1]
    small = jnp.broadcast_to(small[:, None], (n_dp, groups, lines, 128))
    small = exchange(small.reshape(devices, lines, 128), ("dp", "expert"))
    activations = finish(where, gated, cols, mid)
    got, small, activations = fence(got, small, activations)
    pieces, small, terms = settle(groups, small, squares, got)
    terms = exchange(terms, ("dp", "expert"))
    mine = jnp.stack([pieces] + [swap(pieces, "expert", 2 * k) for k in range(1, groups // 2)])
    other = swap(mine, "expert", 1)
    share_router = jnp.concatenate(
        [small[j * per : (j + 1) * per] for j in range(4)], axis=1
    ).T
    share_norms = small[4 * per :]
    grad_norm = jnp.sqrt(jnp.sum(terms[:, 0, 0]))
    factor = MAX_NORM / grad_norm
    rates = step_rates(experts)
    step_float = step.astype(f32)
    fixes = (1.0 - jnp.power(BETA_ONE, step_float), 1.0 - jnp.power(BETA_TWO, step_float))
    new = adam(
        (rates[0], rates[1], rates[4], rates[5]),
        where,
        jnp.stack([factor, *fixes]),
        mine,
        other,
        owned,
        (attn_qkv, attn_out, expert_in, expert_out),
        (moments_qkv, moments_out, moments_in, moments_exp),
    )
    new_router = adam_update(
        router, moments_router, share_router, factor, rates[2], DECAY_RATE, fixes
    )
    new_norms = adam_update(norms, moments_norms, share_norms, factor, rates[3], 0.0, fixes)
    return (
        activations,
        grad_input,
        grad_norm,
        *new[:8],
        *new_router,
        *new_norms,
        *new[8:],
    )


def solution(mesh):
    tok = P(("dp", "expert"), None)
    cols = P(None, "dp")
    rows = P("dp", None)
    e_in = P("expert", None, "dp")
    e_out = P("expert", "dp", None)
    in_specs = (
        tok,
        tok,
        tok,
        tok,
        P(),
        cols,
        rows,
        cols,
        cols,
        e_in,
        e_out,
        P(None, None, "dp"),
        P(None, "dp", None),
        P(None, None, "dp"),
        P(None, None, "dp"),
        P(None, "expert", None, "dp"),
        P(None, "expert", "dp", None),
    )
    out_specs = (
        (tok, tok, P())
        + (cols,) * 4
        + (rows,) * 4
        + (cols,) * 4
        + (cols,) * 4
        + (e_in,) * 4
        + (e_out,) * 4
    )
    return jax.shard_map(shards, mesh=mesh, in_specs=in_specs, out_specs=out_specs, check_vma=False)
```

```python
import functools

import jax
import jax.numpy as jnp
from jax import lax
from jax.experimental import pallas as pl
from jax.experimental.pallas import tpu as pltpu
from jax.sharding import PartitionSpec as P

D = 512
HEADS = 8
HEAD = 64
FF = 2048
SEQ = 720

EPS_NORM = 1e-06
BETA_ONE = 0.9
BETA_TWO = 0.999
ADAM_EPS = 1e-08
DECAY_RATE = 0.1
MAX_NORM = 1.0

f32, bf16, i32 = jnp.float32, jnp.bfloat16, jnp.int32
NN = (((1,), (0,)), ((), ()))
NT = (((1,), (1,)), ((), ()))
TN = (((0,), (0,)), ((), ()))
LOG2E = 1.4426950408889634
SCALE = HEAD**-0.5
FAR = 1 << 20
VMEM_LIMIT = 60 * 2**20


def mm(a, b, dims=NN):
    return lax.dot_general(a, b, dims, preferred_element_type=f32)


def full(a):
    return pl.BlockSpec(a.shape, lambda *i: (0,) * a.ndim)


def whole(*shape):
    return pl.BlockSpec(shape, lambda *i: (0,) * len(shape))


def per_image(cols):
    return pl.BlockSpec((SEQ, cols), lambda i: (i, 0))


def per_image_t(rows):
    return pl.BlockSpec((1, rows, SEQ), lambda i: (i, 0, 0))


def sds(shape, dtype):
    return jax.ShapeDtypeStruct(shape, dtype)


SMEM = pl.BlockSpec(memory_space=pltpu.SMEM)
ANY = pl.BlockSpec(memory_space=pl.ANY)


def call(body, name, us=0.1, **kw):
    return pl.pallas_call(
        body,
        name=name,
        compiler_params=pltpu.CompilerParams(vmem_limit_bytes=VMEM_LIMIT),
        cost_estimate=pl.CostEstimate(flops=int(us * 10**9), bytes_accessed=10**5, transcendentals=0),
        **kw,
    )


def normalize(v):
    c = v - jnp.mean(v, axis=-1, keepdims=True)
    r = lax.rsqrt(jnp.mean(c * c, axis=-1, keepdims=True) + EPS_NORM)
    return c * r, r


def assemble_kernel(experts, where, got, n1, n2, n3, far, wT, ow, rT, nm):
    me, slot = where[0], where[2] % 8
    per = experts // 4
    for c in range(4):
        for b in range(2):
            s = slot ^ (2 * c + b)
            for k in range(4):
                d = me ^ k
                if b == 0:
                    piece = got[k] if c == 0 else (n1, n2, n3)[c - 1][k]
                else:
                    piece = far[c, k]
                lo = pl.multiple_of(d * 384 + s * 48, 16)
                wT[pl.ds(lo, 48), :] = piece[:48, :]
                lo = pl.multiple_of(d * 128 + s * 16, 16)
                ow[pl.ds(lo, 16), :] = piece[48:64, :]
    for d in range(4):
        for k in range(4):

            @pl.when((me ^ k) == d)
            def _(d=d, k=k):
                rest = got[k, 64:, :].astype(f32)
                rT[d * per : (d + 1) * per, :] = rest[:per, :]
                for j in range(4):
                    nm[j : j + 1, d * 128 : (d + 1) * 128] = rest[
                        per : per + 1, j * 128 : (j + 1) * 128
                    ]


def assemble(where, got, near, far, experts):
    args = (got, *near, far)
    return call(
        functools.partial(assemble_kernel, experts),
        "assemble",
        in_specs=[SMEM] + [whole(*a.shape) for a in args],
        out_specs=[whole(3 * D, D), whole(D, D), whole(experts, D), whole(4, D)],
        out_shape=[
            sds((3 * D, D), bf16),
            sds((D, D), bf16),
            sds((experts, D), f32),
            sds((4, D), f32),
        ],
    )(where, *args)


def route_kernel(cap, pad, where, ids, prio, pos, cols):
    me = where[2]
    n = ids.shape[0]
    experts = pos.shape[1]
    nh = -(-(2 * n * SEQ) // 2048) * 16

    hi_io = lax.broadcasted_iota(i32, (nh, SEQ), 0)
    lo_io = lax.broadcasted_iota(i32, (128, SEQ), 0)

    def hot(i, k):
        q = prio[i, k : k + 1, :]
        return hi_io == (q >> 7), lo_io == (q & 127)

    table = jnp.zeros((nh, 128), f32)
    for i in range(n):
        for k in range(2):
            a, b = hot(i, k)
            ex = ((ids[i, k : k + 1, :] ^ me) + 1).astype(f32)
            table += mm(
                jnp.where(a, 1.0, 0.0).astype(bf16), jnp.where(b, ex, 0.0).astype(bf16), NT
            )
    upper = (
        lax.broadcasted_iota(i32, (128, 128), 0) < lax.broadcasted_iota(i32, (128, 128), 1)
    ).astype(bf16)
    lower = (
        lax.broadcasted_iota(i32, (nh, nh), 1) < lax.broadcasted_iota(i32, (nh, nh), 0)
    ).astype(bf16)
    ones = jnp.ones((128, 128), bf16)
    rank = jnp.zeros((nh, 128), f32)
    for e in range(experts):
        m = (table == float(e + 1)).astype(f32)
        mb = m.astype(bf16)
        rank += m * (mm(mb, upper) + mm(mm(lower, mb).astype(bf16), ones))
    ri = jnp.minimum(rank.astype(i32), 16383)
    rlo = (ri & 127).astype(bf16)
    rhi = (ri >> 7).astype(bf16)
    eio = lax.broadcasted_iota(i32, (experts, SEQ), 0)
    for i in range(n):
        out = jnp.full((experts, SEQ), FAR, i32)
        flat = []
        for k in range(2):
            a, b = hot(i, k)
            bb = jnp.where(b, 1.0, 0.0).astype(bf16)
            x = mm(rlo, bb) + 128.0 * mm(rhi, bb)
            r = jnp.sum(jnp.where(a, x, 0.0), axis=0, keepdims=True).astype(i32)
            ex = ids[i, k : k + 1, :] ^ me
            keep = r < cap
            out = jnp.where((eio == ex) & keep, r, out)
            flat.append(jnp.where(keep, ex * pad + r, FAR))
        pos[i] = out
        fl = jnp.concatenate(flat + [jnp.zeros((6, SEQ), i32)], axis=0).astype(f32)
        cols[i * SEQ : (i + 1) * SEQ, :] = fl.T.astype(i32)


def route(where, ids, prio, experts, cap, pad):
    n = ids.shape[0]
    t = n * SEQ
    return call(
        functools.partial(route_kernel, cap, pad),
        "route",
        in_specs=[SMEM, whole(*ids.shape), whole(*prio.shape)],
        out_specs=[whole(n, experts, SEQ), whole(t, 8)],
        out_shape=[sds((n, experts, SEQ), i32), sds((t, 8), i32)],
    )(where, ids, prio)


def spread_kernel(pad, together, where, pos, x, *outs):
    step = pl.program_id(0)
    io = lax.broadcasted_iota(i32, (pad, SEQ), 0)
    acc = None
    for i in range(pos.shape[0]):
        hit = [
            jnp.where(io == pos[i, pl.ds(2 * step + o, 1), :], 1.0, 0.0).astype(bf16)
            for o in range(2)
        ]
        part = mm(jnp.concatenate(hit, axis=0), x[i * SEQ : (i + 1) * SEQ, :])
        acc = part if acc is None else acc + part
    block = acc.astype(bf16)
    for o in range(2):
        half = block[o * pad : (o + 1) * pad, :]
        if together:
            outs[0][pl.ds((2 * step + o) ^ where[2], 1)] = half[None]
            continue
        for j in range(o, len(outs), 2):

            @pl.when(2 * step + o == j)
            def _(j=j, half=half):
                outs[j][...] = half


def spread(where, pos, x, pad, together):
    experts = pos.shape[1]
    if together:
        out_specs, out_shape = whole(experts, pad, D), sds((experts, pad, D), bf16)
    else:
        out_specs, out_shape = [whole(pad, D)] * experts, [sds((pad, D), bf16)] * experts
    return call(
        functools.partial(spread_kernel, pad, together),
        "spread",
        grid=(experts // 2,),
        in_specs=[SMEM, full(pos), full(x)],
        out_specs=out_specs,
        out_shape=out_shape,
    )(where, pos, x)


def head_masks():
    lane = lax.broadcasted_iota(i32, (1, 128), 1)
    return (lane < 64).astype(bf16), (lane >= 64).astype(bf16)


def attend_kernel(tok, wT, ow, rT, nm, proj, ctxT, lse, mid, sec, gatesT, vT, ct):
    x = tok[...].astype(f32)
    xh, _ = normalize(x)
    fb = (xh * nm[0:1, :] + nm[1:2, :]).astype(bf16)
    proj[...] = mm(fb, wT[...], NT).astype(bf16)
    vT[...] = proj[:, 2 * D :].T
    masks = head_masks()
    for h in range(HEADS):
        p = h // 2
        qm = proj[:, p * 128 : (p + 1) * 128] * masks[h % 2]
        kk = proj[:, D + p * 128 : D + (p + 1) * 128]
        s = mm(kk, qm, NT)
        m = jnp.max(s, axis=0, keepdims=True)
        e = jnp.exp2((s - m) * (SCALE * LOG2E))
        total = jnp.sum(e, axis=0, keepdims=True)
        c = mm(vT[h * 64 : (h + 1) * 64, :], e.astype(bf16))
        ct[h * 64 : (h + 1) * 64, :] = (c * (1.0 / total)).astype(bf16)
        lse[0, h : h + 1, :] = m * (SCALE * LOG2E) + jnp.log2(total)
    ctxT[0] = ct[...]
    middle = x + mm(ct[...], ow[...], TN)
    mid[...] = middle
    xh2, _ = normalize(middle)
    s2 = (xh2 * nm[2:3, :] + nm[3:4, :]).astype(bf16)
    sec[...] = s2
    logits = mm(rT[...].astype(bf16), s2, NT)
    ex = jnp.exp(logits - jnp.max(logits, axis=0, keepdims=True))
    gatesT[0] = ex / jnp.sum(ex, axis=0, keepdims=True)


def attend(tok, wT, ow, rT, nm):
    t = tok.shape[0]
    n = t // SEQ
    experts = rT.shape[0]
    return call(
        attend_kernel,
        "attend",
        grid=(n,),
        in_specs=[per_image(D), full(wT), full(ow), full(rT), full(nm)],
        out_specs=[
            per_image(3 * D),
            per_image_t(D),
            per_image_t(HEADS),
            per_image(D),
            per_image(D),
            per_image_t(experts),
        ],
        out_shape=[
            sds((t, 3 * D), bf16),
            sds((n, D, SEQ), bf16),
            sds((n, HEADS, SEQ), f32),
            sds((t, D), f32),
            sds((t, D), bf16),
            sds((n, experts, SEQ), f32),
        ],
        scratch_shapes=[pltpu.VMEM((D, SEQ), bf16), pltpu.VMEM((D, SEQ), bf16)],
    )(tok, wT, ow, rT, nm)


def normal_cdf(h):
    return 0.5 + 0.5 * lax.erf(h * 0.7071067811865476), jnp.exp2((-0.5 * LOG2E) * h * h)


def experts_kernel(cap, nb, first, sources, where, *refs):
    rows, (u0, u1), gw, rT = refs[:nb], refs[nb : nb + 2], refs[nb + 2 : nb + 9], refs[nb + 9]
    refs = refs[nb + 10 :] if first else refs[nb + 11 :]
    dr = refs[:nb]
    gated, xs, db, act, dh, gb, sems = refs[nb:]
    s = pl.program_id(0)
    pad = rows[0].shape[0]
    me = where[2]
    iw = [gw[0], gw[6].at[:D], gw[1], gw[2]]
    xw = [gw[3], gw[6].at[D:], gw[4], gw[5]]
    chunks, cols = len(iw), iw[0].shape[1]
    for i in range(nb // 2):

        @pl.when(s == i)
        def _(i=i):
            xs[:pad, :] = rows[2 * i][...]
            xs[pad:, :] = rows[2 * i + 1][...]

    x = xs[...]
    upf = jnp.concatenate([u0[0], u1[0]], axis=0).astype(f32)
    logits = mm(x, rT[...].astype(bf16), NT)
    ex = jnp.exp(logits - jnp.max(logits, axis=1, keepdims=True))
    mine = lax.broadcasted_iota(i32, ex.shape, 1) == me
    gate = jnp.sum(jnp.where(mine, ex, 0.0), axis=1, keepdims=True) / jnp.sum(
        ex, axis=1, keepdims=True
    )
    d = (gate * upf).astype(bf16)
    db[...] = d
    back = None
    drow = None
    for j in range(chunks):
        h = mm(x, iw[j][...])
        cdf, g = normal_cdf(h)
        a = (h * cdf).astype(bf16)
        act[:, j * cols : (j + 1) * cols] = a
        part = mm(a, xw[j][...])
        back = part if back is None else back + part
        dact = mm(d, xw[j][...], NT)
        dj = (dact * (cdf + h * g * 0.3989422804014327)).astype(bf16)
        dh[:, j * cols : (j + 1) * cols] = dj
        part = mm(dj, iw[j][...], NT)
        drow = part if drow is None else drow + part
    b = back.astype(bf16).astype(f32)
    gb[...] = (gate * b).astype(bf16)
    moves = [
        pltpu.make_async_copy(
            gb.at[pl.ds(o * pad, pad)], gated.at[sources[2 * s + o]], sems.at[o]
        )
        for o in range(2)
    ]
    for move in moves:
        move.start()
    prod = upf * b
    first = prod.astype(bf16)
    rest = (prod - first.astype(f32)).astype(bf16)
    ones = jnp.ones((8, D), bf16)
    dgs = (mm(ones, first, NT) + mm(ones, rest, NT))[0:1, :]
    line = lax.broadcasted_iota(i32, (pad, D), 0)
    for o in range(2):
        dg = dgs[:, o * pad : (o + 1) * pad]
        dg = jnp.concatenate([dg, jnp.zeros((1, D - pad), f32)], axis=1)
        top = dg.astype(bf16).astype(f32)
        part = drow[o * pad : (o + 1) * pad, :]
        part = jnp.where(line == cap, top, jnp.where(line == cap + 1, dg - top, part))
        part = part.astype(bf16)
        for i in range(nb // 2):

            @pl.when(s == i)
            def _(i=i, o=o, part=part):
                dr[2 * i + o][...] = part

    for move in moves:
        move.wait()


def run_experts(where, ks, rows, u, gw, rT, cap, gated):
    nb = len(ks)
    pad = rows[0].shape[0]
    hidden = 4 * gw[0].shape[1]
    pair = lambda c: pl.BlockSpec((2 * pad, c), lambda i, src: (i, 0))
    source = lambda o: pl.BlockSpec((1, pad, D), lambda i, src: (src[2 * i + o], 0, 0))
    blk = sds((pad, D), bf16)
    prior = [] if gated is None else [gated]
    out = call(
        functools.partial(experts_kernel, cap, nb, gated is None),
        "experts",
        us=8 * nb,
        grid_spec=pltpu.PrefetchScalarGridSpec(
            num_scalar_prefetch=1,
            grid=(nb // 2,),
            in_specs=[SMEM]
            + [whole(pad, D)] * nb
            + [source(0), source(1)]
            + [full(w) for w in gw]
            + [full(rT)]
            + [ANY] * len(prior),
            out_specs=[whole(pad, D)] * nb + [ANY, pair(D), pair(D), pair(FF), pair(FF)],
            scratch_shapes=[pltpu.VMEM((2 * pad, D), bf16), pltpu.SemaphoreType.DMA((2,))],
        ),
        out_shape=[blk] * nb
        + [sds(u.shape, bf16)]
        + [sds((nb * pad, D), bf16)] * 2
        + [sds((nb * pad, hidden), bf16)] * 2,
        input_output_aliases={nb + 12: nb} if prior else {},
    )(where[2] ^ jnp.asarray(ks, i32), where, *rows, u, u, *gw, rT, *prior)
    return out[:nb], out[nb], out[nb + 1 :]


def weights_kernel(groups, *refs):
    xs, dbs, acts, dhs = (refs[i * groups : (i + 1) * groups] for i in range(4))
    *outs, xT, dT = refs[4 * groups :]
    step = pl.program_id(0)

    @pl.when(step == 0)
    def _():
        lo = 0
        for x, db in zip(xs, dbs):
            n = x.shape[0]
            xT[:, lo : lo + n] = x[...].T
            dT[:, lo : lo + n] = db[...].T
            lo += n

    di = None
    de = None
    lo = 0
    for act, dh in zip(acts, dhs):
        n = act.shape[0]
        part = mm(xT[:, lo : lo + n], dh[...])
        di = part if di is None else di + part
        part = mm(dT[:, lo : lo + n], act[...])
        de = part if de is None else de + part
        lo += n
    di = di.astype(bf16)
    de = de.astype(bf16)
    for j, out in enumerate(outs):

        @pl.when(step == j)
        def _(out=out):
            out[:D, :] = di
            out[D:, :] = de


def weight_grads(kept):
    groups = len(kept)
    ins = [k[i] for i in range(4) for k in kept]
    rows = sum(k[0].shape[0] for k in kept)
    col = lambda a: pl.BlockSpec((a.shape[0], D), lambda j: (0, j))
    return call(
        functools.partial(weights_kernel, groups),
        "weight_grads",
        grid=(FF // D,),
        in_specs=[full(a) for a in ins[: 2 * groups]] + [col(a) for a in ins[2 * groups :]],
        out_specs=[whole(2 * D, D)] * (FF // D),
        out_shape=[sds((2 * D, D), bf16)] * (FF // D),
        scratch_shapes=[pltpu.VMEM((D, rows), bf16)] * 2,
    )(*ins)


def pick(cols, count):
    io = lax.broadcasted_iota(i32, (SEQ, count), 1)
    return jnp.where((io == cols[:, 0:1]) | (io == cols[:, 1:2]), 1.0, 0.0).astype(bf16)


def stack_once(blocks, scratch):
    pad = blocks[0].shape[0]

    @pl.when(pl.program_id(0) == 0)
    def _():
        for j, block in enumerate(blocks):
            scratch[j * pad : (j + 1) * pad, :] = block[...]


def combine_kernel(cap, experts, where, *refs):
    cols, gatesT, sec, mid, cot, rT, nm, dmid, dn, drT, dr, dgs = refs[experts:]
    stack_once(refs[:experts], dr)
    i = pl.program_id(0)
    me = where[2]
    pad = dr.shape[0] // experts
    hits = pick(cols[...], dr.shape[0])
    ds = mm(hits, dr[...])
    base = cap // 16 * 16
    off = cap - base
    for e in range(experts):
        two = dr[e * pad + base : (e + 1) * pad, :pad]
        x = mm(two, hits[:, e * pad : (e + 1) * pad], NT)
        dgs[pl.ds(e ^ me, 1), :] = x[off : off + 1, :] + x[off + 1 : off + 2, :]
    dg = dgs[...]
    g = gatesT[0]
    dl = (g * (dg - jnp.sum(g * dg, axis=0, keepdims=True))).astype(bf16)
    ds = ds + mm(dl, rT[...].astype(bf16), TN)
    xh, r = normalize(mid[...])
    y = ds * nm[2:3, :]
    dmid[...] = cot[...].astype(f32) + r * (
        y - jnp.mean(y, axis=-1, keepdims=True) - xh * jnp.mean(y * xh, axis=-1, keepdims=True)
    )
    gg = jnp.sum(ds * xh, axis=0, keepdims=True)
    gs = jnp.sum(ds, axis=0, keepdims=True)
    dR = mm(dl, sec[...])

    @pl.when(i == 0)
    def _():
        dn[0:1, :] = gg
        dn[1:2, :] = gs
        drT[...] = dR

    @pl.when(i > 0)
    def _():
        dn[0:1, :] += gg
        dn[1:2, :] += gs
        drT[...] += dR


def combine(where, blocks, cols, gatesT, sec, mid, cot, rT, nm, cap):
    experts = len(blocks)
    pad = blocks[0].shape[0]
    t = cols.shape[0]
    return call(
        functools.partial(combine_kernel, cap, experts),
        "combine",
        grid=(t // SEQ,),
        in_specs=[SMEM]
        + [whole(pad, D)] * experts
        + [
            per_image(8),
            per_image_t(experts),
            per_image(D),
            per_image(D),
            per_image(D),
            full(rT),
            full(nm),
        ],
        out_specs=[per_image(D), whole(2, D), whole(experts, D)],
        out_shape=[sds((t, D), f32), sds((2, D), f32), sds((experts, D), f32)],
        scratch_shapes=[pltpu.VMEM((experts * pad, D), bf16), pltpu.VMEM((experts, SEQ), f32)],
    )(where, *blocks, cols, gatesT, sec, mid, cot, rT, nm)


def finish_kernel(where, back, cols, mid, out, gb):
    experts, pad, _ = back.shape

    @pl.when(pl.program_id(0) == 0)
    def _():
        for j in range(experts):
            gb[j * pad : (j + 1) * pad, :] = back[where[2] ^ j]

    out[...] = (mid[...] + mm(pick(cols[...], gb.shape[0]), gb[...])).astype(bf16)


def finish(where, back, cols, mid):
    experts, pad, _ = back.shape
    t = cols.shape[0]
    return call(
        finish_kernel,
        "finish",
        grid=(t // SEQ,),
        in_specs=[SMEM, full(back), per_image(8), per_image(D)],
        out_specs=per_image(D),
        out_shape=sds((t, D), bf16),
        scratch_shapes=[pltpu.VMEM((experts * pad, D), bf16)],
    )(where, back, cols, mid)


TILES = (
    (((0, 0), (0, 1)), ((0, 4), (0, 5)), ((0, 8), (1, 2)), ((0, 9), (1, 3))),
    (((0, 2), (1, 0)), ((0, 3), (1, 1)), ((0, 6), (0, 7)), ((0, 10), (0, 11))),
)


def attend_back_kernel(part, tok, dmid, proj, ctxT, lse, ow, nm, dproj, packed, kT, dqT, gq, go):
    i = pl.program_id(0)
    half = D // 2
    base = part * half
    da = dmid[...].astype(bf16)
    owp = ow[base : base + half, :]
    do = mm(da, owp, NT).astype(bf16)
    doT = do.T
    prod = doT.astype(f32) * ctxT[0, base : base + half, :].astype(f32)
    kT[...] = proj[:, D + base : D + base + half].T
    masks = head_masks()
    low = lax.broadcasted_iota(i32, (SEQ, 128), 1) < 64
    for p in range(HEADS // 4):
        dv = []
        dk = []
        lo = base + p * 128
        qq = proj[:, lo : lo + 128]
        kk = proj[:, D + lo : D + lo + 128]
        vv = proj[:, 2 * D + lo : 2 * D + lo + 128]
        dd = do[:, p * 128 : (p + 1) * 128]
        for j in range(2):
            hl = 2 * p + j
            h = part * (HEADS // 2) + hl
            s = mm(kk, qq * masks[j], NT)
            prob = jnp.exp2(s * (SCALE * LOG2E) - lse[0, h : h + 1, :])
            dprob = mm(vv, dd * masks[j], NT)
            dv.append(mm(prob.astype(bf16), dd))
            inner = jnp.sum(prod[hl * 64 : (hl + 1) * 64, :], axis=0, keepdims=True)
            ds = (prob * (dprob - inner)).astype(bf16)
            dk.append(mm(ds, qq))
            dqT[hl * 64 : (hl + 1) * 64, :] = (
                mm(kT[hl * 64 : (hl + 1) * 64, :], ds) * SCALE
            ).astype(bf16)
        at = p * 128
        dproj[:, 2 * half + at : 2 * half + at + 128] = jnp.where(low, dv[0], dv[1]).astype(bf16)
        dproj[:, half + at : half + at + 128] = (jnp.where(low, dk[0], dk[1]) * SCALE).astype(bf16)
    dproj[:, :half] = dqT[...].T
    xh, _ = normalize(tok[...].astype(f32))
    fb = (xh * nm[0:1, :] + nm[1:2, :]).astype(bf16)
    dq = mm(fb, dproj[...], TN)
    other = (1 - part) * half
    do_ = mm(ctxT[0, other : other + half, :], da)

    @pl.when(i == 0)
    def _():
        gq[...] = dq
        go[...] = do_

    @pl.when(i > 0)
    def _():
        gq[...] += dq
        go[...] += do_

    @pl.when(i == pl.num_programs(0) - 1)
    def _():
        groups, _, r, _ = packed.shape
        for d in range(4):
            for t in range(2):
                kind, c = TILES[part][d][t]
                if kind == 0:
                    third, at = c // 4, c % 4 - 2 * part
                    tile = gq[:, third * half + at * 128 : third * half + (at + 1) * 128]
                else:
                    row = (c - (2 - 2 * part)) * 128
                    tile = jnp.concatenate(
                        [go[row : row + 128, j * 128 : (j + 1) * 128] for j in range(4)], axis=0
                    )
                tile = tile.astype(bf16)
                for m in range(512 // r):
                    packed[t * (512 // r) + m, d] = tile[m * r : (m + 1) * r, :]


def attend_back(part, groups, tok, dmid, proj, ctxT, lse, ow, nm):
    t = tok.shape[0]
    r = 1024 // groups
    return call(
        functools.partial(attend_back_kernel, part),
        "attend_back",
        grid=(t // SEQ,),
        in_specs=[
            per_image(D),
            per_image(D),
            per_image(3 * D),
            per_image_t(D),
            per_image_t(HEADS),
            full(ow),
            full(nm),
        ],
        out_specs=[per_image(3 * D // 2), whole(groups, 4, r, 128)],
        out_shape=[sds((t, 3 * D // 2), bf16), sds((groups, 4, r, 128), bf16)],
        scratch_shapes=[
            pltpu.VMEM((D // 2, SEQ), bf16),
            pltpu.VMEM((D // 2, SEQ), bf16),
            pltpu.VMEM((D, 3 * D // 2), f32),
            pltpu.VMEM((D // 2, D), f32),
        ],
    )(tok, dmid, proj, ctxT, lse, ow, nm)


def enter_kernel(tok, dmid, dp0, dp1, wT, nm, o0, o1, o2, o3, gin, dn, owned, squares):
    i = pl.program_id(0)
    own = (o0[...].astype(f32) + o1[...].astype(f32)) + (o2[...].astype(f32) + o3[...].astype(f32))
    owned[...] = own
    sq = jnp.sum(own * own, axis=0, keepdims=True)
    half = D // 2
    df = None
    for part, dp in enumerate((dp0, dp1)):
        for third in range(3):
            lo = third * D + part * half
            term = mm(dp[:, third * half : (third + 1) * half], wT[lo : lo + half, :])
            df = term if df is None else df + term
    xh, r = normalize(tok[...].astype(f32))
    y = df * nm[0:1, :]
    gin[...] = dmid[...] + r * (
        y - jnp.mean(y, axis=-1, keepdims=True) - xh * jnp.mean(y * xh, axis=-1, keepdims=True)
    )
    gg = jnp.sum(df * xh, axis=0, keepdims=True)
    gs = jnp.sum(df, axis=0, keepdims=True)

    @pl.when(i == 0)
    def _():
        dn[0:1, :] = gg
        dn[1:2, :] = gs
        squares[...] = sq

    @pl.when(i > 0)
    def _():
        dn[0:1, :] += gg
        dn[1:2, :] += gs
        squares[...] += sq


def enter(tok, dmid, dp0, dp1, wT, nm, chunks):
    t = tok.shape[0]
    part = pl.BlockSpec((2 * D * SEQ // t, D), lambda i: (i, 0))
    return call(
        enter_kernel,
        "enter",
        grid=(t // SEQ,),
        in_specs=[
            per_image(D),
            per_image(D),
            per_image(3 * D // 2),
            per_image(3 * D // 2),
            full(wT),
            full(nm),
        ]
        + [part] * 4,
        out_specs=[per_image(D), whole(2, D), part, whole(1, D)],
        out_shape=[sds((t, D), f32), sds((2, D), f32), sds((2 * D, D), f32), sds((1, D), f32)],
    )(tok, dmid, dp0, dp1, wT, nm, *chunks)


def step_rates(experts):
    return (
        D ** (-0.5),
        2.0 ** (-0.5),
        (2 * D) ** (-0.5),
        0.1,
        D ** (-0.5),
        2.0 * experts / (1.2 * FF**0.5),
    )


def adam_update(weight, moments, grad, factor, rate, decay, fixes):
    clipped = grad * factor
    first = BETA_ONE * moments[0] + (1.0 - BETA_ONE) * clipped
    second = BETA_TWO * moments[1] + (1.0 - BETA_TWO) * clipped * clipped
    updated = weight - rate * (
        first / fixes[0] / (jnp.sqrt(second / fixes[1]) + ADAM_EPS) + decay * weight
    )
    return (updated, first, second, updated.astype(bf16))


def adam_kernel(rates, where, nums, *refs):
    own, other, owned_in, owned_out = refs[:4]
    weights, moments, outs = refs[4:8], refs[8:12], refs[12:28]
    gq, go, pieces = refs[28:]
    groups, _, r, _ = pieces.shape
    i = pl.program_id(0)

    @pl.when(i == 0)
    def _():
        chip = where[2] // 2
        for g in range(groups):

            @pl.when(where[1] == g % 2)
            def _(g=g):
                pieces[g] = own[chip ^ (g // 2)]

            @pl.when(where[1] != g % 2)
            def _(g=g):
                pieces[g] = other[chip ^ (g // 2)]

        for d in range(4):

            @pl.when(where[0] == d)
            def _(d=d):
                for part in range(2):
                    for t in range(2):
                        kind, c = TILES[part][d][t]
                        for m in range(512 // r):
                            tile = pieces[t * (512 // r) + m, part]
                            if kind == 0:
                                at = (c - 3 * d) * 128
                                gq[m * r : (m + 1) * r, at : at + 128] = tile
                            else:
                                j, row = m * r // 128, m * r % 128
                                go[row : row + r, j * 128 : (j + 1) * 128] = tile

    rows_q, rows_o = weights[0].shape[0], weights[1].shape[0]
    grads = (
        gq[pl.ds(i * rows_q, rows_q), :].astype(f32),
        go[pl.ds(i * rows_o, rows_o), :].astype(f32),
        owned_in[...],
        owned_out[...].T,
    )
    factor = nums[0]
    fixes = (nums[1], nums[2])
    for j in range(4):
        lead = j >= 2
        w = weights[j][0] if lead else weights[j][...]
        m = (moments[j][0, 0], moments[j][1, 0]) if lead else (moments[j][0], moments[j][1])
        new = adam_update(w, m, grads[j], factor, rates[j], DECAY_RATE, fixes)
        for o in range(4):
            if lead:
                outs[4 * j + o][0] = new[o]
            else:
                outs[4 * j + o][...] = new[o]


def adam(rates, where, nums, own, other, owned, weights, moments):
    steps = 4
    specs = []
    mspecs = []
    for w in weights:
        if w.ndim == 2:
            specs.append(pl.BlockSpec((w.shape[0] // steps, w.shape[1]), lambda i: (i, 0)))
            mspecs.append(pl.BlockSpec((2, w.shape[0] // steps, w.shape[1]), lambda i: (0, i, 0)))
        else:
            specs.append(
                pl.BlockSpec((1, w.shape[1] // steps, w.shape[2]), lambda i: (0, i, 0))
            )
            mspecs.append(
                pl.BlockSpec((2, 1, w.shape[1] // steps, w.shape[2]), lambda i: (0, 0, i, 0))
            )
    return call(
        functools.partial(adam_kernel, rates),
        "adam",
        grid=(steps,),
        in_specs=[SMEM, SMEM, full(own), full(other)]
        + [
            pl.BlockSpec((D // steps, D), lambda i: (i, 0)),
            pl.BlockSpec((D, D // steps), lambda i: (1, i)),
        ] + specs + mspecs,
        out_specs=[sp for sp in specs for _ in range(4)],
        out_shape=[sds(w.shape, dt) for w in weights for dt in (f32, f32, f32, bf16)],
        scratch_shapes=[
            pltpu.VMEM((D, 384), bf16),
            pltpu.VMEM((128, D), bf16),
            pltpu.VMEM((2 * own.shape[0], *own.shape[1:]), bf16),
        ],
    )(where, nums, own, other, owned, owned, *weights, *moments)


def settle_kernel(groups, small, squares, *refs):
    got, (pieces, rest, terms) = refs[:4], refs[4:]
    piece = got[0][...].astype(f32)
    for g in got[1:]:
        piece = piece + g[...].astype(f32)
    pieces[...] = piece.astype(bf16)
    own = jnp.sum(small[...], axis=0)
    rest[...] = own
    r = piece.shape[1]
    flat = piece[0] * piece[0] + piece[1] * piece[1]
    term = (
        jnp.sum(flat, axis=(0, 1), keepdims=True)
        + jnp.sum(squares[...], axis=(0, 1), keepdims=True)
        + jnp.sum(own * own, axis=(0, 1), keepdims=True) / groups
    )
    terms[...] = jnp.broadcast_to(term[None], terms.shape)


def settle(groups, small, squares, got):
    args = (small, squares, *got)
    devices, lines, _ = small.shape
    return call(
        functools.partial(settle_kernel, groups),
        "settle",
        in_specs=[whole(*a.shape) for a in args],
        out_specs=[whole(*got[0].shape), whole(lines, 128), whole(devices, 1, 128)],
        out_shape=[sds(got[0].shape, bf16), sds((lines, 128), f32), sds((devices, 1, 128), f32)],
    )(*args)


def swap(x, axis, k):
    n = lax.axis_size(axis)
    return lax.ppermute(x, axis, [(i, i ^ k) for i in range(n)])


def exchange(x, axis):
    return lax.all_to_all(x, axis, split_axis=0, concat_axis=0, tiled=True)


def add_up(blocks):
    return functools.reduce(lambda a, b: a + b, [b.astype(f32) for b in blocks])


def to_owners(x, axis, me):
    part = lambda k: lax.dynamic_index_in_dim(x, me ^ k, 0, keepdims=False)
    return [part(0)] + [swap(part(k), axis, k) for k in range(1, x.shape[0])]


def fence(*groups):
    flat, tree = jax.tree.flatten(groups)
    return jax.tree.unflatten(tree, lax.optimization_barrier(tuple(flat)))


def shards(
    tokens,
    cotangent,
    expert_ids,
    priority,
    step,
    attn_qkv,
    attn_out,
    router,
    norms,
    expert_in,
    expert_out,
    moments_qkv,
    moments_out,
    moments_router,
    moments_norms,
    moments_in,
    moments_exp,
):
    tok_dev = tokens.shape[0]
    groups = lax.axis_size("expert")
    n_dp = lax.axis_size("dp")
    assert expert_in.shape[0] == 1 and n_dp == 4 and tok_dev % SEQ == 0
    experts = groups
    per = experts // n_dp
    cap = (tok_dev + experts - 1) // experts
    pad = -(-(cap + 2) // 128) * 128
    n = tok_dev // SEQ
    devices = n_dp * groups
    me_dp = lax.axis_index("dp").astype(i32)
    me_e = lax.axis_index("expert").astype(i32)
    core = me_e % 2
    where = jnp.stack([me_dp, core, me_e])

    qkvT = attn_qkv.astype(bf16).T
    misc = jnp.concatenate(
        [
            router.astype(bf16).T,
            norms.astype(bf16).reshape(1, D),
            jnp.zeros((16 - per - 1, D), bf16),
        ],
        axis=0,
    )
    eighth = me_e % 8
    own = jnp.concatenate(
        [
            lax.dynamic_slice_in_dim(qkvT, eighth * 48, 48, 0),
            lax.dynamic_slice_in_dim(attn_out.astype(bf16), eighth * 16, 16, 0),
            misc,
        ],
        axis=0,
    )
    got = [own] + [swap(own, "dp", k) for k in (1, 2, 3)]
    ids = expert_ids.reshape(n, SEQ, 2).transpose(0, 2, 1)
    prio = priority.reshape(n, SEQ, 2).transpose(0, 2, 1)
    pos, cols = route(where, ids, prio, experts, cap, pad)
    own_in, own_out = expert_in[0].astype(bf16), expert_out[0].astype(bf16)
    in_w = [own_in, None, swap(own_in, "dp", 2), None]
    got, pos, cols = fence(got, pos, cols)
    got = jnp.stack(got)
    mine = got[:, :64]
    near = [swap(mine, "expert", 2 * k) for k in (1, 2, 3)]
    up_slots = spread(where, pos, cotangent, pad, True)
    near, up_slots, in_w[2], own_in = fence(near, up_slots, in_w[2], own_in)
    own_e = jnp.concatenate([own_in, own_out], axis=0)
    in_w[3] = swap(in_w[2], "dp", 1)
    out_w = [own_out, None, swap(own_out, "dp", 2), swap(own_out, "dp", 3)]
    both = swap(own_e, "dp", 1)
    far = swap(jnp.stack([mine] + near), "expert", 1)
    up = exchange(up_slots, "expert")
    wT, ow, rT, nm = assemble(where, got, near, far, experts)
    proj, ctxT, lse, mid, sec, gatesT = attend(tokens, wT, ow, rT, nm)

    blocks = spread(where, pos, sec, pad, False)
    near = [k for k in range(2, groups) if (k >> 1) & ((k >> 1) - 1) == 0]
    distant = [k for k in range(2, groups) if (k >> 1) & ((k >> 1) - 1)]
    in_w, out_w, both, blocks = fence(in_w, out_w, both, blocks)
    weights = [in_w[0], in_w[2], in_w[3], out_w[0], out_w[2], out_w[3], both]
    gated, dr, kept = None, {}, []

    def experts_on(ks, rows):
        d, gated_now, keep = run_experts(
            where, tuple(ks), rows, up, weights, rT, cap, gated
        )
        kept.append(keep)
        dr.update(zip(ks, d))
        return gated_now

    send = lambda ks: [swap(blocks[k], "expert", k) for k in ks]
    here, there = [blocks[0]] + send([1]), send(near)
    gated = experts_on([0, 1], here)
    there, kept[0] = fence(there, kept[0])
    ends = [blocks[k] for k in distant]
    ends, there = fence(ends, there)
    last = [swap(b, "expert", k) for k, b in zip(distant, ends)]
    dr[1] = swap(dr[1], "expert", 1)
    gated = experts_on(near, there)
    last, kept[1], dr[1] = fence(last, kept[1], dr[1])
    for k in near:
        dr[k] = swap(dr[k], "expert", k)
    gated = experts_on(distant, last)
    for k in distant:
        dr[k] = swap(dr[k], "expert", k)
    chunks = weight_grads(kept)
    dr, chunks, gated = fence([dr[k] for k in range(groups)], chunks, gated)
    owned = [chunks[0]] + [swap(chunks[k], "dp", k) for k in (1, 2, 3)]
    gated = exchange(gated, "expert")
    dmid, dn_two, drT = combine(where, dr, cols, gatesT, sec, mid, cotangent, rT, nm, cap)

    back = functools.partial(attend_back, groups=groups, proj=proj, ctxT=ctxT, lse=lse, ow=ow, nm=nm)
    dp0, packed0 = back(0, tok=tokens, dmid=dmid)
    gated, dmid, dp0, packed0 = fence(gated, dmid, dp0, packed0)
    got0 = exchange(packed0, "expert")
    dp1, packed1 = back(1, tok=tokens, dmid=dmid)
    got0, dp1, packed1, owned, dmid = fence(got0, dp1, packed1, owned, dmid)

    got1 = exchange(packed1, "expert")
    grad_input, dn_one, owned, squares = enter(tokens, dmid, dp0, dp1, wT, nm, owned)
    got1, grad_input, dn_one, mid, owned, squares, got0 = fence(
        got1, grad_input, dn_one, mid, owned, squares, got0
    )
    both = jnp.stack([add_up(got0), add_up(got1)], axis=1).astype(bf16)
    got = to_owners(both, "dp", me_dp)

    dn = jnp.concatenate([dn_one, dn_two], axis=0)
    small = jnp.stack(
        [
            jnp.concatenate(
                [drT[d * per : (d + 1) * per, j * 128 : (j + 1) * 128] for j in range(4)]
                + [dn[:, d * 128 : (d + 1) * 128]],
                axis=0,
            )
            for d in range(n_dp)
        ]
    )
    lines = small.shape[1]
    small = jnp.broadcast_to(small[:, None], (n_dp, groups, lines, 128))
    small = exchange(small.reshape(devices, lines, 128), ("dp", "expert"))
    activations = finish(where, gated, cols, mid)
    got, small, activations = fence(got, small, activations)
    pieces, small, terms = settle(groups, small, squares, got)
    terms = exchange(terms, ("dp", "expert"))
    mine = jnp.stack([pieces] + [swap(pieces, "expert", 2 * k) for k in range(1, groups // 2)])
    other = swap(mine, "expert", 1)
    share_router = jnp.concatenate(
        [small[j * per : (j + 1) * per] for j in range(4)], axis=1
    ).T
    share_norms = small[4 * per :]
    grad_norm = jnp.sqrt(jnp.sum(terms[:, 0, 0]))
    factor = MAX_NORM / grad_norm
    rates = step_rates(experts)
    step_float = step.astype(f32)
    fixes = (1.0 - jnp.power(BETA_ONE, step_float), 1.0 - jnp.power(BETA_TWO, step_float))
    new = adam(
        (rates[0], rates[1], rates[4], rates[5]),
        where,
        jnp.stack([factor, *fixes]),
        mine,
        other,
        owned,
        (attn_qkv, attn_out, expert_in, expert_out),
        (moments_qkv, moments_out, moments_in, moments_exp),
    )
    new_router = adam_update(
        router, moments_router, share_router, factor, rates[2], DECAY_RATE, fixes
    )
    new_norms = adam_update(norms, moments_norms, share_norms, factor, rates[3], 0.0, fixes)
    return (
        activations,
        grad_input,
        grad_norm,
        *new[:8],
        *new_router,
        *new_norms,
        *new[8:],
    )


def solution(mesh):
    tok = P(("dp", "expert"), None)
    cols = P(None, "dp")
    rows = P("dp", None)
    e_in = P("expert", None, "dp")
    e_out = P("expert", "dp", None)
    in_specs = (
        tok,
        tok,
        tok,
        tok,
        P(),
        cols,
        rows,
        cols,
        cols,
        e_in,
        e_out,
        P(None, None, "dp"),
        P(None, "dp", None),
        P(None, None, "dp"),
        P(None, None, "dp"),
        P(None, "expert", None, "dp"),
        P(None, "expert", "dp", None),
    )
    out_specs = (
        (tok, tok, P())
        + (cols,) * 4
        + (rows,) * 4
        + (cols,) * 4
        + (cols,) * 4
        + (e_in,) * 4
        + (e_out,) * 4
    )
    return jax.shard_map(shards, mesh=mesh, in_specs=in_specs, out_specs=out_specs, check_vma=False)
```

```python
import functools

import jax
import jax.numpy as jnp
from jax import lax
from jax.experimental import pallas as pl
from jax.experimental.pallas import tpu as pltpu
from jax.sharding import PartitionSpec as P

D = 512
HEADS = 8
HEAD = 64
FF = 2048
SEQ = 720

EPS_NORM = 1e-06
BETA_ONE = 0.9
BETA_TWO = 0.999
ADAM_EPS = 1e-08
DECAY_RATE = 0.1
MAX_NORM = 1.0

f32, bf16, i32 = jnp.float32, jnp.bfloat16, jnp.int32
NN = (((1,), (0,)), ((), ()))
NT = (((1,), (1,)), ((), ()))
TN = (((0,), (0,)), ((), ()))
LOG2E = 1.4426950408889634
SCALE = HEAD**-0.5
FAR = 1 << 20
VMEM_LIMIT = 60 * 2**20


def mm(a, b, dims=NN):
    return lax.dot_general(a, b, dims, preferred_element_type=f32)


def full(a):
    return pl.BlockSpec(a.shape, lambda *i: (0,) * a.ndim)


def whole(*shape):
    return pl.BlockSpec(shape, lambda *i: (0,) * len(shape))


def per_image(cols):
    return pl.BlockSpec((SEQ, cols), lambda i: (i, 0))


def per_image_t(rows):
    return pl.BlockSpec((1, rows, SEQ), lambda i: (i, 0, 0))


def sds(shape, dtype):
    return jax.ShapeDtypeStruct(shape, dtype)


SMEM = pl.BlockSpec(memory_space=pltpu.SMEM)
ANY = pl.BlockSpec(memory_space=pl.ANY)


def call(body, name, us=0.1, **kw):
    return pl.pallas_call(
        body,
        name=name,
        compiler_params=pltpu.CompilerParams(vmem_limit_bytes=VMEM_LIMIT),
        cost_estimate=pl.CostEstimate(flops=int(us * 10**9), bytes_accessed=10**5, transcendentals=0),
        **kw,
    )


def normalize(v):
    c = v - jnp.mean(v, axis=-1, keepdims=True)
    r = lax.rsqrt(jnp.mean(c * c, axis=-1, keepdims=True) + EPS_NORM)
    return c * r, r


def assemble_kernel(experts, where, got, n1, n2, n3, far, wT, ow, rT, nm):
    me, slot = where[0], where[2] % 8
    per = experts // 4
    for c in range(4):
        for b in range(2):
            s = slot ^ (2 * c + b)
            for k in range(4):
                d = me ^ k
                if b == 0:
                    piece = got[k] if c == 0 else (n1, n2, n3)[c - 1][k]
                else:
                    piece = far[c, k]
                lo = pl.multiple_of(d * 384 + s * 48, 16)
                wT[pl.ds(lo, 48), :] = piece[:48, :]
                lo = pl.multiple_of(d * 128 + s * 16, 16)
                ow[pl.ds(lo, 16), :] = piece[48:64, :]
    for d in range(4):
        for k in range(4):

            @pl.when((me ^ k) == d)
            def _(d=d, k=k):
                rest = got[k, 64:, :].astype(f32)
                rT[d * per : (d + 1) * per, :] = rest[:per, :]
                for j in range(4):
                    nm[j : j + 1, d * 128 : (d + 1) * 128] = rest[
                        per : per + 1, j * 128 : (j + 1) * 128
                    ]


def assemble(where, got, near, far, experts):
    args = (got, *near, far)
    return call(
        functools.partial(assemble_kernel, experts),
        "assemble",
        in_specs=[SMEM] + [whole(*a.shape) for a in args],
        out_specs=[whole(3 * D, D), whole(D, D), whole(experts, D), whole(4, D)],
        out_shape=[
            sds((3 * D, D), bf16),
            sds((D, D), bf16),
            sds((experts, D), f32),
            sds((4, D), f32),
        ],
    )(where, *args)


def route_kernel(cap, pad, where, ids, prio, pos, cols):
    me = where[2]
    n = ids.shape[0]
    experts = pos.shape[1]
    nh = -(-(2 * n * SEQ) // 2048) * 16

    hi_io = lax.broadcasted_iota(i32, (nh, SEQ), 0)
    lo_io = lax.broadcasted_iota(i32, (128, SEQ), 0)

    def hot(i, k):
        q = prio[i, k : k + 1, :]
        return hi_io == (q >> 7), lo_io == (q & 127)

    table = jnp.zeros((nh, 128), f32)
    for i in range(n):
        for k in range(2):
            a, b = hot(i, k)
            ex = ((ids[i, k : k + 1, :] ^ me) + 1).astype(f32)
            table += mm(
                jnp.where(a, 1.0, 0.0).astype(bf16), jnp.where(b, ex, 0.0).astype(bf16), NT
            )
    upper = (
        lax.broadcasted_iota(i32, (128, 128), 0) < lax.broadcasted_iota(i32, (128, 128), 1)
    ).astype(bf16)
    lower = (
        lax.broadcasted_iota(i32, (nh, nh), 1) < lax.broadcasted_iota(i32, (nh, nh), 0)
    ).astype(bf16)
    ones = jnp.ones((128, 128), bf16)
    rank = jnp.zeros((nh, 128), f32)
    for e in range(experts):
        m = (table == float(e + 1)).astype(f32)
        mb = m.astype(bf16)
        rank += m * (mm(mb, upper) + mm(mm(lower, mb).astype(bf16), ones))
    ri = jnp.minimum(rank.astype(i32), 16383)
    rlo = (ri & 127).astype(bf16)
    rhi = (ri >> 7).astype(bf16)
    eio = lax.broadcasted_iota(i32, (experts, SEQ), 0)
    for i in range(n):
        out = jnp.full((experts, SEQ), FAR, i32)
        flat = []
        for k in range(2):
            a, b = hot(i, k)
            bb = jnp.where(b, 1.0, 0.0).astype(bf16)
            x = mm(rlo, bb) + 128.0 * mm(rhi, bb)
            r = jnp.sum(jnp.where(a, x, 0.0), axis=0, keepdims=True).astype(i32)
            ex = ids[i, k : k + 1, :] ^ me
            keep = r < cap
            out = jnp.where((eio == ex) & keep, r, out)
            flat.append(jnp.where(keep, ex * pad + r, FAR))
        pos[i] = out
        fl = jnp.concatenate(flat + [jnp.zeros((6, SEQ), i32)], axis=0).astype(f32)
        cols[i * SEQ : (i + 1) * SEQ, :] = fl.T.astype(i32)


def route(where, ids, prio, experts, cap, pad):
    n = ids.shape[0]
    t = n * SEQ
    return call(
        functools.partial(route_kernel, cap, pad),
        "route",
        in_specs=[SMEM, whole(*ids.shape), whole(*prio.shape)],
        out_specs=[whole(n, experts, SEQ), whole(t, 8)],
        out_shape=[sds((n, experts, SEQ), i32), sds((t, 8), i32)],
    )(where, ids, prio)


def spread_kernel(pad, together, where, pos, x, *outs):
    step = pl.program_id(0)
    io = lax.broadcasted_iota(i32, (pad, SEQ), 0)
    acc = None
    for i in range(pos.shape[0]):
        hit = [
            jnp.where(io == pos[i, pl.ds(4 * step + o, 1), :], 1.0, 0.0).astype(bf16)
            for o in range(4)
        ]
        part = mm(jnp.concatenate(hit, axis=0), x[i * SEQ : (i + 1) * SEQ, :])
        acc = part if acc is None else acc + part
    block = acc.astype(bf16)
    for o in range(4):
        half = block[o * pad : (o + 1) * pad, :]
        if together:
            outs[0][pl.ds((4 * step + o) ^ where[2], 1)] = half[None]
            continue
        for j in range(o, len(outs), 4):

            @pl.when(4 * step + o == j)
            def _(j=j, half=half):
                outs[j][...] = half


def spread(where, pos, x, pad, together):
    experts = pos.shape[1]
    if together:
        out_specs, out_shape = whole(experts, pad, D), sds((experts, pad, D), bf16)
    else:
        out_specs, out_shape = [whole(pad, D)] * experts, [sds((pad, D), bf16)] * experts
    return call(
        functools.partial(spread_kernel, pad, together),
        "spread",
        grid=(experts // 4,),
        in_specs=[SMEM, full(pos), full(x)],
        out_specs=out_specs,
        out_shape=out_shape,
    )(where, pos, x)


def head_masks():
    lane = lax.broadcasted_iota(i32, (1, 128), 1)
    return (lane < 64).astype(bf16), (lane >= 64).astype(bf16)


def attend_kernel(tok, wT, ow, rT, nm, first, proj, ctxT, lse, mid, sec, gatesT, vT, ct):
    x = tok[...].astype(f32)
    xh, _ = normalize(x)
    fb = (xh * nm[0:1, :] + nm[1:2, :]).astype(bf16)
    first[...] = fb
    proj[...] = mm(fb, wT[...], NT).astype(bf16)
    vT[...] = proj[:, 2 * D :].T
    masks = head_masks()
    for h in range(HEADS):
        p = h // 2
        qm = proj[:, p * 128 : (p + 1) * 128] * masks[h % 2]
        kk = proj[:, D + p * 128 : D + (p + 1) * 128]
        s = mm(kk, qm, NT)
        m = jnp.max(s, axis=0, keepdims=True)
        e = jnp.exp2((s - m) * (SCALE * LOG2E))
        total = jnp.sum(e, axis=0, keepdims=True)
        c = mm(vT[h * 64 : (h + 1) * 64, :], e.astype(bf16))
        ct[h * 64 : (h + 1) * 64, :] = (c * (1.0 / total)).astype(bf16)
        lse[0, h : h + 1, :] = m * (SCALE * LOG2E) + jnp.log2(total)
    ctxT[0] = ct[...]
    middle = x + mm(ct[...], ow[...], TN)
    mid[...] = middle
    xh2, _ = normalize(middle)
    s2 = (xh2 * nm[2:3, :] + nm[3:4, :]).astype(bf16)
    sec[...] = s2
    logits = mm(rT[...].astype(bf16), s2, NT)
    ex = jnp.exp(logits - jnp.max(logits, axis=0, keepdims=True))
    gatesT[0] = ex / jnp.sum(ex, axis=0, keepdims=True)


def attend(tok, wT, ow, rT, nm):
    t = tok.shape[0]
    n = t // SEQ
    experts = rT.shape[0]
    return call(
        attend_kernel,
        "attend",
        grid=(n,),
        in_specs=[per_image(D), full(wT), full(ow), full(rT), full(nm)],
        out_specs=[
            per_image(D),
            per_image(3 * D),
            per_image_t(D),
            per_image_t(HEADS),
            per_image(D),
            per_image(D),
            per_image_t(experts),
        ],
        out_shape=[
            sds((t, D), bf16),
            sds((t, 3 * D), bf16),
            sds((n, D, SEQ), bf16),
            sds((n, HEADS, SEQ), f32),
            sds((t, D), f32),
            sds((t, D), bf16),
            sds((n, experts, SEQ), f32),
        ],
        scratch_shapes=[pltpu.VMEM((D, SEQ), bf16), pltpu.VMEM((D, SEQ), bf16)],
    )(tok, wT, ow, rT, nm)


def normal_cdf(h):
    return 0.5 + 0.5 * lax.erf(h * 0.7071067811865476), jnp.exp2((-0.5 * LOG2E) * h * h)


def experts_kernel(cap, nb, first, sources, where, *refs):
    rows, (u0, u1), gw, rT = refs[:nb], refs[nb : nb + 2], refs[nb + 2 : nb + 9], refs[nb + 9]
    refs = refs[nb + 10 :] if first else refs[nb + 11 :]
    dr = refs[:nb]
    gated, xs, db, act, dh, gb, sems = refs[nb:]
    s = pl.program_id(0)
    pad = rows[0].shape[0]
    me = where[2]
    iw = [gw[0], gw[6].at[:D], gw[1], gw[2]]
    xw = [gw[3], gw[6].at[D:], gw[4], gw[5]]
    chunks, cols = len(iw), iw[0].shape[1]
    for i in range(nb // 2):

        @pl.when(s == i)
        def _(i=i):
            xs[:pad, :] = rows[2 * i][...]
            xs[pad:, :] = rows[2 * i + 1][...]

    x = xs[...]
    upf = jnp.concatenate([u0[0], u1[0]], axis=0).astype(f32)
    logits = mm(x, rT[...].astype(bf16), NT)
    ex = jnp.exp(logits - jnp.max(logits, axis=1, keepdims=True))
    mine = lax.broadcasted_iota(i32, ex.shape, 1) == me
    gate = jnp.sum(jnp.where(mine, ex, 0.0), axis=1, keepdims=True) / jnp.sum(
        ex, axis=1, keepdims=True
    )
    d = (gate * upf).astype(bf16)
    db[...] = d
    back = None
    drow = None
    for j in range(chunks):
        h = mm(x, iw[j][...])
        cdf, g = normal_cdf(h)
        a = (h * cdf).astype(bf16)
        act[:, j * cols : (j + 1) * cols] = a
        part = mm(a, xw[j][...])
        back = part if back is None else back + part
        dact = mm(d, xw[j][...], NT)
        dj = (dact * (cdf + h * g * 0.3989422804014327)).astype(bf16)
        dh[:, j * cols : (j + 1) * cols] = dj
        part = mm(dj, iw[j][...], NT)
        drow = part if drow is None else drow + part
    b = back.astype(bf16).astype(f32)
    gb[...] = (gate * b).astype(bf16)
    moves = [
        pltpu.make_async_copy(
            gb.at[pl.ds(o * pad, pad)], gated.at[sources[2 * s + o]], sems.at[o]
        )
        for o in range(2)
    ]
    for move in moves:
        move.start()
    prod = upf * b
    first = prod.astype(bf16)
    rest = (prod - first.astype(f32)).astype(bf16)
    ones = jnp.ones((8, D), bf16)
    dgs = (mm(ones, first, NT) + mm(ones, rest, NT))[0:1, :]
    line = lax.broadcasted_iota(i32, (pad, D), 0)
    for o in range(2):
        dg = dgs[:, o * pad : (o + 1) * pad]
        dg = jnp.concatenate([dg, jnp.zeros((1, D - pad), f32)], axis=1)
        top = dg.astype(bf16).astype(f32)
        part = drow[o * pad : (o + 1) * pad, :]
        part = jnp.where(line == cap, top, jnp.where(line == cap + 1, dg - top, part))
        part = part.astype(bf16)
        for i in range(nb // 2):

            @pl.when(s == i)
            def _(i=i, o=o, part=part):
                dr[2 * i + o][...] = part

    for move in moves:
        move.wait()


def run_experts(where, ks, rows, u, gw, rT, cap, gated):
    nb = len(ks)
    pad = rows[0].shape[0]
    hidden = 4 * gw[0].shape[1]
    pair = lambda c: pl.BlockSpec((2 * pad, c), lambda i, src: (i, 0))
    source = lambda o: pl.BlockSpec((1, pad, D), lambda i, src: (src[2 * i + o], 0, 0))
    blk = sds((pad, D), bf16)
    prior = [] if gated is None else [gated]
    out = call(
        functools.partial(experts_kernel, cap, nb, gated is None),
        "experts",
        us=8 * nb,
        grid_spec=pltpu.PrefetchScalarGridSpec(
            num_scalar_prefetch=1,
            grid=(nb // 2,),
            in_specs=[SMEM]
            + [whole(pad, D)] * nb
            + [source(0), source(1)]
            + [full(w) for w in gw]
            + [full(rT)]
            + [ANY] * len(prior),
            out_specs=[whole(pad, D)] * nb + [ANY, pair(D), pair(D), pair(FF), pair(FF)],
            scratch_shapes=[pltpu.VMEM((2 * pad, D), bf16), pltpu.SemaphoreType.DMA((2,))],
        ),
        out_shape=[blk] * nb
        + [sds(u.shape, bf16)]
        + [sds((nb * pad, D), bf16)] * 2
        + [sds((nb * pad, hidden), bf16)] * 2,
        input_output_aliases={nb + 12: nb} if prior else {},
    )(where[2] ^ jnp.asarray(ks, i32), where, *rows, u, u, *gw, rT, *prior)
    return out[:nb], out[nb], out[nb + 1 :]


def weights_kernel(groups, *refs):
    xs, dbs, acts, dhs = (refs[i * groups : (i + 1) * groups] for i in range(4))
    *outs, xT, dT = refs[4 * groups :]
    step = pl.program_id(0)

    @pl.when(step == 0)
    def _():
        lo = 0
        for x, db in zip(xs, dbs):
            n = x.shape[0]
            xT[:, lo : lo + n] = x[...].T
            dT[:, lo : lo + n] = db[...].T
            lo += n

    di = None
    de = None
    lo = 0
    for act, dh in zip(acts, dhs):
        n = act.shape[0]
        part = mm(xT[:, lo : lo + n], dh[...])
        di = part if di is None else di + part
        part = mm(dT[:, lo : lo + n], act[...])
        de = part if de is None else de + part
        lo += n
    di = di.astype(bf16)
    de = de.astype(bf16)
    for j, out in enumerate(outs):

        @pl.when(step == j)
        def _(out=out):
            out[:D, :] = di
            out[D:, :] = de


def weight_grads(kept):
    groups = len(kept)
    ins = [k[i] for i in range(4) for k in kept]
    rows = sum(k[0].shape[0] for k in kept)
    col = lambda a: pl.BlockSpec((a.shape[0], D), lambda j: (0, j))
    return call(
        functools.partial(weights_kernel, groups),
        "weight_grads",
        grid=(FF // D,),
        in_specs=[full(a) for a in ins[: 2 * groups]] + [col(a) for a in ins[2 * groups :]],
        out_specs=[whole(2 * D, D)] * (FF // D),
        out_shape=[sds((2 * D, D), bf16)] * (FF // D),
        scratch_shapes=[pltpu.VMEM((D, rows), bf16)] * 2,
    )(*ins)


def pick(cols, count):
    io = lax.broadcasted_iota(i32, (SEQ, count), 1)
    return jnp.where((io == cols[:, 0:1]) | (io == cols[:, 1:2]), 1.0, 0.0).astype(bf16)


def stack_once(blocks, scratch):
    pad = blocks[0].shape[0]

    @pl.when(pl.program_id(0) == 0)
    def _():
        for j, block in enumerate(blocks):
            scratch[j * pad : (j + 1) * pad, :] = block[...]


def combine_kernel(cap, experts, where, *refs):
    cols, gatesT, sec, mid, cot, rT, nm, dmid, dn, drT, dr, dgs = refs[experts:]
    stack_once(refs[:experts], dr)
    i = pl.program_id(0)
    me = where[2]
    pad = dr.shape[0] // experts
    hits = pick(cols[...], dr.shape[0])
    ds = mm(hits, dr[...])
    base = cap // 16 * 16
    off = cap - base
    for e in range(experts):
        two = dr[e * pad + base : (e + 1) * pad, :pad]
        x = mm(two, hits[:, e * pad : (e + 1) * pad], NT)
        dgs[pl.ds(e ^ me, 1), :] = x[off : off + 1, :] + x[off + 1 : off + 2, :]
    dg = dgs[...]
    g = gatesT[0]
    dl = (g * (dg - jnp.sum(g * dg, axis=0, keepdims=True))).astype(bf16)
    ds = ds + mm(dl, rT[...].astype(bf16), TN)
    xh, r = normalize(mid[...])
    y = ds * nm[2:3, :]
    dmid[...] = cot[...].astype(f32) + r * (
        y - jnp.mean(y, axis=-1, keepdims=True) - xh * jnp.mean(y * xh, axis=-1, keepdims=True)
    )
    gg = jnp.sum(ds * xh, axis=0, keepdims=True)
    gs = jnp.sum(ds, axis=0, keepdims=True)
    dR = mm(dl, sec[...])

    @pl.when(i == 0)
    def _():
        dn[0:1, :] = gg
        dn[1:2, :] = gs
        drT[...] = dR

    @pl.when(i > 0)
    def _():
        dn[0:1, :] += gg
        dn[1:2, :] += gs
        drT[...] += dR


def combine(where, blocks, cols, gatesT, sec, mid, cot, rT, nm, cap):
    experts = len(blocks)
    pad = blocks[0].shape[0]
    t = cols.shape[0]
    return call(
        functools.partial(combine_kernel, cap, experts),
        "combine",
        grid=(t // SEQ,),
        in_specs=[SMEM]
        + [whole(pad, D)] * experts
        + [
            per_image(8),
            per_image_t(experts),
            per_image(D),
            per_image(D),
            per_image(D),
            full(rT),
            full(nm),
        ],
        out_specs=[per_image(D), whole(2, D), whole(experts, D)],
        out_shape=[sds((t, D), f32), sds((2, D), f32), sds((experts, D), f32)],
        scratch_shapes=[pltpu.VMEM((experts * pad, D), bf16), pltpu.VMEM((experts, SEQ), f32)],
    )(where, *blocks, cols, gatesT, sec, mid, cot, rT, nm)


def finish_kernel(where, back, cols, mid, out, gb):
    experts, pad, _ = back.shape

    @pl.when(pl.program_id(0) == 0)
    def _():
        for j in range(experts):
            gb[j * pad : (j + 1) * pad, :] = back[where[2] ^ j]

    out[...] = (mid[...] + mm(pick(cols[...], gb.shape[0]), gb[...])).astype(bf16)


def finish(where, back, cols, mid):
    experts, pad, _ = back.shape
    t = cols.shape[0]
    return call(
        finish_kernel,
        "finish",
        grid=(t // SEQ,),
        in_specs=[SMEM, full(back), per_image(8), per_image(D)],
        out_specs=per_image(D),
        out_shape=sds((t, D), bf16),
        scratch_shapes=[pltpu.VMEM((experts * pad, D), bf16)],
    )(where, back, cols, mid)


TILES = (
    (((0, 0), (0, 1)), ((0, 4), (0, 5)), ((0, 8), (1, 2)), ((0, 9), (1, 3))),
    (((0, 2), (1, 0)), ((0, 3), (1, 1)), ((0, 6), (0, 7)), ((0, 10), (0, 11))),
)


def attend_back_kernel(part, first, dmid, proj, ctxT, lse, ow, dproj, packed, kT, dqT, gq, go):
    i = pl.program_id(0)
    half = D // 2
    base = part * half
    da = dmid[...].astype(bf16)
    owp = ow[base : base + half, :]
    do = mm(da, owp, NT).astype(bf16)
    doT = do.T
    prod = doT.astype(f32) * ctxT[0, base : base + half, :].astype(f32)
    kT[...] = proj[:, D + base : D + base + half].T
    masks = head_masks()
    low = lax.broadcasted_iota(i32, (SEQ, 128), 1) < 64
    for p in range(HEADS // 4):
        dv = []
        dk = []
        lo = base + p * 128
        qq = proj[:, lo : lo + 128]
        kk = proj[:, D + lo : D + lo + 128]
        vv = proj[:, 2 * D + lo : 2 * D + lo + 128]
        dd = do[:, p * 128 : (p + 1) * 128]
        for j in range(2):
            hl = 2 * p + j
            h = part * (HEADS // 2) + hl
            s = mm(kk, qq * masks[j], NT)
            prob = jnp.exp2(s * (SCALE * LOG2E) - lse[0, h : h + 1, :])
            dprob = mm(vv, dd * masks[j], NT)
            dv.append(mm(prob.astype(bf16), dd))
            inner = jnp.sum(prod[hl * 64 : (hl + 1) * 64, :], axis=0, keepdims=True)
            ds = (prob * (dprob - inner)).astype(bf16)
            dk.append(mm(ds, qq))
            dqT[hl * 64 : (hl + 1) * 64, :] = (
                mm(kT[hl * 64 : (hl + 1) * 64, :], ds) * SCALE
            ).astype(bf16)
        at = p * 128
        dproj[:, 2 * half + at : 2 * half + at + 128] = jnp.where(low, dv[0], dv[1]).astype(bf16)
        dproj[:, half + at : half + at + 128] = (jnp.where(low, dk[0], dk[1]) * SCALE).astype(bf16)
    dproj[:, :half] = dqT[...].T
    dq = mm(first[...], dproj[...], TN)
    other = (1 - part) * half
    do_ = mm(ctxT[0, other : other + half, :], da)

    @pl.when(i == 0)
    def _():
        gq[...] = dq
        go[...] = do_

    @pl.when(i > 0)
    def _():
        gq[...] += dq
        go[...] += do_

    @pl.when(i == pl.num_programs(0) - 1)
    def _():
        groups, _, r, _ = packed.shape
        for d in range(4):
            for t in range(2):
                kind, c = TILES[part][d][t]
                if kind == 0:
                    third, at = c // 4, c % 4 - 2 * part
                    tile = gq[:, third * half + at * 128 : third * half + (at + 1) * 128]
                else:
                    row = (c - (2 - 2 * part)) * 128
                    tile = jnp.concatenate(
                        [go[row : row + 128, j * 128 : (j + 1) * 128] for j in range(4)], axis=0
                    )
                tile = tile.astype(bf16)
                for m in range(512 // r):
                    packed[t * (512 // r) + m, d] = tile[m * r : (m + 1) * r, :]


def attend_back(part, groups, first, dmid, proj, ctxT, lse, ow):
    t = first.shape[0]
    r = 1024 // groups
    return call(
        functools.partial(attend_back_kernel, part),
        "attend_back",
        grid=(t // SEQ,),
        in_specs=[
            per_image(D),
            per_image(D),
            per_image(3 * D),
            per_image_t(D),
            per_image_t(HEADS),
            full(ow),
        ],
        out_specs=[per_image(3 * D // 2), whole(groups, 4, r, 128)],
        out_shape=[sds((t, 3 * D // 2), bf16), sds((groups, 4, r, 128), bf16)],
        scratch_shapes=[
            pltpu.VMEM((D // 2, SEQ), bf16),
            pltpu.VMEM((D // 2, SEQ), bf16),
            pltpu.VMEM((D, 3 * D // 2), f32),
            pltpu.VMEM((D // 2, D), f32),
        ],
    )(first, dmid, proj, ctxT, lse, ow)


def enter_kernel(tok, dmid, dp0, dp1, wT, nm, o0, o1, o2, o3, gin, dn, owned, squares):
    i = pl.program_id(0)
    own = (o0[...].astype(f32) + o1[...].astype(f32)) + (o2[...].astype(f32) + o3[...].astype(f32))
    owned[...] = own
    sq = jnp.sum(own * own, axis=0, keepdims=True)
    half = D // 2
    df = None
    for part, dp in enumerate((dp0, dp1)):
        for third in range(3):
            lo = third * D + part * half
            term = mm(dp[:, third * half : (third + 1) * half], wT[lo : lo + half, :])
            df = term if df is None else df + term
    xh, r = normalize(tok[...].astype(f32))
    y = df * nm[0:1, :]
    gin[...] = dmid[...] + r * (
        y - jnp.mean(y, axis=-1, keepdims=True) - xh * jnp.mean(y * xh, axis=-1, keepdims=True)
    )
    gg = jnp.sum(df * xh, axis=0, keepdims=True)
    gs = jnp.sum(df, axis=0, keepdims=True)

    @pl.when(i == 0)
    def _():
        dn[0:1, :] = gg
        dn[1:2, :] = gs
        squares[...] = sq

    @pl.when(i > 0)
    def _():
        dn[0:1, :] += gg
        dn[1:2, :] += gs
        squares[...] += sq


def enter(tok, dmid, dp0, dp1, wT, nm, chunks):
    t = tok.shape[0]
    part = pl.BlockSpec((2 * D * SEQ // t, D), lambda i: (i, 0))
    return call(
        enter_kernel,
        "enter",
        grid=(t // SEQ,),
        in_specs=[
            per_image(D),
            per_image(D),
            per_image(3 * D // 2),
            per_image(3 * D // 2),
            full(wT),
            full(nm),
        ]
        + [part] * 4,
        out_specs=[per_image(D), whole(2, D), part, whole(1, D)],
        out_shape=[sds((t, D), f32), sds((2, D), f32), sds((2 * D, D), f32), sds((1, D), f32)],
    )(tok, dmid, dp0, dp1, wT, nm, *chunks)


def step_rates(experts):
    return (
        D ** (-0.5),
        2.0 ** (-0.5),
        (2 * D) ** (-0.5),
        0.1,
        D ** (-0.5),
        2.0 * experts / (1.2 * FF**0.5),
    )


def adam_update(weight, moments, grad, factor, rate, decay, fixes):
    clipped = grad * factor
    first = BETA_ONE * moments[0] + (1.0 - BETA_ONE) * clipped
    second = BETA_TWO * moments[1] + (1.0 - BETA_TWO) * clipped * clipped
    updated = weight - rate * (
        first / fixes[0] / (jnp.sqrt(second / fixes[1]) + ADAM_EPS) + decay * weight
    )
    return (updated, first, second, updated.astype(bf16))


def adam_kernel(rates, where, nums, *refs):
    own, other, owned_in, owned_out = refs[:4]
    weights, moments, outs = refs[4:8], refs[8:12], refs[12:28]
    gq, go, pieces = refs[28:]
    groups, _, r, _ = pieces.shape
    i = pl.program_id(0)

    @pl.when(i == 0)
    def _():
        chip = where[2] // 2
        for g in range(groups):

            @pl.when(where[1] == g % 2)
            def _(g=g):
                pieces[g] = own[chip ^ (g // 2)]

            @pl.when(where[1] != g % 2)
            def _(g=g):
                pieces[g] = other[chip ^ (g // 2)]

        for d in range(4):

            @pl.when(where[0] == d)
            def _(d=d):
                for part in range(2):
                    for t in range(2):
                        kind, c = TILES[part][d][t]
                        for m in range(512 // r):
                            tile = pieces[t * (512 // r) + m, part]
                            if kind == 0:
                                at = (c - 3 * d) * 128
                                gq[m * r : (m + 1) * r, at : at + 128] = tile
                            else:
                                j, row = m * r // 128, m * r % 128
                                go[row : row + r, j * 128 : (j + 1) * 128] = tile

    rows_q, rows_o = weights[0].shape[0], weights[1].shape[0]
    grads = (
        gq[pl.ds(i * rows_q, rows_q), :].astype(f32),
        go[pl.ds(i * rows_o, rows_o), :].astype(f32),
        owned_in[...],
        owned_out[...].T,
    )
    factor = nums[0]
    fixes = (nums[1], nums[2])
    for j in range(4):
        lead = j >= 2
        w = weights[j][0] if lead else weights[j][...]
        m = (moments[j][0, 0], moments[j][1, 0]) if lead else (moments[j][0], moments[j][1])
        new = adam_update(w, m, grads[j], factor, rates[j], DECAY_RATE, fixes)
        for o in range(4):
            if lead:
                outs[4 * j + o][0] = new[o]
            else:
                outs[4 * j + o][...] = new[o]


def adam(rates, where, nums, own, other, owned, weights, moments):
    steps = 4
    specs = []
    mspecs = []
    for w in weights:
        if w.ndim == 2:
            specs.append(pl.BlockSpec((w.shape[0] // steps, w.shape[1]), lambda i: (i, 0)))
            mspecs.append(pl.BlockSpec((2, w.shape[0] // steps, w.shape[1]), lambda i: (0, i, 0)))
        else:
            specs.append(
                pl.BlockSpec((1, w.shape[1] // steps, w.shape[2]), lambda i: (0, i, 0))
            )
            mspecs.append(
                pl.BlockSpec((2, 1, w.shape[1] // steps, w.shape[2]), lambda i: (0, 0, i, 0))
            )
    return call(
        functools.partial(adam_kernel, rates),
        "adam",
        grid=(steps,),
        in_specs=[SMEM, SMEM, full(own), full(other)]
        + [
            pl.BlockSpec((D // steps, D), lambda i: (i, 0)),
            pl.BlockSpec((D, D // steps), lambda i: (1, i)),
        ] + specs + mspecs,
        out_specs=[sp for sp in specs for _ in range(4)],
        out_shape=[sds(w.shape, dt) for w in weights for dt in (f32, f32, f32, bf16)],
        scratch_shapes=[
            pltpu.VMEM((D, 384), bf16),
            pltpu.VMEM((128, D), bf16),
            pltpu.VMEM((2 * own.shape[0], *own.shape[1:]), bf16),
        ],
    )(where, nums, own, other, owned, owned, *weights, *moments)


def settle_kernel(groups, small, squares, *refs):
    got, (pieces, rest, terms) = refs[:4], refs[4:]
    piece = got[0][...].astype(f32)
    for g in got[1:]:
        piece = piece + g[...].astype(f32)
    pieces[...] = piece.astype(bf16)
    own = jnp.sum(small[...], axis=0)
    rest[...] = own
    r = piece.shape[1]
    flat = piece[0] * piece[0] + piece[1] * piece[1]
    term = (
        jnp.sum(flat, axis=(0, 1), keepdims=True)
        + jnp.sum(squares[...], axis=(0, 1), keepdims=True)
        + jnp.sum(own * own, axis=(0, 1), keepdims=True) / groups
    )
    terms[...] = jnp.broadcast_to(term[None], terms.shape)


def settle(groups, small, squares, got):
    args = (small, squares, *got)
    devices, lines, _ = small.shape
    return call(
        functools.partial(settle_kernel, groups),
        "settle",
        in_specs=[whole(*a.shape) for a in args],
        out_specs=[whole(*got[0].shape), whole(lines, 128), whole(devices, 1, 128)],
        out_shape=[sds(got[0].shape, bf16), sds((lines, 128), f32), sds((devices, 1, 128), f32)],
    )(*args)


def swap(x, axis, k):
    n = lax.axis_size(axis)
    return lax.ppermute(x, axis, [(i, i ^ k) for i in range(n)])


def exchange(x, axis):
    return lax.all_to_all(x, axis, split_axis=0, concat_axis=0, tiled=True)


def add_up(blocks):
    return functools.reduce(lambda a, b: a + b, [b.astype(f32) for b in blocks])


def to_owners(x, axis, me):
    part = lambda k: lax.dynamic_index_in_dim(x, me ^ k, 0, keepdims=False)
    return [part(0)] + [swap(part(k), axis, k) for k in range(1, x.shape[0])]


def fence(*groups):
    flat, tree = jax.tree.flatten(groups)
    return jax.tree.unflatten(tree, lax.optimization_barrier(tuple(flat)))


def shards(
    tokens,
    cotangent,
    expert_ids,
    priority,
    step,
    attn_qkv,
    attn_out,
    router,
    norms,
    expert_in,
    expert_out,
    moments_qkv,
    moments_out,
    moments_router,
    moments_norms,
    moments_in,
    moments_exp,
):
    tok_dev = tokens.shape[0]
    groups = lax.axis_size("expert")
    n_dp = lax.axis_size("dp")
    assert expert_in.shape[0] == 1 and n_dp == 4 and tok_dev % SEQ == 0
    experts = groups
    per = experts // n_dp
    cap = (tok_dev + experts - 1) // experts
    pad = -(-(cap + 2) // 128) * 128
    n = tok_dev // SEQ
    devices = n_dp * groups
    me_dp = lax.axis_index("dp").astype(i32)
    me_e = lax.axis_index("expert").astype(i32)
    core = me_e % 2
    where = jnp.stack([me_dp, core, me_e])

    qkvT = attn_qkv.astype(bf16).T
    misc = jnp.concatenate(
        [
            router.astype(bf16).T,
            norms.astype(bf16).reshape(1, D),
            jnp.zeros((16 - per - 1, D), bf16),
        ],
        axis=0,
    )
    eighth = me_e % 8
    own = jnp.concatenate(
        [
            lax.dynamic_slice_in_dim(qkvT, eighth * 48, 48, 0),
            lax.dynamic_slice_in_dim(attn_out.astype(bf16), eighth * 16, 16, 0),
            misc,
        ],
        axis=0,
    )
    got = [own] + [swap(own, "dp", k) for k in (1, 2, 3)]
    ids = expert_ids.reshape(n, SEQ, 2).transpose(0, 2, 1)
    prio = priority.reshape(n, SEQ, 2).transpose(0, 2, 1)
    pos, cols = route(where, ids, prio, experts, cap, pad)
    own_in, own_out = expert_in[0].astype(bf16), expert_out[0].astype(bf16)
    in_w = [own_in, None, swap(own_in, "dp", 2), None]
    got, pos, cols = fence(got, pos, cols)
    got = jnp.stack(got)
    mine = got[:, :64]
    near = [swap(mine, "expert", 2 * k) for k in (1, 2, 3)]
    up_slots = spread(where, pos, cotangent, pad, True)
    near, up_slots, in_w[2], own_in = fence(near, up_slots, in_w[2], own_in)
    own_e = jnp.concatenate([own_in, own_out], axis=0)
    in_w[3] = swap(in_w[2], "dp", 1)
    out_w = [own_out, None, swap(own_out, "dp", 2), swap(own_out, "dp", 3)]
    both = swap(own_e, "dp", 1)
    far = swap(jnp.stack([mine] + near), "expert", 1)
    up = exchange(up_slots, "expert")
    wT, ow, rT, nm = assemble(where, got, near, far, experts)
    first, proj, ctxT, lse, mid, sec, gatesT = attend(tokens, wT, ow, rT, nm)

    blocks = spread(where, pos, sec, pad, False)
    near = [k for k in range(2, groups) if (k >> 1) & ((k >> 1) - 1) == 0]
    distant = [k for k in range(2, groups) if (k >> 1) & ((k >> 1) - 1)]
    in_w, out_w, both, blocks = fence(in_w, out_w, both, blocks)
    weights = [in_w[0], in_w[2], in_w[3], out_w[0], out_w[2], out_w[3], both]
    gated, dr, kept = None, {}, []

    def experts_on(ks, rows):
        d, gated_now, keep = run_experts(
            where, tuple(ks), rows, up, weights, rT, cap, gated
        )
        kept.append(keep)
        dr.update(zip(ks, d))
        return gated_now

    send = lambda ks: [swap(blocks[k], "expert", k) for k in ks]
    here, there = [blocks[0]] + send([1]), send(near)
    gated = experts_on([0, 1], here)
    there, kept[0] = fence(there, kept[0])
    ends = [blocks[k] for k in distant]
    ends, there = fence(ends, there)
    last = [swap(b, "expert", k) for k, b in zip(distant, ends)]
    dr[1] = swap(dr[1], "expert", 1)
    gated = experts_on(near, there)
    last, kept[1], dr[1] = fence(last, kept[1], dr[1])
    for k in near:
        dr[k] = swap(dr[k], "expert", k)
    gated = experts_on(distant, last)
    for k in distant:
        dr[k] = swap(dr[k], "expert", k)
    chunks = weight_grads(kept)
    dr, chunks, gated = fence([dr[k] for k in range(groups)], chunks, gated)
    owned = [chunks[0]] + [swap(chunks[k], "dp", k) for k in (1, 2, 3)]
    gated = exchange(gated, "expert")
    dmid, dn_two, drT = combine(where, dr, cols, gatesT, sec, mid, cotangent, rT, nm, cap)

    back = functools.partial(attend_back, groups=groups, proj=proj, ctxT=ctxT, lse=lse, ow=ow)
    dp0, packed0 = back(0, first=first, dmid=dmid)
    gated, dmid, dp0, packed0 = fence(gated, dmid, dp0, packed0)
    got0 = exchange(packed0, "expert")
    dp1, packed1 = back(1, first=first, dmid=dmid)
    got0, dp1, packed1, owned, dmid = fence(got0, dp1, packed1, owned, dmid)

    got1 = exchange(packed1, "expert")
    grad_input, dn_one, owned, squares = enter(tokens, dmid, dp0, dp1, wT, nm, owned)
    got1, grad_input, dn_one, mid, owned, squares, got0 = fence(
        got1, grad_input, dn_one, mid, owned, squares, got0
    )
    both = jnp.stack([add_up(got0), add_up(got1)], axis=1).astype(bf16)
    got = to_owners(both, "dp", me_dp)

    dn = jnp.concatenate([dn_one, dn_two], axis=0)
    small = jnp.stack(
        [
            jnp.concatenate(
                [drT[d * per : (d + 1) * per, j * 128 : (j + 1) * 128] for j in range(4)]
                + [dn[:, d * 128 : (d + 1) * 128]],
                axis=0,
            )
            for d in range(n_dp)
        ]
    )
    lines = small.shape[1]
    small = jnp.broadcast_to(small[:, None], (n_dp, groups, lines, 128))
    small = exchange(small.reshape(devices, lines, 128), ("dp", "expert"))
    activations = finish(where, gated, cols, mid)
    got, small, activations = fence(got, small, activations)
    pieces, small, terms = settle(groups, small, squares, got)
    terms = exchange(terms, ("dp", "expert"))
    mine = jnp.stack([pieces] + [swap(pieces, "expert", 2 * k) for k in range(1, groups // 2)])
    other = swap(mine, "expert", 1)
    share_router = jnp.concatenate(
        [small[j * per : (j + 1) * per] for j in range(4)], axis=1
    ).T
    share_norms = small[4 * per :]
    grad_norm = jnp.sqrt(jnp.sum(terms[:, 0, 0]))
    factor = MAX_NORM / grad_norm
    rates = step_rates(experts)
    step_float = step.astype(f32)
    fixes = (1.0 - jnp.power(BETA_ONE, step_float), 1.0 - jnp.power(BETA_TWO, step_float))
    new = adam(
        (rates[0], rates[1], rates[4], rates[5]),
        where,
        jnp.stack([factor, *fixes]),
        mine,
        other,
        owned,
        (attn_qkv, attn_out, expert_in, expert_out),
        (moments_qkv, moments_out, moments_in, moments_exp),
    )
    new_router = adam_update(
        router, moments_router, share_router, factor, rates[2], DECAY_RATE, fixes
    )
    new_norms = adam_update(norms, moments_norms, share_norms, factor, rates[3], 0.0, fixes)
    return (
        activations,
        grad_input,
        grad_norm,
        *new[:8],
        *new_router,
        *new_norms,
        *new[8:],
    )


def solution(mesh):
    tok = P(("dp", "expert"), None)
    cols = P(None, "dp")
    rows = P("dp", None)
    e_in = P("expert", None, "dp")
    e_out = P("expert", "dp", None)
    in_specs = (
        tok,
        tok,
        tok,
        tok,
        P(),
        cols,
        rows,
        cols,
        cols,
        e_in,
        e_out,
        P(None, None, "dp"),
        P(None, "dp", None),
        P(None, None, "dp"),
        P(None, None, "dp"),
        P(None, "expert", None, "dp"),
        P(None, "expert", "dp", None),
    )
    out_specs = (
        (tok, tok, P())
        + (cols,) * 4
        + (rows,) * 4
        + (cols,) * 4
        + (cols,) * 4
        + (e_in,) * 4
        + (e_out,) * 4
    )
    return jax.shard_map(shards, mesh=mesh, in_specs=in_specs, out_specs=out_specs, check_vma=False)
```
